32 devices in a mesh: interval: 2 (over y), seq: 4 (over x, core), head: 4 (over z).
Axes of the slice: x: 2, y: 2, z: 4, core: 2. Of those that a mesh axis runs over, the one named last changes fastest.
Arguments:
- hidden_in: bfloat16 [2, 1024, 1536], P('interval', 'seq'), may hold values from -6 to 6
- ctx_grad: bfloat16 [2, 1024, 1536], P('interval', 'seq', 'head'), may hold values from -6 to 6
- w_query: bfloat16 [1536, 1536], P('head'), may hold values from -0.15625 to 0.15625
- w_key: bfloat16 [1536, 1536], P('head'), may hold values from -0.15625 to 0.15625
- w_value: bfloat16 [1536, 1536], P('head'), may hold values from -0.15625 to 0.15625
- w_junction: bfloat16 [1536, 128], replicated, may hold values from -0.15625 to 0.15625
- donor_pos: int32 [2, 4, 4, 32], P('interval', 'seq', None, 'head'), may hold values from 0 to 255
- acceptor_pos: int32 [2, 4, 4, 32], P('interval', 'seq', None, 'head'), may hold values from 0 to 255
- junction_counts: int32 [2, 4, 4], P('interval', 'seq'), may hold values from 8 to 32, as said below
- pred_grad: float32 [2, 4, 4, 32], P('interval', 'seq', None, 'head'), may hold values from -6 to 6
Outputs:
- grad_input: bfloat16 [2, 1024, 1536], P('interval', 'seq', 'head')
- grad_query: bfloat16 [1536, 1536], P('head')
- grad_key: bfloat16 [1536, 1536], P('head')
- grad_value: bfloat16 [1536, 1536], P('head')
The draws below stay inside these ranges and needn't reach their ends.
Inputs may be any that keep to these rules, and one draw needn't show every extreme that they name: `junction_counts`: slots at or past a bucket's count are empty. In each interval one acceptor shard, drawn from the seed, has 32 live slots from every donor shard; every other bucket has 8 to 16.
All inputs are finite; a program needn't handle non-finite values.
Results may differ from the reference program's by a relative error of at most 0.022.
Values may be sent and summed in bfloat16 or wider, within the bound.
A program may use at most 64 MiB of HBM per device.

```python
import jax
import jax.numpy as jnp
from jax import lax

D = 1536
HEADS = 8
HD = 192
PJ = 128
TOK_DEV = 256
SLOT_HEAD = 8
SEQ = 1024
INTERVALS = 2
CAP = 32
N_SEQ = 4
N_HEAD = 4


def draw_junction_counts(key, part):
    key_hot, key_base = jax.random.split(key)
    hot_shard = jax.random.randint(key_hot, (INTERVALS, 1, 1), 0, N_SEQ)
    base = jax.random.randint(key_base, (INTERVALS, N_SEQ, N_SEQ), CAP // 4, CAP // 2 + 1)
    column = jnp.arange(N_SEQ, dtype=jnp.int32).reshape(1, 1, N_SEQ)
    return jnp.where(column == hot_shard, CAP, base).astype(jnp.int32)


def plant(drawn, stream_key, smallest, high):
    extent = drawn.shape
    spot = [jax.random.randint(jax.random.fold_in(stream_key, axis), (), 0, extent[axis]) for axis in range(len(extent))]
    drawn = drawn.at[tuple(spot)].set(smallest)
    longest = extent.index(max(extent))
    spot[longest] = (spot[longest] + 1) % extent[longest]
    return drawn.at[tuple(spot)].set(high)


def shard_levels(own_key, extent, cuts, least, high):
    loudness, own = 1.0, jax.random.fold_in(own_key, 6)
    for position, shards_of in cuts:
        draws = jnp.exp(jax.random.uniform(jax.random.fold_in(own, position), (shards_of,), jnp.float32, least / len(cuts), high / len(cuts)))
        loudness = loudness * jnp.repeat(draws, extent[position] // shards_of).reshape([-1 if axis == position else 1 for axis in range(len(extent))])
    return loudness


def normal_values(key, shape, scale, limit, cuts=(), kind=jnp.bfloat16):
    values = jax.random.normal(key, shape, jnp.float32) * scale
    if len(cuts) > 0:
        values = shard_levels(key, shape, cuts, -0.22, 0.18) * values
    return jnp.clip(values, min=-limit, max=limit).astype(kind)


def setup_inputs(seed: int = 0) -> dict:
    keys = jax.random.split(jax.random.key(seed), 11)
    return {
        "hidden_in": normal_values(keys[0], (INTERVALS, SEQ, D), 1.0, 6.0, ((0, 2), (1, 4))),
        "ctx_grad": normal_values(keys[1], (INTERVALS, SEQ, HEADS * HD), 1.0, 6.0, ((0, 2), (1, 4), (2, 4))),
        "w_query": normal_values(keys[2], (HEADS * HD, D), D ** -0.5, 0.15625, ((0, 4),)),
        "w_key": normal_values(keys[3], (HEADS * HD, D), D ** -0.5, 0.15625, ((0, 4),)),
        "w_value": normal_values(keys[4], (HEADS * HD, D), D ** -0.5, 0.15625, ((0, 4),)),
        "w_junction": normal_values(keys[5], (D, PJ), D ** -0.5, 0.15625),
        "donor_pos": plant(jax.random.randint(keys[6], (INTERVALS, N_SEQ, N_SEQ, CAP), 0, TOK_DEV), jax.random.fold_in(keys[6], 1), 0, TOK_DEV - 1).astype(jnp.int32),
        "acceptor_pos": plant(jax.random.randint(keys[7], (INTERVALS, N_SEQ, N_SEQ, CAP), 0, TOK_DEV), jax.random.fold_in(keys[7], 1), 0, TOK_DEV - 1).astype(jnp.int32),
        "junction_counts": draw_junction_counts(jax.random.fold_in(keys[10], 71), 0),
        "pred_grad": normal_values(keys[9], (INTERVALS, N_SEQ, N_SEQ, CAP), 1.0, 6.0, ((0, 2), (1, 4), (3, 4)), jnp.float32),
    }


def rounded(value):
    return lax.optimization_barrier(value.astype(jnp.bfloat16)).astype(jnp.float32)


def attention_grads(hidden, ctx, w_query, w_key, w_value):
    total_len = hidden.shape[0]
    softmax_scale = HD ** -0.5
    queries = jnp.dot(hidden, w_query.T, preferred_element_type=jnp.float32).astype(jnp.bfloat16)
    key_rows = jnp.dot(hidden, w_key.T, preferred_element_type=jnp.float32).astype(jnp.bfloat16)
    value_rows = jnp.dot(hidden, w_value.T, preferred_element_type=jnp.float32).astype(jnp.bfloat16)
    key_heads = key_rows.astype(jnp.float32).reshape(total_len, HEADS, HD)
    value_heads = value_rows.astype(jnp.float32).reshape(total_len, HEADS, HD)
    query_blocks = queries.reshape(N_SEQ, TOK_DEV, HEADS, HD)
    grad_blocks = ctx.reshape(N_SEQ, TOK_DEV, HEADS, HD)

    def step_block(totals, inputs):
        query_part = inputs[0].astype(jnp.float32)
        grad_part = inputs[1].astype(jnp.float32)
        scores = jnp.einsum("qhd,khd->hqk", query_part, key_heads) * softmax_scale
        row_max = jnp.max(scores, axis=-1, keepdims=True)
        expd = jnp.exp(scores - row_max)
        probs = expd / jnp.sum(expd, axis=-1, keepdims=True)
        dprobs = jnp.einsum("qhd,khd->hqk", grad_part, value_heads)
        row_delta = jnp.sum(probs * dprobs, axis=-1, keepdims=True)
        dscores = probs * (dprobs - row_delta)
        probs_b = rounded(probs)
        dscores_b = rounded(dscores)
        value_term = jnp.einsum("hqk,qhd->khd", probs_b, grad_part)
        key_term = jnp.einsum("hqk,qhd->khd", dscores_b, query_part) * softmax_scale
        query_grad = (jnp.einsum("hqk,khd->qhd", dscores_b, key_heads) * softmax_scale).astype(jnp.bfloat16)
        return (totals[0] + rounded(key_term), totals[1] + rounded(value_term)), query_grad

    empty = jnp.zeros((total_len, HEADS, HD), jnp.float32)
    sums, query_grads = lax.scan(step_block, (empty, empty), (query_blocks, grad_blocks))
    width = HEADS * HD
    query_grad = query_grads.reshape(total_len, width)
    key_grad = sums[0].reshape(total_len, width).astype(jnp.bfloat16)
    value_grad = sums[1].reshape(total_len, width).astype(jnp.bfloat16)
    return query_grad, key_grad, value_grad


def junction_grads(hidden, w_junction, donor_pos, acceptor_pos, counts, pred_grad):
    total_len = hidden.shape[0]
    pair_scale = PJ ** -0.5
    features = jnp.dot(hidden, w_junction, preferred_element_type=jnp.float32).astype(jnp.bfloat16)
    shard_rows = jnp.arange(N_SEQ, dtype=jnp.int32) * TOK_DEV
    donor_glob = shard_rows.reshape(N_SEQ, 1, 1) + donor_pos
    accept_glob = shard_rows.reshape(1, N_SEQ, 1) + acceptor_pos
    donor_feat = features[donor_glob].astype(jnp.float32)
    accept_feat = features[accept_glob].astype(jnp.float32)
    pair_score = jnp.sum(donor_feat * accept_feat, axis=-1) * pair_scale
    live_slots = jnp.arange(CAP, dtype=jnp.int32).reshape(1, 1, CAP) < counts[:, :, None]
    slot_grad = jnp.where(live_slots, pred_grad * jax.nn.sigmoid(pair_score), 0.0) * pair_scale
    donor_term = slot_grad[..., None] * accept_feat
    accept_term = slot_grad[..., None] * donor_feat
    result = jnp.zeros((total_len, hidden.shape[1]), jnp.float32)
    for group in range(N_HEAD):
        lower = group * SLOT_HEAD
        upper = lower + SLOT_HEAD
        grad_feat = jnp.zeros((total_len, PJ), jnp.float32)
        grad_feat = grad_feat.at[donor_glob[:, :, lower:upper].reshape(-1)].add(donor_term[:, :, lower:upper].reshape(-1, PJ))
        grad_feat = grad_feat.at[accept_glob[:, :, lower:upper].reshape(-1)].add(accept_term[:, :, lower:upper].reshape(-1, PJ))
        result = result + jnp.dot(grad_feat.astype(jnp.bfloat16), w_junction.T, preferred_element_type=jnp.float32)
    return result


def reference(hidden_in, ctx_grad, w_query, w_key, w_value, w_junction, donor_pos, acceptor_pos, junction_counts, pred_grad):
    input_grads = []
    sum_query = jnp.zeros(w_query.shape, jnp.float32)
    sum_key = jnp.zeros(w_query.shape, jnp.float32)
    sum_value = jnp.zeros(w_query.shape, jnp.float32)
    for interval_idx in range(INTERVALS):
        hidden = hidden_in[interval_idx]
        query_grad, key_grad, value_grad = attention_grads(hidden, ctx_grad[interval_idx], w_query, w_key, w_value)
        from_pairs = junction_grads(hidden, w_junction, donor_pos[interval_idx], acceptor_pos[interval_idx], junction_counts[interval_idx], pred_grad[interval_idx])
        total = jnp.dot(query_grad, w_query, preferred_element_type=jnp.float32)
        total = total + jnp.dot(key_grad, w_key, preferred_element_type=jnp.float32)
        total = total + jnp.dot(value_grad, w_value, preferred_element_type=jnp.float32)
        input_grads.append((total + from_pairs).astype(jnp.bfloat16))
        sum_query = sum_query + jnp.dot(query_grad.T, hidden, preferred_element_type=jnp.float32)
        sum_key = sum_key + jnp.dot(key_grad.T, hidden, preferred_element_type=jnp.float32)
        sum_value = sum_value + jnp.dot(value_grad.T, hidden, preferred_element_type=jnp.float32)
    return (jnp.stack(input_grads), sum_query.astype(jnp.bfloat16), sum_key.astype(jnp.bfloat16), sum_value.astype(jnp.bfloat16))
```

```python
import functools

import jax
import jax.numpy as jnp
from jax import lax
from jax.experimental import pallas as pl
from jax.experimental.pallas import tpu as pltpu
from jax.sharding import PartitionSpec as P

HD = 192
PJ = 128
MESH = pl.DeviceIdType.MESH
F32 = jnp.float32
BF16 = jnp.bfloat16


def dot_nn(a, b):
    return lax.dot_general(a, b, (((1,), (0,)), ((), ())), preferred_element_type=F32)


def dot_nt(a, b):
    return lax.dot_general(a, b, (((1,), (1,)), ((), ())), preferred_element_type=F32)


def dot_tn(a, b):
    return lax.dot_general(a, b, (((0,), (0,)), ((), ())), preferred_element_type=F32)


def fused_kernel(
    n_head,
    n_copies,
    hid,
    ctx,
    wq,
    wk,
    wv,
    wj,
    slots,
    out_in,
    out_q,
    out_k,
    out_v,
    kbuf,
    vbuf,
    fbuf,
    slotbuf,
    qbuf,
    hid_sib,
    sref,
    dpref,
    pb,
    dsb,
    term,
    from_sib,
    pair_sum,
    from_xn,
    own_term,
    grads,
    grads_sib,
    dwp,
    rs1,
    s1,
    rs2,
    zsend,
    zrecv,
    zown,
    send_sems,
    recv_sems,
):
    toks = hid.shape[0]
    width = hid.shape[1]
    feats = wq.shape[0]
    heads = feats // HD
    half = width // 2
    quart = half // 2
    row_half = feats // 2
    row_q = feats // 4
    scale = HD**-0.5
    iv = lax.axis_index("interval")
    sq = lax.axis_index("seq")
    hd = lax.axis_index("head")
    xi = lax.div(sq, 2)
    core = lax.rem(sq, 2)
    s_sib = sq + 1 - 2 * core
    s_xn = lax.rem(sq + 2, 4)
    s_dg = lax.rem(s_sib + 2, 4)
    sib = (iv, s_sib, hd)
    xn = (iv, s_xn, hd)
    yn = (1 - iv, sq, hd)
    zpeers = [(iv, sq, lax.rem(hd + d, n_head)) for d in range(1, n_head)]

    counter = [0]
    started = []

    def send(src, dst, dev):
        i = counter[0]
        counter[0] += 1
        copy = pltpu.make_async_remote_copy(
            src_ref=src,
            dst_ref=dst,
            send_sem=send_sems.at[i],
            recv_sem=recv_sems.at[i],
            device_id=dev,
            device_id_type=MESH,
        )
        copy.start()
        started.append(copy)
        return copy

    barrier = pltpu.get_barrier_semaphore()
    for dev in [sib, xn, yn] + zpeers:
        pl.semaphore_signal(barrier, inc=1, device_id=dev, device_id_type=MESH)

    kbuf[0] = dot_nt(hid[...], wk[...]).astype(BF16)
    pl.semaphore_wait(barrier, 3 + len(zpeers))
    k_xn = send(kbuf.at[0], kbuf.at[2], xn)
    k_sib = send(kbuf.at[0], kbuf.at[1], sib)
    vbuf[0] = dot_nt(hid[...], wv[...]).astype(BF16)
    v_xn = send(vbuf.at[0], vbuf.at[2], xn)
    v_sib = send(vbuf.at[0], vbuf.at[1], sib)
    fbuf[0] = dot_nn(hid[...], wj[...]).astype(BF16)
    slotbuf[0] = slots[...]
    f_xn = send(fbuf.at[0], fbuf.at[2], xn)
    f_sib = send(fbuf.at[0], fbuf.at[1], sib)
    t_xn = send(slotbuf.at[0], slotbuf.at[2], xn)
    t_sib = send(slotbuf.at[0], slotbuf.at[1], sib)
    other_half = pl.ds(pl.multiple_of((1 - core) * half, half), half)
    my_half = pl.ds(pl.multiple_of(core * half, half), half)
    h_sib = send(hid.at[:, other_half], hid_sib, sib)
    qbuf[...] = dot_nt(hid[...], wq[...]).astype(BF16)

    def head_cols(h):
        return slice(h * HD, (h + 1) * HD)

    def block_cols(r):
        return slice(r * toks, (r + 1) * toks)

    def scores(r):
        for h in range(heads):
            sref[h, :, block_cols(r)] = dot_nt(qbuf[:, head_cols(h)], kbuf[r, :, head_cols(h)])

    def dprobs(r):
        for h in range(heads):
            dpref[h, :, block_cols(r)] = dot_nt(ctx[:, head_cols(h)], vbuf[r, :, head_cols(h)])

    scores(0)
    dprobs(0)
    k_sib.wait_recv()
    scores(1)
    k_xn.wait_recv()
    k_fw = send(kbuf.at[2], kbuf.at[3], sib)
    scores(2)
    k_fw.wait_recv()
    scores(3)

    rows_step = 32

    for h in range(heads):

        @pl.loop(0, toks // rows_step)
        def _(i, h=h):
            rows = pl.ds(pl.multiple_of(i * rows_step, rows_step), rows_step)
            raw = sref[h, rows, :] * scale
            e = jnp.exp(raw - jnp.max(raw, axis=-1, keepdims=True))
            p = e / jnp.sum(e, axis=-1, keepdims=True)
            sref[h, rows, :] = p
            pb[h, rows, :] = p.astype(BF16)

    def kv_terms(which, left, right, factor):
        def one(r):
            parts = [
                dot_tn(left[h, :, block_cols(r)], right[:, head_cols(h)]) for h in range(heads)
            ]
            full = jnp.concatenate(parts, axis=-1)
            return full * factor if factor != 1.0 else full

        term[which, 0] = one(3).astype(BF16)
        a = send(term.at[which, 0], from_sib.at[which, 0], sib)
        term[which, 1] = one(1).astype(BF16)
        b = send(term.at[which, 1], from_sib.at[which, 1], sib)
        mine = one(2)
        a.wait_recv()
        pair_sum[which] = (mine + from_sib[which, 0].astype(F32)).astype(BF16)
        c = send(pair_sum.at[which], from_xn.at[which], xn)
        own_term[which] = one(0)
        return b, c

    def kv_final(which, slot, b, c):
        b.wait_recv()
        c.wait_recv()
        total = own_term[which] + from_sib[which, 1].astype(F32) + from_xn[which].astype(F32)
        grads[slot] = total.astype(BF16)
        return send(grads.at[slot], grads_sib.at[slot], sib)

    v_pend = kv_terms(1, pb, ctx, 1.0)
    v_sib.wait_recv()
    dprobs(1)
    v_xn.wait_recv()
    v_fw = send(vbuf.at[2], vbuf.at[3], sib)
    f_xn.wait_recv()
    f_fw = send(fbuf.at[2], fbuf.at[3], sib)
    t_xn.wait_recv()
    t_fw = send(slotbuf.at[2], slotbuf.at[3], sib)
    dprobs(2)
    v_fw.wait_recv()
    dprobs(3)

    for h in range(heads):

        @pl.loop(0, toks // rows_step)
        def _(i, h=h):
            rows = pl.ds(pl.multiple_of(i * rows_step, rows_step), rows_step)
            p = sref[h, rows, :]
            dp = dpref[h, rows, :]
            delta = jnp.sum(p * dp, axis=-1, keepdims=True)
            dsb[h, rows, :] = (p * (dp - delta)).astype(BF16)

    k_pend = kv_terms(0, dsb, qbuf, scale)

    q_parts = []
    for h in range(heads):
        acc = dot_nn(dsb[h, :, block_cols(0)], kbuf[0, :, head_cols(h)])
        for r in range(1, 4):
            acc = acc + dot_nn(dsb[h, :, block_cols(r)], kbuf[r, :, head_cols(h)])
        q_parts.append(acc * scale)
    grads[0] = jnp.concatenate(q_parts, axis=-1).astype(BF16)
    g_copy = [None] * 3
    g_copy[0] = send(grads.at[0], grads_sib.at[0], sib)

    outs = (out_q, out_k, out_v)

    first_pos = (xi, iv)
    second_pos = (iv, xi)
    first_dev = (xn, yn)
    second_dev = (yn, xn)
    rs1_copy = {}
    rs2_copy = {}
    ag1_copy = {}
    ag2_copy = {}
    sib_copy = []

    def part_lanes(p):
        return pl.ds(pl.multiple_of(core * half + p * quart, 128), quart)

    def half_rows(p, mine):
        pos = first_pos[p] if mine else 1 - first_pos[p]
        return pl.ds(pl.multiple_of(pos * row_half, 16), row_half)

    def quarter_rows(p):
        return pl.ds(
            pl.multiple_of(first_pos[p] * row_half + second_pos[p] * row_q, 16), row_q
        )

    def dw_start(w):
        g_copy[w].wait_recv()
        for p in (1, 0):
            lanes = part_lanes(p)
            mine = dot_tn(grads[w], hid[:, lanes])
            theirs = dot_tn(grads_sib[w], hid_sib[:, p * quart : (p + 1) * quart])
            dwp[w, p] = (mine + theirs).astype(BF16)
            rs1_copy[w, p] = send(dwp.at[w, p, half_rows(p, False)], rs1.at[w, p], first_dev[p])

    def dw_second(w):
        for p in (1, 0):
            rs1_copy[w, p].wait_recv()
            own = dwp[w, p, half_rows(p, True), :].astype(F32)
            s1[w, p] = (own + rs1[w, p].astype(F32)).astype(BF16)
            away = pl.ds(pl.multiple_of((1 - second_pos[p]) * row_q, 16), row_q)
            rs2_copy[w, p] = send(s1.at[w, p, away], rs2.at[w, p], second_dev[p])

    def dw_gather1(w):
        for p in (1, 0):
            rs2_copy[w, p].wait_recv()
            keep = pl.ds(pl.multiple_of(second_pos[p] * row_q, 16), row_q)
            done = s1[w, p, keep, :].astype(F32) + rs2[w, p].astype(F32)
            outs[w][quarter_rows(p), part_lanes(p)] = done.astype(BF16)
            piece = outs[w].at[quarter_rows(p), part_lanes(p)]
            ag1_copy[w, p] = send(piece, piece, second_dev[p])

    def dw_gather2(w):
        for p in (1, 0):
            ag1_copy[w, p].wait_recv()
            piece = outs[w].at[half_rows(p, True), part_lanes(p)]
            ag2_copy[w, p] = send(piece, piece, first_dev[p])
            sib_copy.append(send(piece, piece, sib))

    def dw_last(w):
        for p in (1, 0):
            ag2_copy[w, p].wait_recv()
            piece = outs[w].at[half_rows(p, False), part_lanes(p)]
            sib_copy.append(send(piece, piece, sib))

    h_sib.wait_recv()
    dw_start(0)

    g_copy[2] = kv_final(1, 2, *v_pend)

    f_sib.wait_recv()
    t_sib.wait_recv()
    f_fw.wait_recv()
    t_fw.wait_recv()
    rows_all = slotbuf[0] + slotbuf[1] + slotbuf[2] + slotbuf[3]
    donor_row = rows_all[0:1, :]
    accept_row = rows_all[1:2, :]
    pred_row = rows_all[2:3, :]
    n_slots = rows_all.shape[1]
    tok_iota = lax.broadcasted_iota(jnp.int32, (toks, n_slots), 0)
    own_donor = None
    own_accept = None
    donor_t = jnp.zeros((PJ, n_slots), F32)
    accept_t = jnp.zeros((PJ, n_slots), F32)
    for r, shard in enumerate((sq, s_sib, s_xn, s_dg)):
        tok = (tok_iota + shard * toks).astype(F32)
        hot_d = jnp.where(tok == donor_row, 1.0, 0.0).astype(BF16)
        hot_a = jnp.where(tok == accept_row, 1.0, 0.0).astype(BF16)
        if r == 0:
            own_donor, own_accept = hot_d, hot_a
        donor_t = donor_t + dot_tn(fbuf[r], hot_d)
        accept_t = accept_t + dot_tn(fbuf[r], hot_a)
    pair_scale = PJ**-0.5
    pair = jnp.sum(donor_t * accept_t, axis=0, keepdims=True) * pair_scale
    slot_grad = pred_row * (1.0 / (1.0 + jnp.exp(-pair))) * pair_scale
    grad_feat = dot_nt(own_donor, (slot_grad * accept_t).astype(BF16)) + dot_nt(
        own_accept, (slot_grad * donor_t).astype(BF16)
    )
    grad_feat = grad_feat.astype(BF16)

    dw_start(2)
    dw_second(0)
    g_copy[1] = kv_final(0, 1, *k_pend)
    dw_start(1)

    cols = width // n_head
    z_copy = []

    def input_block(owner):
        lanes = pl.ds(pl.multiple_of(owner * cols, 128), cols)
        acc = dot_nn(grads[0], wq[:, lanes]) + dot_nn(grads[1], wk[:, lanes])
        acc = acc + dot_nn(grads[2], wv[:, lanes])
        wj_rows = wj[pl.ds(pl.multiple_of(owner * cols, 128), cols), :]
        return acc + dot_nt(grad_feat, wj_rows)

    for d in range(n_head - 1, 0, -1):
        zsend[d - 1] = input_block(lax.rem(hd + d, n_head)).astype(BF16)
        z_copy.append((d, send(zsend.at[d - 1], zrecv.at[d - 1], zpeers[d - 1])))
        if d == n_head - 1:
            dw_second(2)
        elif d == n_head - 2:
            dw_gather1(0)
    zown[...] = input_block(hd)
    dw_second(1)
    dw_gather1(2)
    dw_gather2(0)
    dw_gather1(1)
    dw_gather2(2)
    dw_last(0)
    dw_gather2(1)
    for d, copy in z_copy:
        copy.wait_recv()
    total = zown[...]
    for d in range(n_head - 1):
        total = total + zrecv[d].astype(F32)
    out_in[...] = total.astype(BF16)
    dw_last(2)
    dw_last(1)
    for copy in sib_copy:
        copy.wait_recv()
    for copy in started:
        copy.wait_send()
    assert counter[0] == n_copies


def fused_device(
    n_head,
    hidden_in,
    ctx_grad,
    w_query,
    w_key,
    w_value,
    w_junction,
    donor_pos,
    acceptor_pos,
    junction_counts,
    pred_grad,
):
    hidden = hidden_in[0]
    toks, width = hidden.shape
    feats = w_query.shape[0]
    heads = feats // HD
    n_seq = 4
    sq = lax.axis_index("seq")
    slot_dev = donor_pos.shape[3]
    slot_ids = lax.axis_index("head") * slot_dev + jnp.arange(slot_dev, dtype=jnp.int32)
    live = slot_ids[None, :] < junction_counts[0, 0][:, None]
    donor = (donor_pos[0, 0] + sq * toks).astype(F32)
    accept = (acceptor_pos[0, 0] + jnp.arange(n_seq, dtype=jnp.int32)[:, None] * toks).astype(F32)
    pred = jnp.where(live, pred_grad[0, 0], 0.0)
    n_own = n_seq * slot_dev
    packed = jnp.stack([donor, accept, pred]).reshape(3, 1, n_own)
    place = (jnp.arange(n_seq) == sq).reshape(1, n_seq, 1)
    packed = jnp.where(place, packed, 0.0).reshape(3, n_seq * n_own)
    slots = jnp.concatenate([packed, jnp.zeros((5, n_seq * n_own), F32)], axis=0)
    n_slots = n_seq * n_own
    n_copies = 58 + n_head - 1
    vmem = pl.BlockSpec(memory_space=pltpu.VMEM)
    half, quart = width // 2, width // 4
    cols = width // n_head
    scratch = [
        pltpu.VMEM((4, toks, feats), BF16),
        pltpu.VMEM((4, toks, feats), BF16),
        pltpu.VMEM((4, toks, PJ), BF16),
        pltpu.VMEM((4, 8, n_slots), F32),
        pltpu.VMEM((toks, feats), BF16),
        pltpu.VMEM((toks, half), BF16),
        pltpu.VMEM((heads, toks, 4 * toks), F32),
        pltpu.VMEM((heads, toks, 4 * toks), F32),
        pltpu.VMEM((heads, toks, 4 * toks), BF16),
        pltpu.VMEM((heads, toks, 4 * toks), BF16),
        pltpu.VMEM((2, 2, toks, feats), BF16),
        pltpu.VMEM((2, 2, toks, feats), BF16),
        pltpu.VMEM((2, toks, feats), BF16),
        pltpu.VMEM((2, toks, feats), BF16),
        pltpu.VMEM((2, toks, feats), F32),
        pltpu.VMEM((3, toks, feats), BF16),
        pltpu.VMEM((3, toks, feats), BF16),
        pltpu.VMEM((3, 2, feats, quart), BF16),
        pltpu.VMEM((3, 2, feats // 2, quart), BF16),
        pltpu.VMEM((3, 2, feats // 2, quart), BF16),
        pltpu.VMEM((3, 2, feats // 4, quart), BF16),
        pltpu.VMEM((n_head - 1, toks, cols), BF16),
        pltpu.VMEM((n_head - 1, toks, cols), BF16),
        pltpu.VMEM((toks, cols), F32),
        pltpu.SemaphoreType.DMA((n_copies,)),
        pltpu.SemaphoreType.DMA((n_copies,)),
    ]
    grad_w = jax.ShapeDtypeStruct((feats, width), BF16)
    out_in, out_q, out_k, out_v = pl.pallas_call(
        functools.partial(fused_kernel, n_head, n_copies),
        out_shape=(jax.ShapeDtypeStruct((toks, cols), BF16), grad_w, grad_w, grad_w),
        in_specs=[vmem] * 7,
        out_specs=(vmem,) * 4,
        scratch_shapes=scratch,
        compiler_params=pltpu.CompilerParams(
            collective_id=0, has_side_effects=True, vmem_limit_bytes=56 * 1024 * 1024
        ),
        name="attention_backward",
    )(hidden, ctx_grad[0], w_query, w_key, w_value, w_junction, slots)
    return out_in[None], out_q, out_k, out_v


def on_device(
    hidden_in,
    ctx_grad,
    w_query,
    w_key,
    w_value,
    w_junction,
    donor_pos,
    acceptor_pos,
    junction_counts,
    pred_grad,
):
    hidden = hidden_in[0]
    local_len = hidden.shape[0]
    shard_count = lax.axis_size("seq")
    total_len = local_len * shard_count
    heads_dev = w_query.shape[0] // HD
    softmax_scale = HD ** (-0.5)
    pair_scale = PJ ** (-0.5)
    queries = jnp.einsum("td,cd->tc", hidden, w_query, preferred_element_type=jnp.float32).astype(
        jnp.bfloat16
    )
    key_rows = jnp.einsum("td,cd->tc", hidden, w_key, preferred_element_type=jnp.float32).astype(
        jnp.bfloat16
    )
    value_rows = jnp.einsum(
        "td,cd->tc", hidden, w_value, preferred_element_type=jnp.float32
    ).astype(jnp.bfloat16)
    features = jnp.dot(hidden, w_junction, preferred_element_type=jnp.float32).astype(jnp.bfloat16)
    all_keys, all_values, all_features = (
        lax.all_gather(key_rows, "seq", axis=0, tiled=True),
        lax.all_gather(value_rows, "seq", axis=0, tiled=True),
        lax.all_gather(features, "seq", axis=0, tiled=True),
    )
    query_heads = queries.reshape(local_len, heads_dev, HD)
    grad_heads = ctx_grad[0].reshape(local_len, heads_dev, HD)
    key_heads = all_keys.reshape(total_len, heads_dev, HD)
    value_heads = all_values.reshape(total_len, heads_dev, HD)
    scores = (
        jnp.einsum("qhd,khd->hqk", query_heads, key_heads, preferred_element_type=jnp.float32)
        * softmax_scale
    )
    row_max = jnp.max(scores, axis=-1, keepdims=True)
    expd = jnp.exp(scores - row_max)
    probs = expd / jnp.sum(expd, axis=-1, keepdims=True)
    dprobs = jnp.einsum("qhd,khd->hqk", grad_heads, value_heads, preferred_element_type=jnp.float32)
    row_delta = jnp.sum(probs * dprobs, axis=-1, keepdims=True)
    dscores = probs * (dprobs - row_delta)
    probs_b = probs.astype(jnp.bfloat16)
    dscores_b = dscores.astype(jnp.bfloat16)
    query_grad = (
        (
            jnp.einsum("hqk,khd->qhd", dscores_b, key_heads, preferred_element_type=jnp.float32)
            * softmax_scale
        )
        .astype(jnp.bfloat16)
        .reshape(local_len, heads_dev * HD)
    )
    key_term = (
        jnp.einsum("hqk,qhd->khd", dscores_b, query_heads, preferred_element_type=jnp.float32)
        * softmax_scale
    ).reshape(total_len, heads_dev * HD)
    value_term = jnp.einsum(
        "hqk,qhd->khd", probs_b, grad_heads, preferred_element_type=jnp.float32
    ).reshape(total_len, heads_dev * HD)
    key_sum, value_sum = (
        lax.psum_scatter(
            key_term.astype(jnp.bfloat16), "seq", scatter_dimension=0, tiled=True
        ).astype(jnp.float32),
        lax.psum_scatter(
            value_term.astype(jnp.bfloat16), "seq", scatter_dimension=0, tiled=True
        ).astype(jnp.float32),
    )
    key_grad = key_sum.astype(jnp.bfloat16)
    value_grad = value_sum.astype(jnp.bfloat16)
    donor_idx = donor_pos[0, 0]
    accept_idx = acceptor_pos[0, 0]
    slot_dev = donor_idx.shape[1]
    slot_ids = lax.axis_index("head") * slot_dev + jnp.arange(slot_dev, dtype=jnp.int32)
    live_slots = slot_ids[None, :] < junction_counts[0, 0][:, None]
    donor_feat = features[donor_idx].astype(jnp.float32)
    accept_glob = jnp.arange(shard_count, dtype=jnp.int32)[:, None] * local_len + accept_idx
    accept_rows = all_features[accept_glob]
    accept_feat = accept_rows.astype(jnp.float32)
    pair_score = jnp.sum(donor_feat * accept_feat, axis=-1) * pair_scale
    slot_grad = (
        jnp.where(live_slots, pred_grad[0, 0] * jax.nn.sigmoid(pair_score), 0.0) * pair_scale
    )
    donor_term = slot_grad[..., None] * accept_feat
    accept_term = slot_grad[..., None] * donor_feat
    pair_width = features.shape[1]
    grad_feat = (
        jnp.zeros((local_len, pair_width), jnp.float32)
        .at[donor_idx.reshape(-1)]
        .add(donor_term.reshape(-1, pair_width))
    )
    spread_term = (
        jnp.zeros((total_len, pair_width), jnp.float32)
        .at[accept_glob.reshape(-1)]
        .add(accept_term.reshape(-1, pair_width))
    )
    grad_feat = grad_feat + lax.psum_scatter(
        spread_term.astype(jnp.bfloat16), "seq", scatter_dimension=0, tiled=True
    ).astype(jnp.float32)
    grad_feat_b = grad_feat.astype(jnp.bfloat16)
    input_term = jnp.einsum("tc,cd->td", query_grad, w_query, preferred_element_type=jnp.float32)
    input_term = input_term + jnp.einsum(
        "tc,cd->td", key_grad, w_key, preferred_element_type=jnp.float32
    )
    input_term = input_term + jnp.einsum(
        "tc,cd->td", value_grad, w_value, preferred_element_type=jnp.float32
    )
    input_term = input_term + jnp.einsum(
        "tp,dp->td", grad_feat_b, w_junction, preferred_element_type=jnp.float32
    )
    grad_input = lax.psum_scatter(
        input_term.astype(jnp.bfloat16), "head", scatter_dimension=1, tiled=True
    )
    key_wterm = jnp.einsum("tc,td->cd", key_grad, hidden, preferred_element_type=jnp.float32)
    value_wterm = jnp.einsum("tc,td->cd", value_grad, hidden, preferred_element_type=jnp.float32)
    query_wterm = jnp.einsum("tc,td->cd", query_grad, hidden, preferred_element_type=jnp.float32)
    query_wsum, key_wsum, value_wsum = lax.psum(
        (query_wterm, key_wterm, value_wterm), ("interval", "seq")
    )
    return (
        grad_input[None],
        query_wsum.astype(jnp.bfloat16),
        key_wsum.astype(jnp.bfloat16),
        value_wsum.astype(jnp.bfloat16),
    )


def solution(mesh):
    placed = (
        P("interval", "seq", None),
        P("interval", "seq", "head"),
        P("head", None),
        P("head", None),
        P("head", None),
        P(),
        P("interval", "seq", None, "head"),
        P("interval", "seq", None, "head"),
        P("interval", "seq", None),
        P("interval", "seq", None, "head"),
    )
    shape = dict(mesh.shape)
    fits = shape["interval"] == 2 and shape["seq"] == 4 and shape["head"] == 4
    run = functools.partial(fused_device, shape["head"]) if fits else on_device
    return jax.shard_map(
        run,
        mesh=mesh,
        in_specs=placed,
        out_specs=(P("interval", "seq", "head"), P("head", None), P("head", None), P("head", None)),
        check_vma=False,
    )
```

```python
import functools

import jax
import jax.numpy as jnp
from jax import lax
from jax.experimental import pallas as pl
from jax.experimental.pallas import tpu as pltpu
from jax.sharding import PartitionSpec as P

HD = 192
PJ = 128
MESH = pl.DeviceIdType.MESH
F32 = jnp.float32
BF16 = jnp.bfloat16


def dot_nn(a, b):
    return lax.dot_general(a, b, (((1,), (0,)), ((), ())), preferred_element_type=F32)


def dot_nt(a, b):
    return lax.dot_general(a, b, (((1,), (1,)), ((), ())), preferred_element_type=F32)


def dot_tn(a, b):
    return lax.dot_general(a, b, (((0,), (0,)), ((), ())), preferred_element_type=F32)


def fused_kernel(
    n_head,
    n_copies,
    hid_hbm,
    ctx_hbm,
    wq_hbm,
    wk_hbm,
    wv_hbm,
    wj_hbm,
    donor,
    accept,
    counts,
    pred,
    in_hbm,
    q_hbm,
    k_hbm,
    v_hbm,
    hidbuf,
    ctx,
    wq,
    wk,
    wv,
    wj,
    out_in,
    out_q,
    out_k,
    out_v,
    kbuf,
    vbuf,
    fbuf,
    slotbuf,
    qbuf,
    q_t,
    ctx_t,
    sref,
    dpref,
    pb,
    dsb,
    term,
    from_sib,
    pair_sum,
    from_xn,
    own_term,
    grads,
    grads_t,
    gcat,
    dwp,
    rsum,
    zsend,
    zrecv,
    zown,
    send_sems,
    recv_sems,
    load_sems,
    store_sems,
):
    toks = ctx.shape[0]
    width = hidbuf.shape[1]
    feats = wq.shape[0]
    heads = feats // HD
    half = width // 2
    row_y = feats // 2
    row_c = feats // 4
    row_x = feats // 8
    scale = HD**-0.5
    iv = lax.axis_index("interval")
    sq = lax.axis_index("seq")
    hd = lax.axis_index("head")
    xi = lax.div(sq, 2)
    core = lax.rem(sq, 2)
    s_sib = sq + 1 - 2 * core
    s_xn = lax.rem(sq + 2, 4)
    s_dg = lax.rem(s_sib + 2, 4)
    sib = (iv, s_sib, hd)
    xn = (iv, s_xn, hd)
    yn = (1 - iv, sq, hd)
    ysib = (1 - iv, s_sib, hd)
    zpeers = [(iv, sq, lax.rem(hd + d, n_head)) for d in range(1, n_head)]
    hid = hidbuf.at[0:toks]

    loads = []
    for i, (src, dst) in enumerate(
        (
            (hid_hbm.at[0], hid),
            (wk_hbm, wk),
            (wv_hbm, wv),
            (wq_hbm, wq),
            (wj_hbm, wj),
            (ctx_hbm.at[0], ctx),
        )
    ):
        load = pltpu.make_async_copy(src, dst, load_sems.at[i])
        load.start()
        loads.append(load)

    counter = [0]
    started = []

    def send(src, dst, dev):
        i = counter[0]
        counter[0] += 1
        copy = pltpu.make_async_remote_copy(
            src_ref=src,
            dst_ref=dst,
            send_sem=send_sems.at[i],
            recv_sem=recv_sems.at[i],
            device_id=dev,
            device_id_type=MESH,
        )
        copy.start()
        started.append(copy)
        return copy

    stores = []

    def store(src, dst):
        copy = pltpu.make_async_copy(src, dst, store_sems.at[len(stores)])
        copy.start()
        stores.append(copy)

    barrier = pltpu.get_barrier_semaphore()
    peers = [sib, xn, yn, ysib] + zpeers
    for dev in peers:
        pl.semaphore_signal(barrier, inc=1, device_id=dev, device_id_type=MESH)

    loads[0].wait()
    loads[1].wait()
    kbuf[0] = dot_nt(hid[...], wk[...]).astype(BF16)
    pl.semaphore_wait(barrier, len(peers))
    k_xn = send(kbuf.at[0], kbuf.at[2], xn)
    k_sib = send(kbuf.at[0], kbuf.at[1], sib)
    hid_yn = []
    for p in range(2):
        lanes = slice(p * half, (p + 1) * half)
        hid_yn.append(send(hidbuf.at[0:toks, lanes], hidbuf.at[2 * toks : 3 * toks, lanes], yn))
    loads[2].wait()
    vbuf[0] = dot_nt(hid[...], wv[...]).astype(BF16)
    v_xn = send(vbuf.at[0], vbuf.at[2], xn)
    v_sib = send(vbuf.at[0], vbuf.at[1], sib)
    loads[3].wait()
    q_full = dot_nt(hid[...], wq[...])
    qbuf[...] = q_full.astype(BF16)
    q_t[...] = jnp.transpose(q_full).astype(BF16)
    loads[4].wait()
    fbuf[0] = dot_nn(hid[...], wj[...]).astype(BF16)
    f_xn = send(fbuf.at[0], fbuf.at[2], xn)
    f_sib = send(fbuf.at[0], fbuf.at[1], sib)

    n_acc, slot_dev = donor.shape[2], donor.shape[3]
    n_slots = slotbuf.shape[2]
    acc_iota = lax.broadcasted_iota(jnp.int32, (n_acc, slot_dev), 0)
    slot_ids = lax.broadcasted_iota(jnp.int32, (n_acc, slot_dev), 1) + hd * slot_dev
    live_count = jnp.zeros((n_acc, slot_dev), jnp.int32)
    for j in range(n_acc):
        live_count = jnp.where(acc_iota == j, counts[0, :, j : j + 1], live_count)
    donor_tok = (donor[0, 0] + sq * toks).astype(F32)
    accept_tok = (accept[0, 0] + acc_iota * toks).astype(F32)
    pred_live = jnp.where(slot_ids < live_count, pred[0, 0], 0.0)
    lane_iota = lax.broadcasted_iota(jnp.int32, (n_acc, n_slots), 1)
    row_iota = lax.broadcasted_iota(jnp.int32, (n_acc, n_slots), 0)
    place = lane_iota - (sq * n_acc + row_iota) * slot_dev
    slotbuf[0] = jnp.zeros(slotbuf.shape[1:], F32)
    for i, values in enumerate((donor_tok, accept_tok, pred_live)):
        spread = jnp.zeros((n_acc, n_slots), F32)
        for j in range(slot_dev):
            spread = jnp.where(place == j, values[:, j : j + 1], spread)
        slotbuf[0, i : i + 1, :] = jnp.sum(spread, axis=0, keepdims=True)
    t_xn = send(slotbuf.at[0], slotbuf.at[2], xn)
    t_sib = send(slotbuf.at[0], slotbuf.at[1], sib)
    hid_sib = send(hidbuf.at[0:toks], hidbuf.at[toks : 2 * toks], sib)

    def head_cols(h):
        return slice(h * HD, (h + 1) * HD)

    def block_cols(r):
        return slice(r * toks, (r + 1) * toks)

    def scores(r):
        for h in range(heads):
            sref[h, :, block_cols(r)] = dot_nt(qbuf[:, head_cols(h)], kbuf[r, :, head_cols(h)])

    def dprobs(r):
        for h in range(heads):
            dpref[h, :, block_cols(r)] = dot_nt(ctx[:, head_cols(h)], vbuf[r, :, head_cols(h)])

    scores(0)
    loads[5].wait()
    ctx_t[...] = jnp.transpose(ctx[...].astype(F32)).astype(BF16)
    dprobs(0)
    k_sib.wait_recv()
    scores(1)
    k_xn.wait_recv()
    k_fw = send(kbuf.at[2], kbuf.at[3], sib)
    scores(2)
    k_fw.wait_recv()
    scores(3)

    rows_step = 32

    for h in range(heads):

        @pl.loop(0, toks // rows_step)
        def _(i, h=h):
            rows = pl.ds(pl.multiple_of(i * rows_step, rows_step), rows_step)
            raw = sref[h, rows, :] * scale
            e = jnp.exp(raw - jnp.max(raw, axis=-1, keepdims=True))
            p = e / jnp.sum(e, axis=-1, keepdims=True)
            sref[h, rows, :] = p
            pb[h, rows, :] = p.astype(BF16)

    def kv_terms(which, left_t, right, factor):
        def one(h, r):
            part = dot_nn(left_t[head_cols(h), :], right[h, :, block_cols(r)])
            return part * factor if factor != 1.0 else part

        for h in range(heads):
            term[which, 0, head_cols(h), :] = one(h, 3).astype(BF16)
        a = send(term.at[which, 0], from_sib.at[which, 0], sib)
        for h in range(heads):
            term[which, 1, head_cols(h), :] = one(h, 1).astype(BF16)
        b = send(term.at[which, 1], from_sib.at[which, 1], sib)
        for h in range(heads):
            own_term[which, head_cols(h), :] = one(h, 2)
        a.wait_recv()
        pair_sum[which] = (own_term[which] + from_sib[which, 0].astype(F32)).astype(BF16)
        c = send(pair_sum.at[which], from_xn.at[which], xn)
        for h in range(heads):
            own_term[which, head_cols(h), :] = one(h, 0)
        return b, c

    def g_rows(y, c):
        return pl.ds(pl.multiple_of(y * row_y + c * row_c, 16), row_c)

    g_copy = [None] * 3

    def exchange(slot):
        gcat[slot, :, 0:toks] = grads_t[slot, g_rows(iv, core), :]
        copies = []
        for b, dev, y, c in ((2, yn, 1 - iv, core), (3, ysib, 1 - iv, 1 - core), (1, sib, iv, 1 - core)):
            copies.append(
                send(grads_t.at[slot, g_rows(y, c)], gcat.at[slot, :, block_cols(b)], dev)
            )
        g_copy[slot] = copies

    def kv_final(which, slot, b, c):
        b.wait_recv()
        c.wait_recv()
        total = own_term[which] + from_sib[which, 1].astype(F32) + from_xn[which].astype(F32)
        grads_t[slot] = total.astype(BF16)
        exchange(slot)
        grads[slot] = jnp.transpose(total).astype(BF16)

    v_pend = kv_terms(1, ctx_t, pb, 1.0)
    v_sib.wait_recv()
    dprobs(1)
    v_xn.wait_recv()
    v_fw = send(vbuf.at[2], vbuf.at[3], sib)
    dprobs(2)
    v_fw.wait_recv()
    dprobs(3)

    for h in range(heads):

        @pl.loop(0, toks // rows_step)
        def _(i, h=h):
            rows = pl.ds(pl.multiple_of(i * rows_step, rows_step), rows_step)
            p = sref[h, rows, :]
            dp = dpref[h, rows, :]
            delta = jnp.sum(p * dp, axis=-1, keepdims=True)
            dsb[h, rows, :] = (p * (dp - delta)).astype(BF16)

    k_pend = kv_terms(0, q_t, dsb, scale)

    q_parts = []
    for h in range(heads):
        acc = dot_nn(dsb[h, :, block_cols(0)], kbuf[0, :, head_cols(h)])
        for r in range(1, 4):
            acc = acc + dot_nn(dsb[h, :, block_cols(r)], kbuf[r, :, head_cols(h)])
        q_parts.append(acc * scale)
    q_grad = jnp.concatenate(q_parts, axis=-1)
    grads_t[0] = jnp.transpose(q_grad).astype(BF16)
    exchange(0)
    grads[0] = q_grad.astype(BF16)

    f_xn.wait_recv()
    f_fw = send(fbuf.at[2], fbuf.at[3], sib)
    t_xn.wait_recv()
    t_fw = send(slotbuf.at[2], slotbuf.at[3], sib)
    hid_fw = []
    for p in range(2):
        lanes = slice(p * half, (p + 1) * half)
        hid_yn[p].wait_recv()
        hid_fw.append(
            send(hidbuf.at[2 * toks : 3 * toks, lanes], hidbuf.at[3 * toks : 4 * toks, lanes], sib)
        )

    outs = (out_q, out_k, out_v)
    outs_hbm = (q_hbm, k_hbm, v_hbm)
    pos = (xi, iv)
    rs_copy = {}
    piece_copy = {}
    fwd_copy = {}
    sib_copy = {0: [], 1: [], 2: []}

    def x_rows(x):
        return pl.ds(pl.multiple_of(x * row_x, 16), row_x)

    def piece(w, p, y, x):
        start = pl.multiple_of(y * row_y + core * row_c + x * row_x, 16)
        return outs[w].at[pl.ds(start, row_x), slice(p * half, (p + 1) * half)]

    def to_sib(w, ref):
        sib_copy[w].append(send(ref, ref, sib))

    def dw_start(w):
        for copy in g_copy[w]:
            copy.wait_recv()
        for p in range(2):
            dwp[w, p] = dot_nn(gcat[w], hidbuf[:, p * half : (p + 1) * half]).astype(BF16)
            rs_copy[w, p] = send(dwp.at[w, p, x_rows(1 - xi)], rsum.at[w, p], xn)

    def dw_final(w):
        for p in range(2):
            rs_copy[w, p].wait_recv()
            done = dwp[w, p, x_rows(xi), :].astype(F32) + rsum[w, p].astype(F32)
            ref = piece(w, p, iv, xi)
            ref[...] = done.astype(BF16)
            cx = send(ref, ref, xn)
            cy = send(ref, ref, yn)
            piece_copy[w, p] = (cx, cy)
            to_sib(w, ref)

    def dw_forward(w):
        for p in range(2):
            cx, cy = piece_copy[w, p]
            cx_ref = piece(w, p, iv, 1 - xi)
            cy_ref = piece(w, p, 1 - iv, xi)
            if p == 0:
                cx.wait_recv()
                fwd_copy[w, p] = send(cx_ref, cx_ref, yn)
                to_sib(w, cx_ref)
                cy.wait_recv()
                to_sib(w, cy_ref)
            else:
                cy.wait_recv()
                fwd_copy[w, p] = send(cy_ref, cy_ref, xn)
                to_sib(w, cy_ref)
                cx.wait_recv()
                to_sib(w, cx_ref)

    def dw_last(w):
        for p in range(2):
            fwd_copy[w, p].wait_recv()
            to_sib(w, piece(w, p, 1 - iv, 1 - xi))

    def dw_out(w):
        for copy in sib_copy[w]:
            copy.wait_recv()
        store(outs[w], outs_hbm[w])

    kv_final(1, 2, *v_pend)
    hid_sib.wait_recv()
    hid_fw[0].wait_recv()
    hid_fw[1].wait_recv()
    dw_start(0)
    dw_start(2)

    f_sib.wait_recv()
    t_sib.wait_recv()
    f_fw.wait_recv()
    t_fw.wait_recv()
    rows_all = slotbuf[0] + slotbuf[1] + slotbuf[2] + slotbuf[3]
    donor_row = rows_all[0:1, :]
    accept_row = rows_all[1:2, :]
    pred_row = rows_all[2:3, :]
    tok_iota = lax.broadcasted_iota(jnp.int32, (toks, n_slots), 0)
    own_donor = None
    own_accept = None
    donor_t = jnp.zeros((PJ, n_slots), F32)
    accept_t = jnp.zeros((PJ, n_slots), F32)
    for r, shard in enumerate((sq, s_sib, s_xn, s_dg)):
        tok = (tok_iota + shard * toks).astype(F32)
        hot_d = jnp.where(tok == donor_row, 1.0, 0.0).astype(BF16)
        hot_a = jnp.where(tok == accept_row, 1.0, 0.0).astype(BF16)
        if r == 0:
            own_donor, own_accept = hot_d, hot_a
        donor_t = donor_t + dot_tn(fbuf[r], hot_d)
        accept_t = accept_t + dot_tn(fbuf[r], hot_a)
    pair_scale = PJ**-0.5
    pair = jnp.sum(donor_t * accept_t, axis=0, keepdims=True) * pair_scale
    slot_grad = pred_row * (1.0 / (1.0 + jnp.exp(-pair))) * pair_scale
    grad_feat = dot_nt(own_donor, (slot_grad * accept_t).astype(BF16)) + dot_nt(
        own_accept, (slot_grad * donor_t).astype(BF16)
    )
    grad_feat = grad_feat.astype(BF16)

    kv_final(0, 1, *k_pend)
    dw_final(0)
    dw_start(1)

    cols = width // n_head
    z_copy = []

    def input_block(owner):
        lanes = pl.ds(pl.multiple_of(owner * cols, 128), cols)
        acc = dot_nn(grads[0], wq[:, lanes]) + dot_nn(grads[1], wk[:, lanes])
        acc = acc + dot_nn(grads[2], wv[:, lanes])
        return acc + dot_nt(grad_feat, wj[lanes, :])

    for d in range(n_head - 1, 0, -1):
        zsend[d - 1] = input_block(lax.rem(hd + d, n_head)).astype(BF16)
        z_copy.append((d, send(zsend.at[d - 1], zrecv.at[d - 1], zpeers[d - 1])))
        if d == n_head - 1:
            dw_final(2)
    zown[...] = input_block(hd)
    dw_forward(0)
    dw_final(1)
    dw_forward(2)
    dw_last(0)
    dw_forward(1)
    dw_last(2)
    dw_out(0)
    dw_last(1)
    for d, copy in z_copy:
        copy.wait_recv()
    total = zown[...]
    for d in range(n_head - 1):
        total = total + zrecv[d].astype(F32)
    out_in[...] = total.astype(BF16)
    store(out_in, in_hbm.at[0])
    dw_out(2)
    dw_out(1)
    for copy in started:
        copy.wait_send()
    for copy in stores:
        copy.wait()
    assert counter[0] <= n_copies


def write_kernel(*refs):
    n = 4
    copies = [pltpu.make_async_copy(refs[i], refs[n + i], refs[2 * n].at[i]) for i in range(n)]
    for copy in copies:
        copy.start()
    for copy in copies:
        copy.wait()


def fused_device(
    n_head,
    hidden_in,
    ctx_grad,
    w_query,
    w_key,
    w_value,
    w_junction,
    donor_pos,
    acceptor_pos,
    junction_counts,
    pred_grad,
):
    toks, width = hidden_in.shape[1:]
    feats = w_query.shape[0]
    heads = feats // HD
    n_seq = 4
    n_slots = n_seq * donor_pos.shape[2] * donor_pos.shape[3]
    n_copies = 96
    vmem = pl.BlockSpec(memory_space=pltpu.VMEM)
    hbm = pl.BlockSpec(memory_space=pl.ANY)
    half = width // 2
    cols = width // n_head
    scratch = [
        pltpu.VMEM((4 * toks, width), BF16),
        pltpu.VMEM((toks, feats), BF16),
        pltpu.VMEM((feats, width), BF16),
        pltpu.VMEM((feats, width), BF16),
        pltpu.VMEM((feats, width), BF16),
        pltpu.VMEM((width, PJ), BF16),
        pltpu.VMEM((toks, cols), BF16),
        pltpu.VMEM((feats, width), BF16),
        pltpu.VMEM((feats, width), BF16),
        pltpu.VMEM((feats, width), BF16),
        pltpu.VMEM((4, toks, feats), BF16),
        pltpu.VMEM((4, toks, feats), BF16),
        pltpu.VMEM((4, toks, PJ), BF16),
        pltpu.VMEM((4, 8, n_slots), F32),
        pltpu.VMEM((toks, feats), BF16),
        pltpu.VMEM((feats, toks), BF16),
        pltpu.VMEM((feats, toks), BF16),
        pltpu.VMEM((heads, toks, 4 * toks), F32),
        pltpu.VMEM((heads, toks, 4 * toks), F32),
        pltpu.VMEM((heads, toks, 4 * toks), BF16),
        pltpu.VMEM((heads, toks, 4 * toks), BF16),
        pltpu.VMEM((2, 2, feats, toks), BF16),
        pltpu.VMEM((2, 2, feats, toks), BF16),
        pltpu.VMEM((2, feats, toks), BF16),
        pltpu.VMEM((2, feats, toks), BF16),
        pltpu.VMEM((2, feats, toks), F32),
        pltpu.VMEM((3, toks, feats), BF16),
        pltpu.VMEM((3, feats, toks), BF16),
        pltpu.VMEM((3, feats // 4, 4 * toks), BF16),
        pltpu.VMEM((3, 2, feats // 4, half), BF16),
        pltpu.VMEM((3, 2, feats // 8, half), BF16),
        pltpu.VMEM((n_head - 1, toks, cols), BF16),
        pltpu.VMEM((n_head - 1, toks, cols), BF16),
        pltpu.VMEM((toks, cols), F32),
        pltpu.SemaphoreType.DMA((n_copies,)),
        pltpu.SemaphoreType.DMA((n_copies,)),
        pltpu.SemaphoreType.DMA((6,)),
        pltpu.SemaphoreType.DMA((4,)),
    ]
    grad_w = jax.ShapeDtypeStruct((feats, width), BF16)
    shapes = (jax.ShapeDtypeStruct((1, toks, cols), BF16), grad_w, grad_w, grad_w)
    results = pl.pallas_call(
        functools.partial(fused_kernel, n_head, n_copies),
        out_shape=shapes,
        in_specs=[hbm] * 6 + [vmem] * 4,
        out_specs=(hbm,) * 4,
        scratch_shapes=scratch,
        compiler_params=pltpu.CompilerParams(
            collective_id=0, has_side_effects=True, vmem_limit_bytes=56 * 1024 * 1024
        ),
        name="attention_backward",
    )(
        hidden_in,
        ctx_grad,
        w_query,
        w_key,
        w_value,
        w_junction,
        donor_pos,
        acceptor_pos,
        junction_counts,
        pred_grad,
    )
    return pl.pallas_call(
        write_kernel,
        out_shape=shapes,
        in_specs=[hbm] * 4,
        out_specs=(hbm,) * 4,
        scratch_shapes=[pltpu.SemaphoreType.DMA((4,))],
        name="write_results",
    )(*results)


def on_device(
    hidden_in,
    ctx_grad,
    w_query,
    w_key,
    w_value,
    w_junction,
    donor_pos,
    acceptor_pos,
    junction_counts,
    pred_grad,
):
    hidden = hidden_in[0]
    local_len = hidden.shape[0]
    shard_count = lax.axis_size("seq")
    total_len = local_len * shard_count
    heads_dev = w_query.shape[0] // HD
    softmax_scale = HD ** (-0.5)
    pair_scale = PJ ** (-0.5)
    queries = jnp.einsum("td,cd->tc", hidden, w_query, preferred_element_type=jnp.float32).astype(
        jnp.bfloat16
    )
    key_rows = jnp.einsum("td,cd->tc", hidden, w_key, preferred_element_type=jnp.float32).astype(
        jnp.bfloat16
    )
    value_rows = jnp.einsum(
        "td,cd->tc", hidden, w_value, preferred_element_type=jnp.float32
    ).astype(jnp.bfloat16)
    features = jnp.dot(hidden, w_junction, preferred_element_type=jnp.float32).astype(jnp.bfloat16)
    all_keys, all_values, all_features = (
        lax.all_gather(key_rows, "seq", axis=0, tiled=True),
        lax.all_gather(value_rows, "seq", axis=0, tiled=True),
        lax.all_gather(features, "seq", axis=0, tiled=True),
    )
    query_heads = queries.reshape(local_len, heads_dev, HD)
    grad_heads = ctx_grad[0].reshape(local_len, heads_dev, HD)
    key_heads = all_keys.reshape(total_len, heads_dev, HD)
    value_heads = all_values.reshape(total_len, heads_dev, HD)
    scores = (
        jnp.einsum("qhd,khd->hqk", query_heads, key_heads, preferred_element_type=jnp.float32)
        * softmax_scale
    )
    row_max = jnp.max(scores, axis=-1, keepdims=True)
    expd = jnp.exp(scores - row_max)
    probs = expd / jnp.sum(expd, axis=-1, keepdims=True)
    dprobs = jnp.einsum("qhd,khd->hqk", grad_heads, value_heads, preferred_element_type=jnp.float32)
    row_delta = jnp.sum(probs * dprobs, axis=-1, keepdims=True)
    dscores = probs * (dprobs - row_delta)
    probs_b = probs.astype(jnp.bfloat16)
    dscores_b = dscores.astype(jnp.bfloat16)
    query_grad = (
        (
            jnp.einsum("hqk,khd->qhd", dscores_b, key_heads, preferred_element_type=jnp.float32)
            * softmax_scale
        )
        .astype(jnp.bfloat16)
        .reshape(local_len, heads_dev * HD)
    )
    key_term = (
        jnp.einsum("hqk,qhd->khd", dscores_b, query_heads, preferred_element_type=jnp.float32)
        * softmax_scale
    ).reshape(total_len, heads_dev * HD)
    value_term = jnp.einsum(
        "hqk,qhd->khd", probs_b, grad_heads, preferred_element_type=jnp.float32
    ).reshape(total_len, heads_dev * HD)
    key_sum, value_sum = (
        lax.psum_scatter(
            key_term.astype(jnp.bfloat16), "seq", scatter_dimension=0, tiled=True
        ).astype(jnp.float32),
        lax.psum_scatter(
            value_term.astype(jnp.bfloat16), "seq", scatter_dimension=0, tiled=True
        ).astype(jnp.float32),
    )
    key_grad = key_sum.astype(jnp.bfloat16)
    value_grad = value_sum.astype(jnp.bfloat16)
    donor_idx = donor_pos[0, 0]
    accept_idx = acceptor_pos[0, 0]
    slot_dev = donor_idx.shape[1]
    slot_ids = lax.axis_index("head") * slot_dev + jnp.arange(slot_dev, dtype=jnp.int32)
    live_slots = slot_ids[None, :] < junction_counts[0, 0][:, None]
    donor_feat = features[donor_idx].astype(jnp.float32)
    accept_glob = jnp.arange(shard_count, dtype=jnp.int32)[:, None] * local_len + accept_idx
    accept_rows = all_features[accept_glob]
    accept_feat = accept_rows.astype(jnp.float32)
    pair_score = jnp.sum(donor_feat * accept_feat, axis=-1) * pair_scale
    slot_grad = (
        jnp.where(live_slots, pred_grad[0, 0] * jax.nn.sigmoid(pair_score), 0.0) * pair_scale
    )
    donor_term = slot_grad[..., None] * accept_feat
    accept_term = slot_grad[..., None] * donor_feat
    pair_width = features.shape[1]
    grad_feat = (
        jnp.zeros((local_len, pair_width), jnp.float32)
        .at[donor_idx.reshape(-1)]
        .add(donor_term.reshape(-1, pair_width))
    )
    spread_term = (
        jnp.zeros((total_len, pair_width), jnp.float32)
        .at[accept_glob.reshape(-1)]
        .add(accept_term.reshape(-1, pair_width))
    )
    grad_feat = grad_feat + lax.psum_scatter(
        spread_term.astype(jnp.bfloat16), "seq", scatter_dimension=0, tiled=True
    ).astype(jnp.float32)
    grad_feat_b = grad_feat.astype(jnp.bfloat16)
    input_term = jnp.einsum("tc,cd->td", query_grad, w_query, preferred_element_type=jnp.float32)
    input_term = input_term + jnp.einsum(
        "tc,cd->td", key_grad, w_key, preferred_element_type=jnp.float32
    )
    input_term = input_term + jnp.einsum(
        "tc,cd->td", value_grad, w_value, preferred_element_type=jnp.float32
    )
    input_term = input_term + jnp.einsum(
        "tp,dp->td", grad_feat_b, w_junction, preferred_element_type=jnp.float32
    )
    grad_input = lax.psum_scatter(
        input_term.astype(jnp.bfloat16), "head", scatter_dimension=1, tiled=True
    )
    key_wterm = jnp.einsum("tc,td->cd", key_grad, hidden, preferred_element_type=jnp.float32)
    value_wterm = jnp.einsum("tc,td->cd", value_grad, hidden, preferred_element_type=jnp.float32)
    query_wterm = jnp.einsum("tc,td->cd", query_grad, hidden, preferred_element_type=jnp.float32)
    query_wsum, key_wsum, value_wsum = lax.psum(
        (query_wterm, key_wterm, value_wterm), ("interval", "seq")
    )
    return (
        grad_input[None],
        query_wsum.astype(jnp.bfloat16),
        key_wsum.astype(jnp.bfloat16),
        value_wsum.astype(jnp.bfloat16),
    )


def solution(mesh):
    placed = (
        P("interval", "seq", None),
        P("interval", "seq", "head"),
        P("head", None),
        P("head", None),
        P("head", None),
        P(),
        P("interval", "seq", None, "head"),
        P("interval", "seq", None, "head"),
        P("interval", "seq", None),
        P("interval", "seq", None, "head"),
    )
    shape = dict(mesh.shape)
    fits = shape["interval"] == 2 and shape["seq"] == 4 and shape["head"] == 4
    run = functools.partial(fused_device, shape["head"]) if fits else on_device
    return jax.shard_map(
        run,
        mesh=mesh,
        in_specs=placed,
        out_specs=(P("interval", "seq", "head"), P("head", None), P("head", None), P("head", None)),
        check_vma=False,
    )
```

```python
import functools

import jax
import jax.numpy as jnp
from jax import lax
from jax.experimental import pallas as pl
from jax.experimental.pallas import tpu as pltpu
from jax.sharding import PartitionSpec as P

HD = 192
PJ = 128
MESH = pl.DeviceIdType.MESH
F32 = jnp.float32
BF16 = jnp.bfloat16


def dot_nn(a, b):
    return lax.dot_general(a, b, (((1,), (0,)), ((), ())), preferred_element_type=F32)


def dot_nt(a, b):
    return lax.dot_general(a, b, (((1,), (1,)), ((), ())), preferred_element_type=F32)


def dot_tn(a, b):
    return lax.dot_general(a, b, (((0,), (0,)), ((), ())), preferred_element_type=F32)


def fused_kernel(
    n_head,
    n_copies,
    hid_hbm,
    ctx_hbm,
    wq_hbm,
    wk_hbm,
    wv_hbm,
    wj_hbm,
    donor,
    accept,
    counts,
    pred,
    q_hbm,
    k_hbm,
    v_hbm,
    in_hbm,
    hidbuf,
    ctx,
    wq,
    wk,
    wv,
    wj,
    out_in,
    out_q,
    out_k,
    out_v,
    kbuf,
    vbuf,
    fbuf,
    slotbuf,
    qbuf,
    q_t,
    ctx_t,
    sref,
    dpref,
    pb,
    dsb,
    term,
    from_sib,
    pair_sum,
    from_xn,
    own_term,
    grads,
    grads_t,
    gcat,
    dwp,
    rsum,
    zsend,
    zrecv,
    zown,
    send_sems,
    recv_sems,
    load_sems,
    store_sems,
):
    toks = ctx.shape[0]
    width = hidbuf.shape[1]
    feats = wq.shape[0]
    heads = feats // HD
    half = width // 2
    row_y = feats // 2
    row_c = feats // 4
    row_x = feats // 8
    scale = HD**-0.5
    iv = lax.axis_index("interval")
    sq = lax.axis_index("seq")
    hd = lax.axis_index("head")
    xi = lax.div(sq, 2)
    core = lax.rem(sq, 2)
    s_sib = sq + 1 - 2 * core
    s_xn = lax.rem(sq + 2, 4)
    s_dg = lax.rem(s_sib + 2, 4)
    sib = (iv, s_sib, hd)
    xn = (iv, s_xn, hd)
    yn = (1 - iv, sq, hd)
    ysib = (1 - iv, s_sib, hd)
    zpeers = [(iv, sq, lax.rem(hd + d, n_head)) for d in range(1, n_head)]
    zpair = (iv, sq, hd + 1 - 2 * lax.rem(hd, 2))
    split = toks // 2
    mine_z = lax.rem(hd, 2) * split
    hid = hidbuf.at[0:toks]

    def z_rows(base):
        return pl.ds(pl.multiple_of(base + mine_z, 16), split)


    loads = []
    for i, (src, dst) in enumerate(
        (
            (hid_hbm.at[0], hid),
            (wk_hbm, wk),
            (wv_hbm, wv),
            (wq_hbm, wq),
            (wj_hbm, wj),
            (ctx_hbm.at[0], ctx),
        )
    ):
        load = pltpu.make_async_copy(src, dst, load_sems.at[i])
        load.start()
        loads.append(load)

    counter = [0]
    started = []

    def send(src, dst, dev):
        i = counter[0]
        counter[0] += 1
        copy = pltpu.make_async_remote_copy(
            src_ref=src,
            dst_ref=dst,
            send_sem=send_sems.at[i],
            recv_sem=recv_sems.at[i],
            device_id=dev,
            device_id_type=MESH,
        )
        copy.start()
        started.append(copy)
        return copy

    stores = []

    def store(src, dst):
        copy = pltpu.make_async_copy(src, dst, store_sems.at[len(stores)])
        copy.start()
        stores.append(copy)

    barrier = pltpu.get_barrier_semaphore()
    peers = [sib, xn, yn, ysib] + zpeers
    for dev in peers:
        pl.semaphore_signal(barrier, inc=1, device_id=dev, device_id_type=MESH)

    loads[0].wait()
    loads[1].wait()
    kbuf[0] = dot_nt(hid[...], wk[...]).astype(BF16)
    pl.semaphore_wait(barrier, len(peers))
    k_xn = send(kbuf.at[0], kbuf.at[2], xn)
    k_sib = send(kbuf.at[0], kbuf.at[1], sib)
    hid_yn = []
    for p in range(2):
        lanes = slice(p * half, (p + 1) * half)
        hid_yn.append(
            send(hidbuf.at[z_rows(0), lanes], hidbuf.at[z_rows(2 * toks), lanes], yn)
        )
    loads[2].wait()
    vbuf[0] = dot_nt(hid[...], wv[...]).astype(BF16)
    v_xn = send(vbuf.at[0], vbuf.at[2], xn)
    v_sib = send(vbuf.at[0], vbuf.at[1], sib)
    loads[3].wait()
    q_full = dot_nt(hid[...], wq[...])
    qbuf[...] = q_full.astype(BF16)
    q_t[...] = jnp.transpose(q_full).astype(BF16)
    loads[4].wait()
    fbuf[0] = dot_nn(hid[...], wj[...]).astype(BF16)
    f_xn = send(fbuf.at[0, z_rows(0)], fbuf.at[2, z_rows(0)], xn)
    f_sib = send(fbuf.at[0], fbuf.at[1], sib)

    n_acc, slot_dev = donor.shape[2], donor.shape[3]
    n_slots = slotbuf.shape[2]
    acc_iota = lax.broadcasted_iota(jnp.int32, (n_acc, slot_dev), 0)
    slot_ids = lax.broadcasted_iota(jnp.int32, (n_acc, slot_dev), 1) + hd * slot_dev
    live_count = jnp.zeros((n_acc, slot_dev), jnp.int32)
    for j in range(n_acc):
        live_count = jnp.where(acc_iota == j, counts[0, :, j : j + 1], live_count)
    donor_tok = (donor[0, 0] + sq * toks).astype(F32)
    accept_tok = (accept[0, 0] + acc_iota * toks).astype(F32)
    pred_live = jnp.where(slot_ids < live_count, pred[0, 0], 0.0)
    lane_iota = lax.broadcasted_iota(jnp.int32, (n_acc, n_slots), 1)
    row_iota = lax.broadcasted_iota(jnp.int32, (n_acc, n_slots), 0)
    place = lane_iota - (sq * n_acc + row_iota) * slot_dev
    slotbuf[0] = jnp.zeros(slotbuf.shape[1:], F32)
    for i, values in enumerate((donor_tok, accept_tok, pred_live)):
        spread = jnp.zeros((n_acc, n_slots), F32)
        for j in range(slot_dev):
            spread = jnp.where(place == j, values[:, j : j + 1], spread)
        slotbuf[0, i : i + 1, :] = jnp.sum(spread, axis=0, keepdims=True)
    t_xn = send(slotbuf.at[0], slotbuf.at[2], xn)
    t_sib = send(slotbuf.at[0], slotbuf.at[1], sib)
    hid_sib = send(hidbuf.at[0:toks], hidbuf.at[toks : 2 * toks], sib)

    def head_cols(h):
        return slice(h * HD, (h + 1) * HD)

    def block_cols(r):
        return slice(r * toks, (r + 1) * toks)

    def scores(r):
        for h in range(heads):
            sref[h, :, block_cols(r)] = dot_nt(qbuf[:, head_cols(h)], kbuf[r, :, head_cols(h)])

    def dprobs(r):
        for h in range(heads):
            dpref[h, :, block_cols(r)] = dot_nt(ctx[:, head_cols(h)], vbuf[r, :, head_cols(h)])

    scores(0)
    loads[5].wait()
    ctx_t[...] = jnp.transpose(ctx[...].astype(F32)).astype(BF16)
    dprobs(0)
    k_sib.wait_recv()
    scores(1)
    k_xn.wait_recv()
    k_fw = send(kbuf.at[2], kbuf.at[3], sib)
    scores(2)
    k_fw.wait_recv()
    scores(3)

    rows_step = 32

    for h in range(heads):

        @pl.loop(0, toks // rows_step)
        def _(i, h=h):
            rows = pl.ds(pl.multiple_of(i * rows_step, rows_step), rows_step)
            raw = sref[h, rows, :] * scale
            e = jnp.exp(raw - jnp.max(raw, axis=-1, keepdims=True))
            p = e / jnp.sum(e, axis=-1, keepdims=True)
            sref[h, rows, :] = p
            pb[h, rows, :] = p.astype(BF16)

    def kv_terms(which, left_t, right, factor):
        def one(h, r):
            part = dot_nn(left_t[head_cols(h), :], right[h, :, block_cols(r)])
            return part * factor if factor != 1.0 else part

        for h in range(heads):
            term[which, 0, head_cols(h), :] = one(h, 3).astype(BF16)
        a = send(term.at[which, 0], from_sib.at[which, 0], sib)
        for h in range(heads):
            term[which, 1, head_cols(h), :] = one(h, 1).astype(BF16)
        b = send(term.at[which, 1], from_sib.at[which, 1], sib)
        for h in range(heads):
            own_term[which, head_cols(h), :] = one(h, 2)
        a.wait_recv()
        pair_sum[which] = (own_term[which] + from_sib[which, 0].astype(F32)).astype(BF16)
        c = send(pair_sum.at[which], from_xn.at[which], xn)
        for h in range(heads):
            own_term[which, head_cols(h), :] = one(h, 0)
        return b, c

    def g_rows(y, c):
        return pl.ds(pl.multiple_of(y * row_y + c * row_c, 16), row_c)

    g_copy = [None] * 3

    def exchange(slot):
        gcat[slot, :, 0:toks] = grads_t[slot, g_rows(iv, core), :]
        copies = []
        for b, dev, y, c in ((2, yn, 1 - iv, core), (3, ysib, 1 - iv, 1 - core), (1, sib, iv, 1 - core)):
            copies.append(
                send(grads_t.at[slot, g_rows(y, c)], gcat.at[slot, :, block_cols(b)], dev)
            )
        g_copy[slot] = copies

    def kv_final(which, slot, b, c):
        b.wait_recv()
        c.wait_recv()
        total = own_term[which] + from_sib[which, 1].astype(F32) + from_xn[which].astype(F32)
        grads_t[slot] = total.astype(BF16)
        exchange(slot)
        grads[slot] = jnp.transpose(total).astype(BF16)

    def pass_on(arrived, ref):
        arrived.wait_recv()
        return send(ref, ref, zpair)

    def hid_lanes(p):
        return slice(p * half, (p + 1) * half)

    hid_z = [pass_on(hid_yn[0], hidbuf.at[z_rows(2 * toks), hid_lanes(0)])]
    v_pend = kv_terms(1, ctx_t, pb, 1.0)
    v_sib.wait_recv()
    dprobs(1)
    v_xn.wait_recv()
    v_fw = send(vbuf.at[2], vbuf.at[3], sib)
    hid_z.append(pass_on(hid_yn[1], hidbuf.at[z_rows(2 * toks), hid_lanes(1)]))
    f_z = pass_on(f_xn, fbuf.at[2, z_rows(0)])
    t_xn.wait_recv()
    t_fw = send(slotbuf.at[2], slotbuf.at[3], sib)
    dprobs(2)
    v_fw.wait_recv()
    dprobs(3)

    for h in range(heads):

        @pl.loop(0, toks // rows_step)
        def _(i, h=h):
            rows = pl.ds(pl.multiple_of(i * rows_step, rows_step), rows_step)
            p = sref[h, rows, :]
            dp = dpref[h, rows, :]
            delta = jnp.sum(p * dp, axis=-1, keepdims=True)
            dsb[h, rows, :] = (p * (dp - delta)).astype(BF16)

    k_pend = kv_terms(0, q_t, dsb, scale)

    q_parts = []
    for h in range(heads):
        acc = dot_nn(dsb[h, :, block_cols(0)], kbuf[0, :, head_cols(h)])
        for r in range(1, 4):
            acc = acc + dot_nn(dsb[h, :, block_cols(r)], kbuf[r, :, head_cols(h)])
        q_parts.append(acc * scale)
    q_grad = jnp.concatenate(q_parts, axis=-1)
    grads_t[0] = jnp.transpose(q_grad).astype(BF16)
    exchange(0)
    grads[0] = q_grad.astype(BF16)

    f_z.wait_recv()
    f_fw = send(fbuf.at[2], fbuf.at[3], sib)
    hid_fw = []
    for p in range(2):
        lanes = hid_lanes(p)
        hid_z[p].wait_recv()
        hid_fw.append(
            send(hidbuf.at[2 * toks : 3 * toks, lanes], hidbuf.at[3 * toks : 4 * toks, lanes], sib)
        )

    outs = (out_q, out_k, out_v)
    outs_hbm = (q_hbm, k_hbm, v_hbm)
    rs_copy = {}
    piece_copy = {}
    fwd_copy = {}
    sib_copy = {0: [], 1: [], 2: []}

    def x_rows(x):
        return pl.ds(pl.multiple_of(x * row_x, 16), row_x)

    def piece(w, p, y, x):
        start = pl.multiple_of(y * row_y + core * row_c + x * row_x, 16)
        return outs[w].at[pl.ds(start, row_x), slice(p * half, (p + 1) * half)]

    def to_sib(w, ref):
        sib_copy[w].append(send(ref, ref, sib))

    def dw_start(w):
        for copy in g_copy[w]:
            copy.wait_recv()
        for p in range(2):
            dwp[w, p] = dot_nn(gcat[w], hidbuf[:, p * half : (p + 1) * half]).astype(BF16)
            rs_copy[w, p] = send(dwp.at[w, p, x_rows(1 - xi)], rsum.at[w, p], xn)

    def dw_final(w):
        for p in range(2):
            rs_copy[w, p].wait_recv()
            done = dwp[w, p, x_rows(xi), :].astype(F32) + rsum[w, p].astype(F32)
            ref = piece(w, p, iv, xi)
            ref[...] = done.astype(BF16)
            cx = send(ref, ref, xn)
            cy = send(ref, ref, yn)
            piece_copy[w, p] = (cx, cy)
            to_sib(w, ref)

    def dw_forward(w):
        for p in range(2):
            cx = piece_copy[w, p][0]
            cx_ref = piece(w, p, iv, 1 - xi)
            cx.wait_recv()
            fwd_copy[w, p] = send(cx_ref, cx_ref, yn)
            to_sib(w, cx_ref)
        for p in range(2):
            piece_copy[w, p][1].wait_recv()
            to_sib(w, piece(w, p, 1 - iv, xi))

    def dw_last(w):
        for p in range(2):
            fwd_copy[w, p].wait_recv()
            to_sib(w, piece(w, p, 1 - iv, 1 - xi))

    def dw_out(w):
        for copy in sib_copy[w]:
            copy.wait_recv()
        store(outs[w], outs_hbm[w])

    kv_final(1, 2, *v_pend)
    hid_sib.wait_recv()
    hid_fw[0].wait_recv()
    hid_fw[1].wait_recv()
    dw_start(0)
    dw_start(2)

    f_sib.wait_recv()
    t_sib.wait_recv()
    f_fw.wait_recv()
    t_fw.wait_recv()
    rows_all = slotbuf[0] + slotbuf[1] + slotbuf[2] + slotbuf[3]
    donor_row = rows_all[0:1, :]
    accept_row = rows_all[1:2, :]
    pred_row = rows_all[2:3, :]
    tok_iota = lax.broadcasted_iota(jnp.int32, (toks, n_slots), 0)
    own_donor = None
    own_accept = None
    donor_t = jnp.zeros((PJ, n_slots), F32)
    accept_t = jnp.zeros((PJ, n_slots), F32)
    for r, shard in enumerate((sq, s_sib, s_xn, s_dg)):
        tok = (tok_iota + shard * toks).astype(F32)
        hot_d = jnp.where(tok == donor_row, 1.0, 0.0).astype(BF16)
        hot_a = jnp.where(tok == accept_row, 1.0, 0.0).astype(BF16)
        if r == 0:
            own_donor, own_accept = hot_d, hot_a
        donor_t = donor_t + dot_tn(fbuf[r], hot_d)
        accept_t = accept_t + dot_tn(fbuf[r], hot_a)
    pair_scale = PJ**-0.5
    pair = jnp.sum(donor_t * accept_t, axis=0, keepdims=True) * pair_scale
    slot_grad = pred_row * (1.0 / (1.0 + jnp.exp(-pair))) * pair_scale
    grad_feat = dot_nt(own_donor, (slot_grad * accept_t).astype(BF16)) + dot_nt(
        own_accept, (slot_grad * donor_t).astype(BF16)
    )
    grad_feat = grad_feat.astype(BF16)

    kv_final(0, 1, *k_pend)
    dw_final(0)
    dw_start(1)

    cols = width // n_head
    z_copy = []

    def input_block(owner):
        lanes = pl.ds(pl.multiple_of(owner * cols, 128), cols)
        acc = dot_nn(grads[0], wq[:, lanes]) + dot_nn(grads[1], wk[:, lanes])
        acc = acc + dot_nn(grads[2], wv[:, lanes])
        return acc + dot_nt(grad_feat, wj[lanes, :])

    for d in range(n_head - 1, 0, -1):
        zsend[d - 1] = input_block(lax.rem(hd + d, n_head)).astype(BF16)
        z_copy.append((d, send(zsend.at[d - 1], zrecv.at[d - 1], zpeers[d - 1])))
        if d == n_head - 1:
            dw_final(2)
    zown[...] = input_block(hd)
    dw_forward(0)
    dw_final(1)
    dw_forward(2)
    dw_last(0)
    dw_forward(1)
    dw_last(2)
    dw_out(0)
    dw_last(1)
    for d, copy in z_copy:
        copy.wait_recv()
    total = zown[...]
    for d in range(n_head - 1):
        total = total + zrecv[d].astype(F32)
    out_in[...] = total.astype(BF16)
    store(out_in, in_hbm)
    dw_out(2)
    dw_out(1)
    for copy in started:
        copy.wait_send()
    for copy in stores:
        copy.wait()
    assert counter[0] <= n_copies


def write_kernel(n, chunks, *refs):
    sources, targets = refs[:n], refs[n : 2 * n]
    staged = refs[2 * n : 3 * n]
    load_sems, store_sems = refs[3 * n :]
    steps = []
    for a in range(n):
        rows = staged[a].shape[0] // chunks
        for c in range(chunks):
            part = pl.ds(c * rows, rows)
            i = len(steps)
            load = pltpu.make_async_copy(sources[a].at[part], staged[a].at[part], load_sems.at[i])
            store = pltpu.make_async_copy(staged[a].at[part], targets[a].at[part], store_sems.at[i])
            load.start()
            steps.append((load, store))
    for load, store in steps:
        load.wait()
        store.start()
    for _, store in steps:
        store.wait()


def fused_device(
    n_head,
    hidden_in,
    ctx_grad,
    w_query,
    w_key,
    w_value,
    w_junction,
    donor_pos,
    acceptor_pos,
    junction_counts,
    pred_grad,
):
    toks, width = hidden_in.shape[1:]
    feats = w_query.shape[0]
    heads = feats // HD
    n_seq = 4
    n_slots = n_seq * donor_pos.shape[2] * donor_pos.shape[3]
    n_copies = 96
    vmem = pl.BlockSpec(memory_space=pltpu.VMEM)
    hbm = pl.BlockSpec(memory_space=pl.ANY)
    half = width // 2
    cols = width // n_head
    scratch = [
        pltpu.VMEM((4 * toks, width), BF16),
        pltpu.VMEM((toks, feats), BF16),
        pltpu.VMEM((feats, width), BF16),
        pltpu.VMEM((feats, width), BF16),
        pltpu.VMEM((feats, width), BF16),
        pltpu.VMEM((width, PJ), BF16),
        pltpu.VMEM((toks, cols), BF16),
        pltpu.VMEM((feats, width), BF16),
        pltpu.VMEM((feats, width), BF16),
        pltpu.VMEM((feats, width), BF16),
        pltpu.VMEM((4, toks, feats), BF16),
        pltpu.VMEM((4, toks, feats), BF16),
        pltpu.VMEM((4, toks, PJ), BF16),
        pltpu.VMEM((4, 8, n_slots), F32),
        pltpu.VMEM((toks, feats), BF16),
        pltpu.VMEM((feats, toks), BF16),
        pltpu.VMEM((feats, toks), BF16),
        pltpu.VMEM((heads, toks, 4 * toks), F32),
        pltpu.VMEM((heads, toks, 4 * toks), F32),
        pltpu.VMEM((heads, toks, 4 * toks), BF16),
        pltpu.VMEM((heads, toks, 4 * toks), BF16),
        pltpu.VMEM((2, 2, feats, toks), BF16),
        pltpu.VMEM((2, 2, feats, toks), BF16),
        pltpu.VMEM((2, feats, toks), BF16),
        pltpu.VMEM((2, feats, toks), BF16),
        pltpu.VMEM((2, feats, toks), F32),
        pltpu.VMEM((3, toks, feats), BF16),
        pltpu.VMEM((3, feats, toks), BF16),
        pltpu.VMEM((3, feats // 4, 4 * toks), BF16),
        pltpu.VMEM((3, 2, feats // 4, half), BF16),
        pltpu.VMEM((3, 2, feats // 8, half), BF16),
        pltpu.VMEM((n_head - 1, toks, cols), BF16),
        pltpu.VMEM((n_head - 1, toks, cols), BF16),
        pltpu.VMEM((toks, cols), F32),
        pltpu.SemaphoreType.DMA((n_copies,)),
        pltpu.SemaphoreType.DMA((n_copies,)),
        pltpu.SemaphoreType.DMA((6,)),
        pltpu.SemaphoreType.DMA((4,)),
    ]
    grad_w = jax.ShapeDtypeStruct((feats, width), BF16)
    shapes = (grad_w, grad_w, grad_w, jax.ShapeDtypeStruct((toks, cols), BF16))
    results = pl.pallas_call(
        functools.partial(fused_kernel, n_head, n_copies),
        out_shape=shapes,
        in_specs=[hbm] * 6 + [vmem] * 4,
        out_specs=(hbm,) * 4,
        scratch_shapes=scratch,
        compiler_params=pltpu.CompilerParams(
            collective_id=0, has_side_effects=True, vmem_limit_bytes=56 * 1024 * 1024
        ),
        name="attention_backward",
    )(
        hidden_in,
        ctx_grad,
        w_query,
        w_key,
        w_value,
        w_junction,
        donor_pos,
        acceptor_pos,
        junction_counts,
        pred_grad,
    )
    chunks = 4
    out_q, out_k, out_v, out_in = pl.pallas_call(
        functools.partial(write_kernel, 4, chunks),
        out_shape=shapes,
        in_specs=[hbm] * 4,
        out_specs=(hbm,) * 4,
        scratch_shapes=[pltpu.VMEM(s.shape, s.dtype) for s in shapes]
        + [pltpu.SemaphoreType.DMA((4 * chunks,)), pltpu.SemaphoreType.DMA((4 * chunks,))],
        compiler_params=pltpu.CompilerParams(vmem_limit_bytes=16 * 1024 * 1024),
        name="write_results",
    )(*results)
    return out_in[None], out_q, out_k, out_v


def on_device(
    hidden_in,
    ctx_grad,
    w_query,
    w_key,
    w_value,
    w_junction,
    donor_pos,
    acceptor_pos,
    junction_counts,
    pred_grad,
):
    hidden = hidden_in[0]
    local_len = hidden.shape[0]
    shard_count = lax.axis_size("seq")
    total_len = local_len * shard_count
    heads_dev = w_query.shape[0] // HD
    softmax_scale = HD ** (-0.5)
    pair_scale = PJ ** (-0.5)
    queries = jnp.einsum("td,cd->tc", hidden, w_query, preferred_element_type=jnp.float32).astype(
        jnp.bfloat16
    )
    key_rows = jnp.einsum("td,cd->tc", hidden, w_key, preferred_element_type=jnp.float32).astype(
        jnp.bfloat16
    )
    value_rows = jnp.einsum(
        "td,cd->tc", hidden, w_value, preferred_element_type=jnp.float32
    ).astype(jnp.bfloat16)
    features = jnp.dot(hidden, w_junction, preferred_element_type=jnp.float32).astype(jnp.bfloat16)
    all_keys, all_values, all_features = (
        lax.all_gather(key_rows, "seq", axis=0, tiled=True),
        lax.all_gather(value_rows, "seq", axis=0, tiled=True),
        lax.all_gather(features, "seq", axis=0, tiled=True),
    )
    query_heads = queries.reshape(local_len, heads_dev, HD)
    grad_heads = ctx_grad[0].reshape(local_len, heads_dev, HD)
    key_heads = all_keys.reshape(total_len, heads_dev, HD)
    value_heads = all_values.reshape(total_len, heads_dev, HD)
    scores = (
        jnp.einsum("qhd,khd->hqk", query_heads, key_heads, preferred_element_type=jnp.float32)
        * softmax_scale
    )
    row_max = jnp.max(scores, axis=-1, keepdims=True)
    expd = jnp.exp(scores - row_max)
    probs = expd / jnp.sum(expd, axis=-1, keepdims=True)
    dprobs = jnp.einsum("qhd,khd->hqk", grad_heads, value_heads, preferred_element_type=jnp.float32)
    row_delta = jnp.sum(probs * dprobs, axis=-1, keepdims=True)
    dscores = probs * (dprobs - row_delta)
    probs_b = probs.astype(jnp.bfloat16)
    dscores_b = dscores.astype(jnp.bfloat16)
    query_grad = (
        (
            jnp.einsum("hqk,khd->qhd", dscores_b, key_heads, preferred_element_type=jnp.float32)
            * softmax_scale
        )
        .astype(jnp.bfloat16)
        .reshape(local_len, heads_dev * HD)
    )
    key_term = (
        jnp.einsum("hqk,qhd->khd", dscores_b, query_heads, preferred_element_type=jnp.float32)
        * softmax_scale
    ).reshape(total_len, heads_dev * HD)
    value_term = jnp.einsum(
        "hqk,qhd->khd", probs_b, grad_heads, preferred_element_type=jnp.float32
    ).reshape(total_len, heads_dev * HD)
    key_sum, value_sum = (
        lax.psum_scatter(
            key_term.astype(jnp.bfloat16), "seq", scatter_dimension=0, tiled=True
        ).astype(jnp.float32),
        lax.psum_scatter(
            value_term.astype(jnp.bfloat16), "seq", scatter_dimension=0, tiled=True
        ).astype(jnp.float32),
    )
    key_grad = key_sum.astype(jnp.bfloat16)
    value_grad = value_sum.astype(jnp.bfloat16)
    donor_idx = donor_pos[0, 0]
    accept_idx = acceptor_pos[0, 0]
    slot_dev = donor_idx.shape[1]
    slot_ids = lax.axis_index("head") * slot_dev + jnp.arange(slot_dev, dtype=jnp.int32)
    live_slots = slot_ids[None, :] < junction_counts[0, 0][:, None]
    donor_feat = features[donor_idx].astype(jnp.float32)
    accept_glob = jnp.arange(shard_count, dtype=jnp.int32)[:, None] * local_len + accept_idx
    accept_rows = all_features[accept_glob]
    accept_feat = accept_rows.astype(jnp.float32)
    pair_score = jnp.sum(donor_feat * accept_feat, axis=-1) * pair_scale
    slot_grad = (
        jnp.where(live_slots, pred_grad[0, 0] * jax.nn.sigmoid(pair_score), 0.0) * pair_scale
    )
    donor_term = slot_grad[..., None] * accept_feat
    accept_term = slot_grad[..., None] * donor_feat
    pair_width = features.shape[1]
    grad_feat = (
        jnp.zeros((local_len, pair_width), jnp.float32)
        .at[donor_idx.reshape(-1)]
        .add(donor_term.reshape(-1, pair_width))
    )
    spread_term = (
        jnp.zeros((total_len, pair_width), jnp.float32)
        .at[accept_glob.reshape(-1)]
        .add(accept_term.reshape(-1, pair_width))
    )
    grad_feat = grad_feat + lax.psum_scatter(
        spread_term.astype(jnp.bfloat16), "seq", scatter_dimension=0, tiled=True
    ).astype(jnp.float32)
    grad_feat_b = grad_feat.astype(jnp.bfloat16)
    input_term = jnp.einsum("tc,cd->td", query_grad, w_query, preferred_element_type=jnp.float32)
    input_term = input_term + jnp.einsum(
        "tc,cd->td", key_grad, w_key, preferred_element_type=jnp.float32
    )
    input_term = input_term + jnp.einsum(
        "tc,cd->td", value_grad, w_value, preferred_element_type=jnp.float32
    )
    input_term = input_term + jnp.einsum(
        "tp,dp->td", grad_feat_b, w_junction, preferred_element_type=jnp.float32
    )
    grad_input = lax.psum_scatter(
        input_term.astype(jnp.bfloat16), "head", scatter_dimension=1, tiled=True
    )
    key_wterm = jnp.einsum("tc,td->cd", key_grad, hidden, preferred_element_type=jnp.float32)
    value_wterm = jnp.einsum("tc,td->cd", value_grad, hidden, preferred_element_type=jnp.float32)
    query_wterm = jnp.einsum("tc,td->cd", query_grad, hidden, preferred_element_type=jnp.float32)
    query_wsum, key_wsum, value_wsum = lax.psum(
        (query_wterm, key_wterm, value_wterm), ("interval", "seq")
    )
    return (
        grad_input[None],
        query_wsum.astype(jnp.bfloat16),
        key_wsum.astype(jnp.bfloat16),
        value_wsum.astype(jnp.bfloat16),
    )


def solution(mesh):
    placed = (
        P("interval", "seq", None),
        P("interval", "seq", "head"),
        P("head", None),
        P("head", None),
        P("head", None),
        P(),
        P("interval", "seq", None, "head"),
        P("interval", "seq", None, "head"),
        P("interval", "seq", None),
        P("interval", "seq", None, "head"),
    )
    shape = dict(mesh.shape)
    fits = shape["interval"] == 2 and shape["seq"] == 4 and shape["head"] == 4
    run = functools.partial(fused_device, shape["head"]) if fits else on_device
    return jax.shard_map(
        run,
        mesh=mesh,
        in_specs=placed,
        out_specs=(P("interval", "seq", "head"), P("head", None), P("head", None), P("head", None)),
        check_vma=False,
    )
```

```python
import functools

import jax
import jax.numpy as jnp
from jax import lax
from jax.experimental import pallas as pl
from jax.experimental.pallas import tpu as pltpu
from jax.sharding import PartitionSpec as P

HD = 192
PJ = 128
MESH = pl.DeviceIdType.MESH
F32 = jnp.float32
BF16 = jnp.bfloat16


def dot_nn(a, b):
    return lax.dot_general(a, b, (((1,), (0,)), ((), ())), preferred_element_type=F32)


def dot_nt(a, b):
    return lax.dot_general(a, b, (((1,), (1,)), ((), ())), preferred_element_type=F32)


def dot_tn(a, b):
    return lax.dot_general(a, b, (((0,), (0,)), ((), ())), preferred_element_type=F32)


def fused_kernel(
    n_head,
    n_copies,
    hid_hbm,
    ctx_hbm,
    wq_hbm,
    wk_hbm,
    wv_hbm,
    wj_hbm,
    donor,
    accept,
    counts,
    pred,
    q_hbm,
    k_hbm,
    v_hbm,
    in_hbm,
    hidbuf,
    ctx,
    wq,
    wk,
    wv,
    wj,
    out_in,
    out_q,
    out_k,
    out_v,
    kbuf,
    vbuf,
    fbuf,
    slotbuf,
    qbuf,
    ctx_h,
    q_t,
    ctx_t,
    sref,
    dpref,
    pb,
    dsb,
    term,
    from_sib,
    pair_sum,
    from_xn,
    own_term,
    grads,
    grads_t,
    gcat,
    dwp,
    rsum,
    zsend,
    zrecv,
    zown,
    send_sems,
    recv_sems,
    load_sems,
    store_sems,
):
    toks = ctx.shape[0]
    width = hidbuf.shape[1]
    feats = wq.shape[0]
    heads = feats // HD
    half = width // 2
    row_y = feats // 2
    row_c = feats // 4
    row_x = feats // 8
    scale = HD**-0.5
    iv = lax.axis_index("interval")
    sq = lax.axis_index("seq")
    hd = lax.axis_index("head")
    xi = lax.div(sq, 2)
    core = lax.rem(sq, 2)
    s_sib = sq + 1 - 2 * core
    s_xn = lax.rem(sq + 2, 4)
    s_dg = lax.rem(s_sib + 2, 4)
    sib = (iv, s_sib, hd)
    xn = (iv, s_xn, hd)
    yn = (1 - iv, sq, hd)
    ysib = (1 - iv, s_sib, hd)
    zpeers = [(iv, sq, lax.rem(hd + d, n_head)) for d in range(1, n_head)]
    zpair = (iv, sq, hd + 1 - 2 * lax.rem(hd, 2))
    split = toks // 2
    mine_z = lax.rem(hd, 2) * split
    hid = hidbuf.at[0:toks]

    def z_rows(base):
        return pl.ds(pl.multiple_of(base + mine_z, 16), split)


    loads = []
    for i, (src, dst) in enumerate(
        (
            (hid_hbm.at[0], hid),
            (wk_hbm, wk),
            (wv_hbm, wv),
            (wq_hbm, wq),
            (wj_hbm, wj),
            (ctx_hbm.at[0], ctx),
        )
    ):
        load = pltpu.make_async_copy(src, dst, load_sems.at[i])
        load.start()
        loads.append(load)

    counter = [0]
    started = []

    def send(src, dst, dev):
        i = counter[0]
        counter[0] += 1
        copy = pltpu.make_async_remote_copy(
            src_ref=src,
            dst_ref=dst,
            send_sem=send_sems.at[i],
            recv_sem=recv_sems.at[i],
            device_id=dev,
            device_id_type=MESH,
        )
        copy.start()
        started.append(copy)
        return copy

    stores = []

    def store(src, dst):
        copy = pltpu.make_async_copy(src, dst, store_sems.at[len(stores)])
        copy.start()
        stores.append(copy)

    barrier = pltpu.get_barrier_semaphore()
    peers = [sib, xn, yn, ysib] + zpeers
    for dev in peers:
        pl.semaphore_signal(barrier, inc=1, device_id=dev, device_id_type=MESH)

    loads[0].wait()
    loads[1].wait()
    kbuf[0] = dot_nt(hid[...], wk[...]).astype(BF16)
    pl.semaphore_wait(barrier, len(peers))
    k_xn = send(kbuf.at[0], kbuf.at[2], xn)
    k_sib = send(kbuf.at[0], kbuf.at[1], sib)
    hid_yn = []
    for p in range(2):
        lanes = slice(p * half, (p + 1) * half)
        hid_yn.append(
            send(hidbuf.at[z_rows(0), lanes], hidbuf.at[z_rows(2 * toks), lanes], yn)
        )
    loads[2].wait()
    vbuf[0] = dot_nt(hid[...], wv[...]).astype(BF16)
    v_xn = send(vbuf.at[0], vbuf.at[2], xn)
    v_sib = send(vbuf.at[0], vbuf.at[1], sib)
    loads[3].wait()
    q_full = dot_nt(hid[...], wq[...])
    for h in range(heads):
        qbuf[h] = q_full[:, h * HD : (h + 1) * HD].astype(BF16)
    q_t[...] = jnp.transpose(q_full).astype(BF16)
    loads[4].wait()
    fbuf[0] = dot_nn(hid[...], wj[...]).astype(BF16)
    f_xn = send(fbuf.at[0, z_rows(0)], fbuf.at[2, z_rows(0)], xn)
    f_sib = send(fbuf.at[0], fbuf.at[1], sib)

    n_acc, slot_dev = donor.shape[2], donor.shape[3]
    n_slots = slotbuf.shape[2]
    acc_iota = lax.broadcasted_iota(jnp.int32, (n_acc, slot_dev), 0)
    slot_ids = lax.broadcasted_iota(jnp.int32, (n_acc, slot_dev), 1) + hd * slot_dev
    live_count = jnp.zeros((n_acc, slot_dev), jnp.int32)
    for j in range(n_acc):
        live_count = jnp.where(acc_iota == j, counts[0, :, j : j + 1], live_count)
    donor_tok = (donor[0, 0] + sq * toks).astype(F32)
    accept_tok = (accept[0, 0] + acc_iota * toks).astype(F32)
    pred_live = jnp.where(slot_ids < live_count, pred[0, 0], 0.0)
    lane_iota = lax.broadcasted_iota(jnp.int32, (n_acc, n_slots), 1)
    row_iota = lax.broadcasted_iota(jnp.int32, (n_acc, n_slots), 0)
    place = lane_iota - (sq * n_acc + row_iota) * slot_dev
    slotbuf[0] = jnp.zeros(slotbuf.shape[1:], F32)
    for i, values in enumerate((donor_tok, accept_tok, pred_live)):
        spread = jnp.zeros((n_acc, n_slots), F32)
        for j in range(slot_dev):
            spread = jnp.where(place == j, values[:, j : j + 1], spread)
        slotbuf[0, i : i + 1, :] = jnp.sum(spread, axis=0, keepdims=True)
    t_xn = send(slotbuf.at[0], slotbuf.at[2], xn)
    t_sib = send(slotbuf.at[0], slotbuf.at[1], sib)
    hid_sib = send(hidbuf.at[0:toks], hidbuf.at[toks : 2 * toks], sib)

    def head_cols(h):
        return slice(h * HD, (h + 1) * HD)

    def block_cols(r):
        return slice(r * toks, (r + 1) * toks)

    def scores(r):
        for h in range(heads):
            sref[h, :, block_cols(r)] = dot_nt(qbuf[h], kbuf[r, :, head_cols(h)])

    def dprobs(r):
        for h in range(heads):
            dpref[h, :, block_cols(r)] = dot_nt(ctx_h[h], vbuf[r, :, head_cols(h)])

    scores(0)
    loads[5].wait()
    ctx_t[...] = jnp.transpose(ctx[...].astype(F32)).astype(BF16)
    for h in range(heads):
        ctx_h[h] = ctx[:, head_cols(h)]
    dprobs(0)
    k_sib.wait_recv()
    scores(1)
    k_xn.wait_recv()
    k_fw = send(kbuf.at[2], kbuf.at[3], sib)
    scores(2)
    k_fw.wait_recv()
    scores(3)

    rows_step = 16

    @pl.loop(0, toks // rows_step)
    def _(i):
        rows = pl.ds(pl.multiple_of(i * rows_step, rows_step), rows_step)
        raws = [sref[h, rows, :] * scale for h in range(heads)]
        tops = [jnp.max(raw, axis=-1, keepdims=True) for raw in raws]
        es = [jnp.exp(raw - top) for raw, top in zip(raws, tops)]
        sums = [jnp.sum(e, axis=-1, keepdims=True) for e in es]
        ps = [e * (1.0 / total) for e, total in zip(es, sums)]
        for h in range(heads):
            sref[h, rows, :] = ps[h]
            pb[h, rows, :] = ps[h].astype(BF16)

    def kv_terms(which, left_t, right, factor):
        def one(h, r):
            part = dot_nn(left_t[head_cols(h), :], right[h, :, block_cols(r)])
            return part * factor if factor != 1.0 else part

        for h in range(heads):
            term[which, 0, head_cols(h), :] = one(h, 3).astype(BF16)
        a = send(term.at[which, 0], from_sib.at[which, 0], sib)
        for h in range(heads):
            term[which, 1, head_cols(h), :] = one(h, 1).astype(BF16)
        b = send(term.at[which, 1], from_sib.at[which, 1], sib)
        for h in range(heads):
            own_term[which, head_cols(h), :] = one(h, 2)
        a.wait_recv()
        pair_sum[which] = (own_term[which] + from_sib[which, 0].astype(F32)).astype(BF16)
        c = send(pair_sum.at[which], from_xn.at[which], xn)
        for h in range(heads):
            own_term[which, head_cols(h), :] = one(h, 0)
        return b, c

    def g_rows(y, c):
        return pl.ds(pl.multiple_of(y * row_y + c * row_c, 16), row_c)

    g_copy = [None] * 3

    def exchange(slot):
        gcat[slot, :, 0:toks] = grads_t[slot, g_rows(iv, core), :]
        copies = []
        for b, dev, y, c in ((2, yn, 1 - iv, core), (3, ysib, 1 - iv, 1 - core), (1, sib, iv, 1 - core)):
            copies.append(
                send(grads_t.at[slot, g_rows(y, c)], gcat.at[slot, :, block_cols(b)], dev)
            )
        g_copy[slot] = copies

    def kv_final(which, slot, b, c):
        b.wait_recv()
        c.wait_recv()
        total = own_term[which] + from_sib[which, 1].astype(F32) + from_xn[which].astype(F32)
        grads_t[slot] = total.astype(BF16)
        exchange(slot)
        grads[slot] = jnp.transpose(total).astype(BF16)

    def pass_on(arrived, ref):
        arrived.wait_recv()
        return send(ref, ref, zpair)

    def hid_lanes(p):
        return slice(p * half, (p + 1) * half)

    hid_z = [pass_on(hid_yn[0], hidbuf.at[z_rows(2 * toks), hid_lanes(0)])]
    v_pend = kv_terms(1, ctx_t, pb, 1.0)
    v_sib.wait_recv()
    dprobs(1)
    v_xn.wait_recv()
    v_fw = send(vbuf.at[2], vbuf.at[3], sib)
    hid_z.append(pass_on(hid_yn[1], hidbuf.at[z_rows(2 * toks), hid_lanes(1)]))
    f_z = pass_on(f_xn, fbuf.at[2, z_rows(0)])
    t_xn.wait_recv()
    t_fw = send(slotbuf.at[2], slotbuf.at[3], sib)
    dprobs(2)
    v_fw.wait_recv()
    dprobs(3)

    @pl.loop(0, toks // rows_step)
    def _(i):
        rows = pl.ds(pl.multiple_of(i * rows_step, rows_step), rows_step)
        ps = [sref[h, rows, :] for h in range(heads)]
        dps = [dpref[h, rows, :] for h in range(heads)]
        deltas = [jnp.sum(p * dp, axis=-1, keepdims=True) for p, dp in zip(ps, dps)]
        for h in range(heads):
            dsb[h, rows, :] = (ps[h] * (dps[h] - deltas[h])).astype(BF16)

    k_pend = kv_terms(0, q_t, dsb, scale)

    q_parts = []
    for h in range(heads):
        acc = dot_nn(dsb[h, :, block_cols(0)], kbuf[0, :, head_cols(h)])
        for r in range(1, 4):
            acc = acc + dot_nn(dsb[h, :, block_cols(r)], kbuf[r, :, head_cols(h)])
        q_parts.append(acc * scale)
    q_grad = jnp.concatenate(q_parts, axis=-1)
    grads_t[0] = jnp.transpose(q_grad).astype(BF16)
    exchange(0)
    grads[0] = q_grad.astype(BF16)

    f_z.wait_recv()
    f_fw = send(fbuf.at[2], fbuf.at[3], sib)
    hid_fw = []
    for p in range(2):
        lanes = hid_lanes(p)
        hid_z[p].wait_recv()
        hid_fw.append(
            send(hidbuf.at[2 * toks : 3 * toks, lanes], hidbuf.at[3 * toks : 4 * toks, lanes], sib)
        )

    outs = (out_q, out_k, out_v)
    outs_hbm = (q_hbm, k_hbm, v_hbm)
    rs_copy = {}
    piece_copy = {}
    fwd_copy = {}
    sib_copy = {0: [], 1: [], 2: []}

    def x_rows(x):
        return pl.ds(pl.multiple_of(x * row_x, 16), row_x)

    def piece(w, p, y, x):
        start = pl.multiple_of(y * row_y + core * row_c + x * row_x, 16)
        return outs[w].at[pl.ds(start, row_x), slice(p * half, (p + 1) * half)]

    def to_sib(w, ref):
        sib_copy[w].append(send(ref, ref, sib))

    def dw_start(w):
        for copy in g_copy[w]:
            copy.wait_recv()
        for p in range(2):
            dwp[w, p] = dot_nn(gcat[w], hidbuf[:, p * half : (p + 1) * half]).astype(BF16)
            rs_copy[w, p] = send(dwp.at[w, p, x_rows(1 - xi)], rsum.at[w, p], xn)

    def dw_final(w):
        for p in range(2):
            rs_copy[w, p].wait_recv()
            done = dwp[w, p, x_rows(xi), :].astype(F32) + rsum[w, p].astype(F32)
            ref = piece(w, p, iv, xi)
            ref[...] = done.astype(BF16)
            cx = send(ref, ref, xn)
            cy = send(ref, ref, yn)
            piece_copy[w, p] = (cx, cy)
            to_sib(w, ref)

    def dw_forward(w):
        for p in range(2):
            cx = piece_copy[w, p][0]
            cx_ref = piece(w, p, iv, 1 - xi)
            cx.wait_recv()
            fwd_copy[w, p] = send(cx_ref, cx_ref, yn)
            to_sib(w, cx_ref)
        for p in range(2):
            piece_copy[w, p][1].wait_recv()
            to_sib(w, piece(w, p, 1 - iv, xi))

    def dw_last(w):
        for p in range(2):
            fwd_copy[w, p].wait_recv()
            to_sib(w, piece(w, p, 1 - iv, 1 - xi))

    def dw_out(w):
        for copy in sib_copy[w]:
            copy.wait_recv()
        store(outs[w], outs_hbm[w])

    kv_final(1, 2, *v_pend)
    hid_sib.wait_recv()
    hid_fw[0].wait_recv()
    hid_fw[1].wait_recv()
    dw_start(0)
    dw_start(2)

    f_sib.wait_recv()
    t_sib.wait_recv()
    f_fw.wait_recv()
    t_fw.wait_recv()
    rows_all = slotbuf[0] + slotbuf[1] + slotbuf[2] + slotbuf[3]
    donor_row = rows_all[0:1, :]
    accept_row = rows_all[1:2, :]
    pred_row = rows_all[2:3, :]
    tok_iota = lax.broadcasted_iota(jnp.int32, (toks, n_slots), 0)
    own_donor = None
    own_accept = None
    donor_t = jnp.zeros((PJ, n_slots), F32)
    accept_t = jnp.zeros((PJ, n_slots), F32)
    for r, shard in enumerate((sq, s_sib, s_xn, s_dg)):
        tok = (tok_iota + shard * toks).astype(F32)
        hot_d = jnp.where(tok == donor_row, 1.0, 0.0).astype(BF16)
        hot_a = jnp.where(tok == accept_row, 1.0, 0.0).astype(BF16)
        if r == 0:
            own_donor, own_accept = hot_d, hot_a
        donor_t = donor_t + dot_tn(fbuf[r], hot_d)
        accept_t = accept_t + dot_tn(fbuf[r], hot_a)
    pair_scale = PJ**-0.5
    pair = jnp.sum(donor_t * accept_t, axis=0, keepdims=True) * pair_scale
    slot_grad = pred_row * (1.0 / (1.0 + jnp.exp(-pair))) * pair_scale
    grad_feat = dot_nt(own_donor, (slot_grad * accept_t).astype(BF16)) + dot_nt(
        own_accept, (slot_grad * donor_t).astype(BF16)
    )
    grad_feat = grad_feat.astype(BF16)

    cols = width // n_head

    def owner_lanes(d):
        owner = lax.rem(hd + d, n_head) if d > 0 else hd
        return pl.ds(pl.multiple_of(owner * cols, 128), cols)

    for d in range(n_head):
        lanes = owner_lanes(d)
        acc = dot_nn(grads[0], wq[:, lanes]) + dot_nn(grads[2], wv[:, lanes])
        zown[d] = acc + dot_nt(grad_feat, wj[lanes, :])

    kv_final(0, 1, *k_pend)
    z_copy = []
    far_first = [2, 1, 3] if n_head == 4 else list(range(n_head - 1, 0, -1))
    for d in far_first:
        block = zown[d] + dot_nn(grads[1], wk[:, owner_lanes(d)])
        zsend[d - 1] = block.astype(BF16)
        z_copy.append((d, send(zsend.at[d - 1], zrecv.at[d - 1], zpeers[d - 1])))
    dw_start(1)
    dw_final(0)
    zown[0] = zown[0] + dot_nn(grads[1], wk[:, owner_lanes(0)])
    dw_final(2)
    dw_forward(0)
    dw_final(1)
    dw_forward(2)
    dw_last(0)
    dw_forward(1)
    dw_last(2)
    dw_out(0)
    dw_last(1)
    for d, copy in z_copy:
        copy.wait_recv()
    total = zown[0]
    for d in range(n_head - 1):
        total = total + zrecv[d].astype(F32)
    out_in[...] = total.astype(BF16)
    store(out_in, in_hbm)
    dw_out(2)
    dw_out(1)
    for copy in started:
        copy.wait_send()
    for copy in stores:
        copy.wait()
    assert counter[0] <= n_copies


def write_kernel(n, chunks, *refs):
    sources, targets = refs[:n], refs[n : 2 * n]
    staged = refs[2 * n : 3 * n]
    load_sems, store_sems = refs[3 * n :]
    steps = []
    for a in range(n):
        rows = staged[a].shape[0] // chunks
        for c in range(chunks):
            part = pl.ds(c * rows, rows)
            i = len(steps)
            load = pltpu.make_async_copy(sources[a].at[part], staged[a].at[part], load_sems.at[i])
            store = pltpu.make_async_copy(staged[a].at[part], targets[a].at[part], store_sems.at[i])
            load.start()
            steps.append((load, store))
    for load, store in steps:
        load.wait()
        store.start()
    for _, store in steps:
        store.wait()


def fused_device(
    n_head,
    hidden_in,
    ctx_grad,
    w_query,
    w_key,
    w_value,
    w_junction,
    donor_pos,
    acceptor_pos,
    junction_counts,
    pred_grad,
):
    toks, width = hidden_in.shape[1:]
    feats = w_query.shape[0]
    heads = feats // HD
    n_seq = 4
    n_slots = n_seq * donor_pos.shape[2] * donor_pos.shape[3]
    n_copies = 96
    vmem = pl.BlockSpec(memory_space=pltpu.VMEM)
    hbm = pl.BlockSpec(memory_space=pl.ANY)
    half = width // 2
    cols = width // n_head
    scratch = [
        pltpu.VMEM((4 * toks, width), BF16),
        pltpu.VMEM((toks, feats), BF16),
        pltpu.VMEM((feats, width), BF16),
        pltpu.VMEM((feats, width), BF16),
        pltpu.VMEM((feats, width), BF16),
        pltpu.VMEM((width, PJ), BF16),
        pltpu.VMEM((toks, cols), BF16),
        pltpu.VMEM((feats, width), BF16),
        pltpu.VMEM((feats, width), BF16),
        pltpu.VMEM((feats, width), BF16),
        pltpu.VMEM((4, toks, feats), BF16),
        pltpu.VMEM((4, toks, feats), BF16),
        pltpu.VMEM((4, toks, PJ), BF16),
        pltpu.VMEM((4, 8, n_slots), F32),
        pltpu.VMEM((heads, toks, HD), BF16),
        pltpu.VMEM((heads, toks, HD), BF16),
        pltpu.VMEM((feats, toks), BF16),
        pltpu.VMEM((feats, toks), BF16),
        pltpu.VMEM((heads, toks, 4 * toks), F32),
        pltpu.VMEM((heads, toks, 4 * toks), F32),
        pltpu.VMEM((heads, toks, 4 * toks), BF16),
        pltpu.VMEM((heads, toks, 4 * toks), BF16),
        pltpu.VMEM((2, 2, feats, toks), BF16),
        pltpu.VMEM((2, 2, feats, toks), BF16),
        pltpu.VMEM((2, feats, toks), BF16),
        pltpu.VMEM((2, feats, toks), BF16),
        pltpu.VMEM((2, feats, toks), F32),
        pltpu.VMEM((3, toks, feats), BF16),
        pltpu.VMEM((3, feats, toks), BF16),
        pltpu.VMEM((3, feats // 4, 4 * toks), BF16),
        pltpu.VMEM((3, 2, feats // 4, half), BF16),
        pltpu.VMEM((3, 2, feats // 8, half), BF16),
        pltpu.VMEM((n_head - 1, toks, cols), BF16),
        pltpu.VMEM((n_head - 1, toks, cols), BF16),
        pltpu.VMEM((n_head, toks, cols), F32),
        pltpu.SemaphoreType.DMA((n_copies,)),
        pltpu.SemaphoreType.DMA((n_copies,)),
        pltpu.SemaphoreType.DMA((6,)),
        pltpu.SemaphoreType.DMA((4,)),
    ]
    grad_w = jax.ShapeDtypeStruct((feats, width), BF16)
    shapes = (grad_w, grad_w, grad_w, jax.ShapeDtypeStruct((toks, cols), BF16))
    results = pl.pallas_call(
        functools.partial(fused_kernel, n_head, n_copies),
        out_shape=shapes,
        in_specs=[hbm] * 6 + [vmem] * 4,
        out_specs=(hbm,) * 4,
        scratch_shapes=scratch,
        compiler_params=pltpu.CompilerParams(
            collective_id=0, has_side_effects=True, vmem_limit_bytes=56 * 1024 * 1024
        ),
        name="attention_backward",
    )(
        hidden_in,
        ctx_grad,
        w_query,
        w_key,
        w_value,
        w_junction,
        donor_pos,
        acceptor_pos,
        junction_counts,
        pred_grad,
    )
    chunks = 4
    out_q, out_k, out_v, out_in = pl.pallas_call(
        functools.partial(write_kernel, 4, chunks),
        out_shape=shapes,
        in_specs=[hbm] * 4,
        out_specs=(hbm,) * 4,
        scratch_shapes=[pltpu.VMEM(s.shape, s.dtype) for s in shapes]
        + [pltpu.SemaphoreType.DMA((4 * chunks,)), pltpu.SemaphoreType.DMA((4 * chunks,))],
        compiler_params=pltpu.CompilerParams(vmem_limit_bytes=56 * 1024 * 1024),
        name="write_results",
    )(*results)
    return out_in[None], out_q, out_k, out_v


def on_device(
    hidden_in,
    ctx_grad,
    w_query,
    w_key,
    w_value,
    w_junction,
    donor_pos,
    acceptor_pos,
    junction_counts,
    pred_grad,
):
    hidden = hidden_in[0]
    local_len = hidden.shape[0]
    shard_count = lax.axis_size("seq")
    total_len = local_len * shard_count
    heads_dev = w_query.shape[0] // HD
    softmax_scale = HD ** (-0.5)
    pair_scale = PJ ** (-0.5)
    queries = jnp.einsum("td,cd->tc", hidden, w_query, preferred_element_type=jnp.float32).astype(
        jnp.bfloat16
    )
    key_rows = jnp.einsum("td,cd->tc", hidden, w_key, preferred_element_type=jnp.float32).astype(
        jnp.bfloat16
    )
    value_rows = jnp.einsum(
        "td,cd->tc", hidden, w_value, preferred_element_type=jnp.float32
    ).astype(jnp.bfloat16)
    features = jnp.dot(hidden, w_junction, preferred_element_type=jnp.float32).astype(jnp.bfloat16)
    all_keys, all_values, all_features = (
        lax.all_gather(key_rows, "seq", axis=0, tiled=True),
        lax.all_gather(value_rows, "seq", axis=0, tiled=True),
        lax.all_gather(features, "seq", axis=0, tiled=True),
    )
    query_heads = queries.reshape(local_len, heads_dev, HD)
    grad_heads = ctx_grad[0].reshape(local_len, heads_dev, HD)
    key_heads = all_keys.reshape(total_len, heads_dev, HD)
    value_heads = all_values.reshape(total_len, heads_dev, HD)
    scores = (
        jnp.einsum("qhd,khd->hqk", query_heads, key_heads, preferred_element_type=jnp.float32)
        * softmax_scale
    )
    row_max = jnp.max(scores, axis=-1, keepdims=True)
    expd = jnp.exp(scores - row_max)
    probs = expd / jnp.sum(expd, axis=-1, keepdims=True)
    dprobs = jnp.einsum("qhd,khd->hqk", grad_heads, value_heads, preferred_element_type=jnp.float32)
    row_delta = jnp.sum(probs * dprobs, axis=-1, keepdims=True)
    dscores = probs * (dprobs - row_delta)
    probs_b = probs.astype(jnp.bfloat16)
    dscores_b = dscores.astype(jnp.bfloat16)
    query_grad = (
        (
            jnp.einsum("hqk,khd->qhd", dscores_b, key_heads, preferred_element_type=jnp.float32)
            * softmax_scale
        )
        .astype(jnp.bfloat16)
        .reshape(local_len, heads_dev * HD)
    )
    key_term = (
        jnp.einsum("hqk,qhd->khd", dscores_b, query_heads, preferred_element_type=jnp.float32)
        * softmax_scale
    ).reshape(total_len, heads_dev * HD)
    value_term = jnp.einsum(
        "hqk,qhd->khd", probs_b, grad_heads, preferred_element_type=jnp.float32
    ).reshape(total_len, heads_dev * HD)
    key_sum, value_sum = (
        lax.psum_scatter(
            key_term.astype(jnp.bfloat16), "seq", scatter_dimension=0, tiled=True
        ).astype(jnp.float32),
        lax.psum_scatter(
            value_term.astype(jnp.bfloat16), "seq", scatter_dimension=0, tiled=True
        ).astype(jnp.float32),
    )
    key_grad = key_sum.astype(jnp.bfloat16)
    value_grad = value_sum.astype(jnp.bfloat16)
    donor_idx = donor_pos[0, 0]
    accept_idx = acceptor_pos[0, 0]
    slot_dev = donor_idx.shape[1]
    slot_ids = lax.axis_index("head") * slot_dev + jnp.arange(slot_dev, dtype=jnp.int32)
    live_slots = slot_ids[None, :] < junction_counts[0, 0][:, None]
    donor_feat = features[donor_idx].astype(jnp.float32)
    accept_glob = jnp.arange(shard_count, dtype=jnp.int32)[:, None] * local_len + accept_idx
    accept_rows = all_features[accept_glob]
    accept_feat = accept_rows.astype(jnp.float32)
    pair_score = jnp.sum(donor_feat * accept_feat, axis=-1) * pair_scale
    slot_grad = (
        jnp.where(live_slots, pred_grad[0, 0] * jax.nn.sigmoid(pair_score), 0.0) * pair_scale
    )
    donor_term = slot_grad[..., None] * accept_feat
    accept_term = slot_grad[..., None] * donor_feat
    pair_width = features.shape[1]
    grad_feat = (
        jnp.zeros((local_len, pair_width), jnp.float32)
        .at[donor_idx.reshape(-1)]
        .add(donor_term.reshape(-1, pair_width))
    )
    spread_term = (
        jnp.zeros((total_len, pair_width), jnp.float32)
        .at[accept_glob.reshape(-1)]
        .add(accept_term.reshape(-1, pair_width))
    )
    grad_feat = grad_feat + lax.psum_scatter(
        spread_term.astype(jnp.bfloat16), "seq", scatter_dimension=0, tiled=True
    ).astype(jnp.float32)
    grad_feat_b = grad_feat.astype(jnp.bfloat16)
    input_term = jnp.einsum("tc,cd->td", query_grad, w_query, preferred_element_type=jnp.float32)
    input_term = input_term + jnp.einsum(
        "tc,cd->td", key_grad, w_key, preferred_element_type=jnp.float32
    )
    input_term = input_term + jnp.einsum(
        "tc,cd->td", value_grad, w_value, preferred_element_type=jnp.float32
    )
    input_term = input_term + jnp.einsum(
        "tp,dp->td", grad_feat_b, w_junction, preferred_element_type=jnp.float32
    )
    grad_input = lax.psum_scatter(
        input_term.astype(jnp.bfloat16), "head", scatter_dimension=1, tiled=True
    )
    key_wterm = jnp.einsum("tc,td->cd", key_grad, hidden, preferred_element_type=jnp.float32)
    value_wterm = jnp.einsum("tc,td->cd", value_grad, hidden, preferred_element_type=jnp.float32)
    query_wterm = jnp.einsum("tc,td->cd", query_grad, hidden, preferred_element_type=jnp.float32)
    query_wsum, key_wsum, value_wsum = lax.psum(
        (query_wterm, key_wterm, value_wterm), ("interval", "seq")
    )
    return (
        grad_input[None],
        query_wsum.astype(jnp.bfloat16),
        key_wsum.astype(jnp.bfloat16),
        value_wsum.astype(jnp.bfloat16),
    )


def solution(mesh):
    placed = (
        P("interval", "seq", None),
        P("interval", "seq", "head"),
        P("head", None),
        P("head", None),
        P("head", None),
        P(),
        P("interval", "seq", None, "head"),
        P("interval", "seq", None, "head"),
        P("interval", "seq", None),
        P("interval", "seq", None, "head"),
    )
    shape = dict(mesh.shape)
    fits = shape["interval"] == 2 and shape["seq"] == 4 and shape["head"] == 4
    run = functools.partial(fused_device, shape["head"]) if fits else on_device
    return jax.shard_map(
        run,
        mesh=mesh,
        in_specs=placed,
        out_specs=(P("interval", "seq", "head"), P("head", None), P("head", None), P("head", None)),
        check_vma=False,
    )
```

```python
import functools

import jax
import jax.numpy as jnp
from jax import lax
from jax.experimental import pallas as pl
from jax.experimental.pallas import tpu as pltpu
from jax.sharding import PartitionSpec as P

HD = 192
PJ = 128
MESH = pl.DeviceIdType.MESH
F32 = jnp.float32
BF16 = jnp.bfloat16


def dot_nn(a, b):
    return lax.dot_general(a, b, (((1,), (0,)), ((), ())), preferred_element_type=F32)


def dot_nt(a, b):
    return lax.dot_general(a, b, (((1,), (1,)), ((), ())), preferred_element_type=F32)


def dot_tn(a, b):
    return lax.dot_general(a, b, (((0,), (0,)), ((), ())), preferred_element_type=F32)


def fused_kernel(
    n_head,
    n_copies,
    hid_hbm,
    ctx_hbm,
    wq_hbm,
    wk_hbm,
    wv_hbm,
    wj_hbm,
    donor,
    accept,
    counts,
    pred,
    q_hbm,
    k_hbm,
    v_hbm,
    in_hbm,
    hidbuf,
    ctx,
    wq,
    wk,
    wv,
    wj,
    out_in,
    out_q,
    out_k,
    out_v,
    kbuf,
    vbuf,
    fbuf,
    slotbuf,
    qbuf,
    ctx_h,
    q_t,
    ctx_t,
    sref,
    dpref,
    pb,
    dsb,
    term,
    from_sib,
    pair_sum,
    from_xn,
    own_term,
    grads,
    grads_t,
    gcat,
    dwp,
    rsum,
    zsend,
    zrecv,
    zown,
    send_sems,
    recv_sems,
    load_sems,
    store_sems,
):
    toks = ctx.shape[0]
    width = hidbuf.shape[1]
    feats = wq.shape[0]
    heads = feats // HD
    half = width // 2
    row_y = feats // 2
    row_c = feats // 4
    row_x = feats // 8
    scale = HD**-0.5
    iv = lax.axis_index("interval")
    sq = lax.axis_index("seq")
    hd = lax.axis_index("head")
    xi = lax.div(sq, 2)
    core = lax.rem(sq, 2)
    s_sib = sq + 1 - 2 * core
    s_xn = lax.rem(sq + 2, 4)
    s_dg = lax.rem(s_sib + 2, 4)
    sib = (iv, s_sib, hd)
    xn = (iv, s_xn, hd)
    yn = (1 - iv, sq, hd)
    ysib = (1 - iv, s_sib, hd)
    zpeers = [(iv, sq, lax.rem(hd + d, n_head)) for d in range(1, n_head)]
    zpair = (iv, sq, hd + 1 - 2 * lax.rem(hd, 2))
    split = toks // 2
    mine_z = lax.rem(hd, 2) * split
    hid = hidbuf.at[0:toks]

    def z_rows(base):
        return pl.ds(pl.multiple_of(base + mine_z, 16), split)


    loads = []
    for i, (src, dst) in enumerate(
        (
            (hid_hbm.at[0], hid),
            (wj_hbm, wj),
            (wk_hbm, wk),
            (wv_hbm, wv),
            (wq_hbm, wq),
            (ctx_hbm.at[0], ctx),
        )
    ):
        load = pltpu.make_async_copy(src, dst, load_sems.at[i])
        load.start()
        loads.append(load)

    counter = [0]
    started = []

    def send(src, dst, dev):
        i = counter[0]
        counter[0] += 1
        copy = pltpu.make_async_remote_copy(
            src_ref=src,
            dst_ref=dst,
            send_sem=send_sems.at[i],
            recv_sem=recv_sems.at[i],
            device_id=dev,
            device_id_type=MESH,
        )
        copy.start()
        started.append(copy)
        return copy

    stores = []

    def store(src, dst):
        copy = pltpu.make_async_copy(src, dst, store_sems.at[len(stores)])
        copy.start()
        stores.append(copy)

    barrier = pltpu.get_barrier_semaphore()
    peers = [sib, xn, yn, ysib] + zpeers
    for dev in peers:
        pl.semaphore_signal(barrier, inc=1, device_id=dev, device_id_type=MESH)

    loads[0].wait()
    loads[1].wait()
    fbuf[0] = dot_nn(hid[...], wj[...]).astype(BF16)
    loads[2].wait()
    kbuf[0] = dot_nt(hid[...], wk[...]).astype(BF16)
    pl.semaphore_wait(barrier, len(peers))
    f_xn = send(fbuf.at[0, z_rows(0)], fbuf.at[2, z_rows(0)], xn)
    f_sib = send(fbuf.at[0], fbuf.at[1], sib)
    k_xn = send(kbuf.at[0], kbuf.at[2], xn)
    k_sib = send(kbuf.at[0], kbuf.at[1], sib)
    hid_yn = []
    for p in range(2):
        lanes = slice(p * half, (p + 1) * half)
        hid_yn.append(
            send(hidbuf.at[z_rows(0), lanes], hidbuf.at[z_rows(2 * toks), lanes], yn)
        )
    n_acc, slot_dev = donor.shape[2], donor.shape[3]
    n_slots = slotbuf.shape[2]
    acc_iota = lax.broadcasted_iota(jnp.int32, (n_acc, slot_dev), 0)
    slot_ids = lax.broadcasted_iota(jnp.int32, (n_acc, slot_dev), 1) + hd * slot_dev
    live_count = jnp.zeros((n_acc, slot_dev), jnp.int32)
    for j in range(n_acc):
        live_count = jnp.where(acc_iota == j, counts[0, :, j : j + 1], live_count)
    donor_tok = (donor[0, 0] + sq * toks).astype(F32)
    accept_tok = (accept[0, 0] + acc_iota * toks).astype(F32)
    pred_live = jnp.where(slot_ids < live_count, pred[0, 0], 0.0)
    lane_iota = lax.broadcasted_iota(jnp.int32, (n_acc, n_slots), 1)
    row_iota = lax.broadcasted_iota(jnp.int32, (n_acc, n_slots), 0)
    place = lane_iota - (sq * n_acc + row_iota) * slot_dev
    slotbuf[0] = jnp.zeros(slotbuf.shape[1:], F32)
    for i, values in enumerate((donor_tok, accept_tok, pred_live)):
        spread = jnp.zeros((n_acc, n_slots), F32)
        for j in range(slot_dev):
            spread = jnp.where(place == j, values[:, j : j + 1], spread)
        slotbuf[0, i : i + 1, :] = jnp.sum(spread, axis=0, keepdims=True)
    t_xn = send(slotbuf.at[0], slotbuf.at[2], xn)
    t_sib = send(slotbuf.at[0], slotbuf.at[1], sib)
    loads[3].wait()
    vbuf[0] = dot_nt(hid[...], wv[...]).astype(BF16)
    v_xn = send(vbuf.at[0], vbuf.at[2], xn)
    v_sib = send(vbuf.at[0], vbuf.at[1], sib)
    loads[4].wait()
    q_full = dot_nt(hid[...], wq[...])
    for h in range(heads):
        qbuf[h] = q_full[:, h * HD : (h + 1) * HD].astype(BF16)
    q_t[...] = jnp.transpose(q_full).astype(BF16)
    hid_sib = send(hidbuf.at[0:toks], hidbuf.at[toks : 2 * toks], sib)

    def head_cols(h):
        return slice(h * HD, (h + 1) * HD)

    def block_cols(r):
        return slice(r * toks, (r + 1) * toks)

    def scores(r):
        for h in range(heads):
            sref[h, :, block_cols(r)] = dot_nt(qbuf[h], kbuf[r, :, head_cols(h)])

    def dprobs(r):
        for h in range(heads):
            dpref[h, :, block_cols(r)] = dot_nt(ctx_h[h], vbuf[r, :, head_cols(h)])

    def pass_on(arrived, ref):
        arrived.wait_recv()
        return send(ref, ref, zpair)

    def hid_lanes(p):
        return slice(p * half, (p + 1) * half)

    f_z = pass_on(f_xn, fbuf.at[2, z_rows(0)])
    t_xn.wait_recv()
    t_fw = send(slotbuf.at[2], slotbuf.at[3], sib)
    scores(0)
    loads[5].wait()
    ctx_t[...] = jnp.transpose(ctx[...].astype(F32)).astype(BF16)
    for h in range(heads):
        ctx_h[h] = ctx[:, head_cols(h)]
    dprobs(0)
    f_z.wait_recv()
    f_fw = send(fbuf.at[2], fbuf.at[3], sib)
    k_sib.wait_recv()
    scores(1)
    f_sib.wait_recv()
    t_sib.wait_recv()
    f_fw.wait_recv()
    t_fw.wait_recv()
    rows_all = slotbuf[0] + slotbuf[1] + slotbuf[2] + slotbuf[3]
    donor_row = rows_all[0:1, :]
    accept_row = rows_all[1:2, :]
    pred_row = rows_all[2:3, :]
    tok_iota = lax.broadcasted_iota(jnp.int32, (toks, n_slots), 0)
    own_donor = None
    own_accept = None
    donor_t = jnp.zeros((PJ, n_slots), F32)
    accept_t = jnp.zeros((PJ, n_slots), F32)
    for r, shard in enumerate((sq, s_sib, s_xn, s_dg)):
        tok = (tok_iota + shard * toks).astype(F32)
        hot_d = jnp.where(tok == donor_row, 1.0, 0.0).astype(BF16)
        hot_a = jnp.where(tok == accept_row, 1.0, 0.0).astype(BF16)
        if r == 0:
            own_donor, own_accept = hot_d, hot_a
        donor_t = donor_t + dot_tn(fbuf[r], hot_d)
        accept_t = accept_t + dot_tn(fbuf[r], hot_a)
    pair_scale = PJ**-0.5
    pair = jnp.sum(donor_t * accept_t, axis=0, keepdims=True) * pair_scale
    slot_grad = pred_row * (1.0 / (1.0 + jnp.exp(-pair))) * pair_scale
    grad_feat = dot_nt(own_donor, (slot_grad * accept_t).astype(BF16)) + dot_nt(
        own_accept, (slot_grad * donor_t).astype(BF16)
    )
    grad_feat = grad_feat.astype(BF16)

    k_xn.wait_recv()
    k_fw = send(kbuf.at[2], kbuf.at[3], sib)
    scores(2)
    k_fw.wait_recv()
    scores(3)

    rows_step = 16

    @pl.loop(0, toks // rows_step)
    def _(i):
        rows = pl.ds(pl.multiple_of(i * rows_step, rows_step), rows_step)
        raws = [sref[h, rows, :] * scale for h in range(heads)]
        tops = [jnp.max(raw, axis=-1, keepdims=True) for raw in raws]
        es = [jnp.exp(raw - top) for raw, top in zip(raws, tops)]
        sums = [jnp.sum(e, axis=-1, keepdims=True) for e in es]
        ps = [e * (1.0 / total) for e, total in zip(es, sums)]
        for h in range(heads):
            sref[h, rows, :] = ps[h]
            pb[h, rows, :] = ps[h].astype(BF16)

    def kv_terms(which, left_t, right, factor):
        def one(h, r):
            part = dot_nn(left_t[head_cols(h), :], right[h, :, block_cols(r)])
            return part * factor if factor != 1.0 else part

        for h in range(heads):
            term[which, 0, head_cols(h), :] = one(h, 3).astype(BF16)
        a = send(term.at[which, 0], from_sib.at[which, 0], sib)
        for h in range(heads):
            term[which, 1, head_cols(h), :] = one(h, 1).astype(BF16)
        b = send(term.at[which, 1], from_sib.at[which, 1], sib)
        for h in range(heads):
            own_term[which, head_cols(h), :] = one(h, 2)
        a.wait_recv()
        pair_sum[which] = (own_term[which] + from_sib[which, 0].astype(F32)).astype(BF16)
        c = send(pair_sum.at[which], from_xn.at[which], xn)
        for h in range(heads):
            own_term[which, head_cols(h), :] = one(h, 0)
        return b, c

    def g_rows(y, c):
        return pl.ds(pl.multiple_of(y * row_y + c * row_c, 16), row_c)

    g_copy = [None] * 3

    def exchange(slot):
        gcat[slot, :, 0:toks] = grads_t[slot, g_rows(iv, core), :]
        copies = []
        for b, dev, y, c in ((2, yn, 1 - iv, core), (3, ysib, 1 - iv, 1 - core), (1, sib, iv, 1 - core)):
            copies.append(
                send(grads_t.at[slot, g_rows(y, c)], gcat.at[slot, :, block_cols(b)], dev)
            )
        g_copy[slot] = copies

    def kv_final(which, slot, b, c):
        b.wait_recv()
        c.wait_recv()
        total = own_term[which] + from_sib[which, 1].astype(F32) + from_xn[which].astype(F32)
        grads_t[slot] = total.astype(BF16)
        exchange(slot)

    hid_z = [pass_on(hid_yn[0], hidbuf.at[z_rows(2 * toks), hid_lanes(0)])]
    v_pend = kv_terms(1, ctx_t, pb, 1.0)
    v_sib.wait_recv()
    dprobs(1)
    v_xn.wait_recv()
    v_fw = send(vbuf.at[2], vbuf.at[3], sib)
    hid_z.append(pass_on(hid_yn[1], hidbuf.at[z_rows(2 * toks), hid_lanes(1)]))
    dprobs(2)
    v_fw.wait_recv()
    dprobs(3)

    @pl.loop(0, toks // rows_step)
    def _(i):
        rows = pl.ds(pl.multiple_of(i * rows_step, rows_step), rows_step)
        ps = [sref[h, rows, :] for h in range(heads)]
        dps = [dpref[h, rows, :] for h in range(heads)]
        deltas = [jnp.sum(p * dp, axis=-1, keepdims=True) for p, dp in zip(ps, dps)]
        for h in range(heads):
            dsb[h, rows, :] = (ps[h] * (dps[h] - deltas[h])).astype(BF16)

    k_pend = kv_terms(0, q_t, dsb, scale)

    q_parts = []
    for h in range(heads):
        acc = dot_nn(dsb[h, :, block_cols(0)], kbuf[0, :, head_cols(h)])
        for r in range(1, 4):
            acc = acc + dot_nn(dsb[h, :, block_cols(r)], kbuf[r, :, head_cols(h)])
        q_parts.append(acc * scale)
    q_grad = jnp.concatenate(q_parts, axis=-1)
    grads_t[0] = jnp.transpose(q_grad).astype(BF16)
    exchange(0)
    grads[0] = q_grad.astype(BF16)

    hid_fw = []
    for p in range(2):
        lanes = hid_lanes(p)
        hid_z[p].wait_recv()
        hid_fw.append(
            send(hidbuf.at[2 * toks : 3 * toks, lanes], hidbuf.at[3 * toks : 4 * toks, lanes], sib)
        )

    outs = (out_q, out_k, out_v)
    outs_hbm = (q_hbm, k_hbm, v_hbm)
    rs_copy = {}
    piece_copy = {}
    fwd_copy = {}
    sib_copy = {0: [], 1: [], 2: []}

    def x_rows(x):
        return pl.ds(pl.multiple_of(x * row_x, 16), row_x)

    def piece(w, p, y, x):
        start = pl.multiple_of(y * row_y + core * row_c + x * row_x, 16)
        return outs[w].at[pl.ds(start, row_x), slice(p * half, (p + 1) * half)]

    def to_sib(w, ref):
        sib_copy[w].append(send(ref, ref, sib))

    def dw_start(w):
        for copy in g_copy[w]:
            copy.wait_recv()
        for p in range(2):
            dwp[w, p] = dot_nn(gcat[w], hidbuf[:, p * half : (p + 1) * half]).astype(BF16)
            rs_copy[w, p] = send(dwp.at[w, p, x_rows(1 - xi)], rsum.at[w, p], xn)

    def dw_final(w):
        for p in range(2):
            rs_copy[w, p].wait_recv()
            done = dwp[w, p, x_rows(xi), :].astype(F32) + rsum[w, p].astype(F32)
            ref = piece(w, p, iv, xi)
            ref[...] = done.astype(BF16)
            cx = send(ref, ref, xn)
            cy = send(ref, ref, yn)
            piece_copy[w, p] = (cx, cy)
            to_sib(w, ref)

    def dw_forward(w):
        for p in range(2):
            cx, cy = piece_copy[w, p]
            cx_ref = piece(w, p, iv, 1 - xi)
            cy_ref = piece(w, p, 1 - iv, xi)
            first, ref, dev = ((cx, cx_ref, yn), (cy, cy_ref, xn))[p]
            first.wait_recv()
            fwd_copy[w, p] = send(ref, ref, dev)
            to_sib(w, ref)
        for p in range(2):
            cx, cy = piece_copy[w, p]
            if p == 0:
                cy.wait_recv()
                to_sib(w, piece(w, p, 1 - iv, xi))
            else:
                cx.wait_recv()
                to_sib(w, piece(w, p, iv, 1 - xi))

    def dw_last(w):
        for p in range(2):
            fwd_copy[w, p].wait_recv()
            to_sib(w, piece(w, p, 1 - iv, 1 - xi))

    def dw_out(w):
        for copy in sib_copy[w]:
            copy.wait_recv()
        store(outs[w], outs_hbm[w])

    kv_final(1, 2, *v_pend)
    hid_sib.wait_recv()
    hid_fw[0].wait_recv()
    hid_fw[1].wait_recv()
    dw_start(0)
    kv_final(0, 1, *k_pend)
    dw_start(2)
    dw_final(0)
    dw_start(1)
    for slot in (1, 2):
        grads[slot] = jnp.transpose(grads_t[slot].astype(F32)).astype(BF16)
    dw_final(2)

    cols = width // n_head
    z_copy = []

    def input_block(d):
        owner = lax.rem(hd + d, n_head) if d > 0 else hd
        lanes = pl.ds(pl.multiple_of(owner * cols, 128), cols)
        acc = dot_nn(grads[0], wq[:, lanes]) + dot_nn(grads[1], wk[:, lanes])
        acc = acc + dot_nn(grads[2], wv[:, lanes])
        return acc + dot_nt(grad_feat, wj[lanes, :])

    def input_send(d):
        zsend[d - 1] = input_block(d).astype(BF16)
        z_copy.append((d, send(zsend.at[d - 1], zrecv.at[d - 1], zpeers[d - 1])))

    input_send(2)
    dw_final(1)
    input_send(1)
    dw_forward(0)
    input_send(3)
    dw_forward(2)
    zown[...] = input_block(0)
    dw_forward(1)
    dw_last(0)
    dw_last(2)
    dw_out(0)
    dw_last(1)
    for d, copy in z_copy:
        copy.wait_recv()
    total = zown[...]
    for d in range(n_head - 1):
        total = total + zrecv[d].astype(F32)
    out_in[...] = total.astype(BF16)
    store(out_in, in_hbm)
    dw_out(2)
    dw_out(1)
    for copy in started:
        copy.wait_send()
    for copy in stores:
        copy.wait()
    assert counter[0] <= n_copies


def write_kernel(n, chunks, *refs):
    sources, targets = refs[:n], refs[n : 2 * n]
    staged = refs[2 * n : 3 * n]
    load_sems, store_sems = refs[3 * n :]
    steps = []
    for a in range(n):
        rows = staged[a].shape[0] // chunks
        for c in range(chunks):
            part = pl.ds(c * rows, rows)
            i = len(steps)
            load = pltpu.make_async_copy(sources[a].at[part], staged[a].at[part], load_sems.at[i])
            store = pltpu.make_async_copy(staged[a].at[part], targets[a].at[part], store_sems.at[i])
            load.start()
            steps.append((load, store))
    for load, store in steps:
        load.wait()
        store.start()
    for _, store in steps:
        store.wait()


def fused_device(
    n_head,
    hidden_in,
    ctx_grad,
    w_query,
    w_key,
    w_value,
    w_junction,
    donor_pos,
    acceptor_pos,
    junction_counts,
    pred_grad,
):
    toks, width = hidden_in.shape[1:]
    feats = w_query.shape[0]
    heads = feats // HD
    n_seq = 4
    n_slots = n_seq * donor_pos.shape[2] * donor_pos.shape[3]
    n_copies = 96
    vmem = pl.BlockSpec(memory_space=pltpu.VMEM)
    hbm = pl.BlockSpec(memory_space=pl.ANY)
    half = width // 2
    cols = width // n_head
    scratch = [
        pltpu.VMEM((4 * toks, width), BF16),
        pltpu.VMEM((toks, feats), BF16),
        pltpu.VMEM((feats, width), BF16),
        pltpu.VMEM((feats, width), BF16),
        pltpu.VMEM((feats, width), BF16),
        pltpu.VMEM((width, PJ), BF16),
        pltpu.VMEM((toks, cols), BF16),
        pltpu.VMEM((feats, width), BF16),
        pltpu.VMEM((feats, width), BF16),
        pltpu.VMEM((feats, width), BF16),
        pltpu.VMEM((4, toks, feats), BF16),
        pltpu.VMEM((4, toks, feats), BF16),
        pltpu.VMEM((4, toks, PJ), BF16),
        pltpu.VMEM((4, 8, n_slots), F32),
        pltpu.VMEM((heads, toks, HD), BF16),
        pltpu.VMEM((heads, toks, HD), BF16),
        pltpu.VMEM((feats, toks), BF16),
        pltpu.VMEM((feats, toks), BF16),
        pltpu.VMEM((heads, toks, 4 * toks), F32),
        pltpu.VMEM((heads, toks, 4 * toks), F32),
        pltpu.VMEM((heads, toks, 4 * toks), BF16),
        pltpu.VMEM((heads, toks, 4 * toks), BF16),
        pltpu.VMEM((2, 2, feats, toks), BF16),
        pltpu.VMEM((2, 2, feats, toks), BF16),
        pltpu.VMEM((2, feats, toks), BF16),
        pltpu.VMEM((2, feats, toks), BF16),
        pltpu.VMEM((2, feats, toks), F32),
        pltpu.VMEM((3, toks, feats), BF16),
        pltpu.VMEM((3, feats, toks), BF16),
        pltpu.VMEM((3, feats // 4, 4 * toks), BF16),
        pltpu.VMEM((3, 2, feats // 4, half), BF16),
        pltpu.VMEM((3, 2, feats // 8, half), BF16),
        pltpu.VMEM((n_head - 1, toks, cols), BF16),
        pltpu.VMEM((n_head - 1, toks, cols), BF16),
        pltpu.VMEM((toks, cols), F32),
        pltpu.SemaphoreType.DMA((n_copies,)),
        pltpu.SemaphoreType.DMA((n_copies,)),
        pltpu.SemaphoreType.DMA((6,)),
        pltpu.SemaphoreType.DMA((4,)),
    ]
    grad_w = jax.ShapeDtypeStruct((feats, width), BF16)
    shapes = (grad_w, grad_w, grad_w, jax.ShapeDtypeStruct((toks, cols), BF16))
    results = pl.pallas_call(
        functools.partial(fused_kernel, n_head, n_copies),
        out_shape=shapes,
        in_specs=[hbm] * 6 + [vmem] * 4,
        out_specs=(hbm,) * 4,
        scratch_shapes=scratch,
        compiler_params=pltpu.CompilerParams(
            collective_id=0, has_side_effects=True, vmem_limit_bytes=56 * 1024 * 1024
        ),
        name="attention_backward",
    )(
        hidden_in,
        ctx_grad,
        w_query,
        w_key,
        w_value,
        w_junction,
        donor_pos,
        acceptor_pos,
        junction_counts,
        pred_grad,
    )
    chunks = 4
    out_q, out_k, out_v, out_in = pl.pallas_call(
        functools.partial(write_kernel, 4, chunks),
        out_shape=shapes,
        in_specs=[hbm] * 4,
        out_specs=(hbm,) * 4,
        scratch_shapes=[pltpu.VMEM(s.shape, s.dtype) for s in shapes]
        + [pltpu.SemaphoreType.DMA((4 * chunks,)), pltpu.SemaphoreType.DMA((4 * chunks,))],
        compiler_params=pltpu.CompilerParams(vmem_limit_bytes=56 * 1024 * 1024),
        name="write_results",
    )(*results)
    return out_in[None], out_q, out_k, out_v


def on_device(
    hidden_in,
    ctx_grad,
    w_query,
    w_key,
    w_value,
    w_junction,
    donor_pos,
    acceptor_pos,
    junction_counts,
    pred_grad,
):
    hidden = hidden_in[0]
    local_len = hidden.shape[0]
    shard_count = lax.axis_size("seq")
    total_len = local_len * shard_count
    heads_dev = w_query.shape[0] // HD
    softmax_scale = HD ** (-0.5)
    pair_scale = PJ ** (-0.5)
    queries = jnp.einsum("td,cd->tc", hidden, w_query, preferred_element_type=jnp.float32).astype(
        jnp.bfloat16
    )
    key_rows = jnp.einsum("td,cd->tc", hidden, w_key, preferred_element_type=jnp.float32).astype(
        jnp.bfloat16
    )
    value_rows = jnp.einsum(
        "td,cd->tc", hidden, w_value, preferred_element_type=jnp.float32
    ).astype(jnp.bfloat16)
    features = jnp.dot(hidden, w_junction, preferred_element_type=jnp.float32).astype(jnp.bfloat16)
    all_keys, all_values, all_features = (
        lax.all_gather(key_rows, "seq", axis=0, tiled=True),
        lax.all_gather(value_rows, "seq", axis=0, tiled=True),
        lax.all_gather(features, "seq", axis=0, tiled=True),
    )
    query_heads = queries.reshape(local_len, heads_dev, HD)
    grad_heads = ctx_grad[0].reshape(local_len, heads_dev, HD)
    key_heads = all_keys.reshape(total_len, heads_dev, HD)
    value_heads = all_values.reshape(total_len, heads_dev, HD)
    scores = (
        jnp.einsum("qhd,khd->hqk", query_heads, key_heads, preferred_element_type=jnp.float32)
        * softmax_scale
    )
    row_max = jnp.max(scores, axis=-1, keepdims=True)
    expd = jnp.exp(scores - row_max)
    probs = expd / jnp.sum(expd, axis=-1, keepdims=True)
    dprobs = jnp.einsum("qhd,khd->hqk", grad_heads, value_heads, preferred_element_type=jnp.float32)
    row_delta = jnp.sum(probs * dprobs, axis=-1, keepdims=True)
    dscores = probs * (dprobs - row_delta)
    probs_b = probs.astype(jnp.bfloat16)
    dscores_b = dscores.astype(jnp.bfloat16)
    query_grad = (
        (
            jnp.einsum("hqk,khd->qhd", dscores_b, key_heads, preferred_element_type=jnp.float32)
            * softmax_scale
        )
        .astype(jnp.bfloat16)
        .reshape(local_len, heads_dev * HD)
    )
    key_term = (
        jnp.einsum("hqk,qhd->khd", dscores_b, query_heads, preferred_element_type=jnp.float32)
        * softmax_scale
    ).reshape(total_len, heads_dev * HD)
    value_term = jnp.einsum(
        "hqk,qhd->khd", probs_b, grad_heads, preferred_element_type=jnp.float32
    ).reshape(total_len, heads_dev * HD)
    key_sum, value_sum = (
        lax.psum_scatter(
            key_term.astype(jnp.bfloat16), "seq", scatter_dimension=0, tiled=True
        ).astype(jnp.float32),
        lax.psum_scatter(
            value_term.astype(jnp.bfloat16), "seq", scatter_dimension=0, tiled=True
        ).astype(jnp.float32),
    )
    key_grad = key_sum.astype(jnp.bfloat16)
    value_grad = value_sum.astype(jnp.bfloat16)
    donor_idx = donor_pos[0, 0]
    accept_idx = acceptor_pos[0, 0]
    slot_dev = donor_idx.shape[1]
    slot_ids = lax.axis_index("head") * slot_dev + jnp.arange(slot_dev, dtype=jnp.int32)
    live_slots = slot_ids[None, :] < junction_counts[0, 0][:, None]
    donor_feat = features[donor_idx].astype(jnp.float32)
    accept_glob = jnp.arange(shard_count, dtype=jnp.int32)[:, None] * local_len + accept_idx
    accept_rows = all_features[accept_glob]
    accept_feat = accept_rows.astype(jnp.float32)
    pair_score = jnp.sum(donor_feat * accept_feat, axis=-1) * pair_scale
    slot_grad = (
        jnp.where(live_slots, pred_grad[0, 0] * jax.nn.sigmoid(pair_score), 0.0) * pair_scale
    )
    donor_term = slot_grad[..., None] * accept_feat
    accept_term = slot_grad[..., None] * donor_feat
    pair_width = features.shape[1]
    grad_feat = (
        jnp.zeros((local_len, pair_width), jnp.float32)
        .at[donor_idx.reshape(-1)]
        .add(donor_term.reshape(-1, pair_width))
    )
    spread_term = (
        jnp.zeros((total_len, pair_width), jnp.float32)
        .at[accept_glob.reshape(-1)]
        .add(accept_term.reshape(-1, pair_width))
    )
    grad_feat = grad_feat + lax.psum_scatter(
        spread_term.astype(jnp.bfloat16), "seq", scatter_dimension=0, tiled=True
    ).astype(jnp.float32)
    grad_feat_b = grad_feat.astype(jnp.bfloat16)
    input_term = jnp.einsum("tc,cd->td", query_grad, w_query, preferred_element_type=jnp.float32)
    input_term = input_term + jnp.einsum(
        "tc,cd->td", key_grad, w_key, preferred_element_type=jnp.float32
    )
    input_term = input_term + jnp.einsum(
        "tc,cd->td", value_grad, w_value, preferred_element_type=jnp.float32
    )
    input_term = input_term + jnp.einsum(
        "tp,dp->td", grad_feat_b, w_junction, preferred_element_type=jnp.float32
    )
    grad_input = lax.psum_scatter(
        input_term.astype(jnp.bfloat16), "head", scatter_dimension=1, tiled=True
    )
    key_wterm = jnp.einsum("tc,td->cd", key_grad, hidden, preferred_element_type=jnp.float32)
    value_wterm = jnp.einsum("tc,td->cd", value_grad, hidden, preferred_element_type=jnp.float32)
    query_wterm = jnp.einsum("tc,td->cd", query_grad, hidden, preferred_element_type=jnp.float32)
    query_wsum, key_wsum, value_wsum = lax.psum(
        (query_wterm, key_wterm, value_wterm), ("interval", "seq")
    )
    return (
        grad_input[None],
        query_wsum.astype(jnp.bfloat16),
        key_wsum.astype(jnp.bfloat16),
        value_wsum.astype(jnp.bfloat16),
    )


def solution(mesh):
    placed = (
        P("interval", "seq", None),
        P("interval", "seq", "head"),
        P("head", None),
        P("head", None),
        P("head", None),
        P(),
        P("interval", "seq", None, "head"),
        P("interval", "seq", None, "head"),
        P("interval", "seq", None),
        P("interval", "seq", None, "head"),
    )
    shape = dict(mesh.shape)
    fits = shape["interval"] == 2 and shape["seq"] == 4 and shape["head"] == 4
    run = functools.partial(fused_device, shape["head"]) if fits else on_device
    return jax.shard_map(
        run,
        mesh=mesh,
        in_specs=placed,
        out_specs=(P("interval", "seq", "head"), P("head", None), P("head", None), P("head", None)),
        check_vma=False,
    )
```

```python
import functools

import jax
import jax.numpy as jnp
from jax import lax
from jax.experimental import pallas as pl
from jax.experimental.pallas import tpu as pltpu
from jax.sharding import PartitionSpec as P

HD = 192
PJ = 128
MESH = pl.DeviceIdType.MESH
F32 = jnp.float32
BF16 = jnp.bfloat16


def dot_nn(a, b):
    return lax.dot_general(a, b, (((1,), (0,)), ((), ())), preferred_element_type=F32)


def dot_nt(a, b):
    return lax.dot_general(a, b, (((1,), (1,)), ((), ())), preferred_element_type=F32)


def dot_tn(a, b):
    return lax.dot_general(a, b, (((0,), (0,)), ((), ())), preferred_element_type=F32)


def fused_kernel(
    n_head,
    n_copies,
    hid_hbm,
    ctx_hbm,
    wq_hbm,
    wk_hbm,
    wv_hbm,
    wj_hbm,
    donor,
    accept,
    counts,
    pred,
    out_q,
    out_k,
    out_v,
    out_in,
    hidbuf,
    ctx,
    wq,
    wk,
    wv,
    wj,
    kbuf,
    vbuf,
    fbuf,
    slotbuf,
    qbuf,
    ctx_h,
    q_t,
    ctx_t,
    sref,
    dpref,
    pb,
    dsb,
    term,
    from_sib,
    pair_sum,
    from_xn,
    own_term,
    grads,
    grads_t,
    gcat,
    dwp,
    rsum,
    zsend,
    zrecv,
    zown,
    send_sems,
    recv_sems,
    load_sems,
):
    toks = ctx.shape[0]
    width = hidbuf.shape[1]
    feats = wq.shape[0]
    heads = feats // HD
    half = width // 2
    row_y = feats // 2
    row_c = feats // 4
    row_x = feats // 8
    scale = HD**-0.5
    iv = lax.axis_index("interval")
    sq = lax.axis_index("seq")
    hd = lax.axis_index("head")
    xi = lax.div(sq, 2)
    core = lax.rem(sq, 2)
    s_sib = sq + 1 - 2 * core
    s_xn = lax.rem(sq + 2, 4)
    s_dg = lax.rem(s_sib + 2, 4)
    sib = (iv, s_sib, hd)
    xn = (iv, s_xn, hd)
    yn = (1 - iv, sq, hd)
    ysib = (1 - iv, s_sib, hd)
    zpeers = [(iv, sq, lax.rem(hd + d, n_head)) for d in range(1, n_head)]
    zpair = (iv, sq, hd + 1 - 2 * lax.rem(hd, 2))
    split = toks // 2
    mine_z = lax.rem(hd, 2) * split
    hid = hidbuf.at[0:toks]

    def z_rows(base):
        return pl.ds(pl.multiple_of(base + mine_z, 16), split)


    loads = []
    for i, (src, dst) in enumerate(
        (
            (hid_hbm.at[0], hid),
            (wj_hbm, wj),
            (wk_hbm, wk),
            (wv_hbm, wv),
            (wq_hbm, wq),
            (ctx_hbm.at[0], ctx),
        )
    ):
        load = pltpu.make_async_copy(src, dst, load_sems.at[i])
        load.start()
        loads.append(load)

    counter = [0]
    started = []

    def send(src, dst, dev):
        i = counter[0]
        counter[0] += 1
        copy = pltpu.make_async_remote_copy(
            src_ref=src,
            dst_ref=dst,
            send_sem=send_sems.at[i],
            recv_sem=recv_sems.at[i],
            device_id=dev,
            device_id_type=MESH,
        )
        copy.start()
        started.append(copy)
        return copy

    barrier = pltpu.get_barrier_semaphore()
    peers = [sib, xn, yn, ysib] + zpeers
    for dev in peers:
        pl.semaphore_signal(barrier, inc=1, device_id=dev, device_id_type=MESH)

    loads[0].wait()
    loads[1].wait()
    fbuf[0] = dot_nn(hid[...], wj[...]).astype(BF16)
    loads[2].wait()
    kbuf[0] = dot_nt(hid[...], wk[...]).astype(BF16)
    pl.semaphore_wait(barrier, len(peers))
    f_xn = send(fbuf.at[0, z_rows(0)], fbuf.at[2, z_rows(0)], xn)
    f_sib = send(fbuf.at[0], fbuf.at[1], sib)
    k_xn = send(kbuf.at[0], kbuf.at[2], xn)
    k_sib = send(kbuf.at[0], kbuf.at[1], sib)
    hid_yn = []
    for p in range(2):
        lanes = slice(p * half, (p + 1) * half)
        hid_yn.append(
            send(hidbuf.at[z_rows(0), lanes], hidbuf.at[z_rows(2 * toks), lanes], yn)
        )
    n_acc, slot_dev = donor.shape[2], donor.shape[3]
    n_slots = slotbuf.shape[2]
    acc_iota = lax.broadcasted_iota(jnp.int32, (n_acc, slot_dev), 0)
    slot_ids = lax.broadcasted_iota(jnp.int32, (n_acc, slot_dev), 1) + hd * slot_dev
    live_count = jnp.zeros((n_acc, slot_dev), jnp.int32)
    for j in range(n_acc):
        live_count = jnp.where(acc_iota == j, counts[0, :, j : j + 1], live_count)
    donor_tok = (donor[0, 0] + sq * toks).astype(F32)
    accept_tok = (accept[0, 0] + acc_iota * toks).astype(F32)
    pred_live = jnp.where(slot_ids < live_count, pred[0, 0], 0.0)
    lane_iota = lax.broadcasted_iota(jnp.int32, (n_acc, n_slots), 1)
    row_iota = lax.broadcasted_iota(jnp.int32, (n_acc, n_slots), 0)
    place = lane_iota - (sq * n_acc + row_iota) * slot_dev
    slotbuf[0] = jnp.zeros(slotbuf.shape[1:], F32)
    for i, values in enumerate((donor_tok, accept_tok, pred_live)):
        spread = jnp.zeros((n_acc, n_slots), F32)
        for j in range(slot_dev):
            spread = jnp.where(place == j, values[:, j : j + 1], spread)
        slotbuf[0, i : i + 1, :] = jnp.sum(spread, axis=0, keepdims=True)
    t_xn = send(slotbuf.at[0], slotbuf.at[2], xn)
    t_sib = send(slotbuf.at[0], slotbuf.at[1], sib)
    loads[3].wait()
    vbuf[0] = dot_nt(hid[...], wv[...]).astype(BF16)
    v_xn = send(vbuf.at[0], vbuf.at[2], xn)
    v_sib = send(vbuf.at[0], vbuf.at[1], sib)
    loads[4].wait()
    q_full = dot_nt(hid[...], wq[...])
    for h in range(heads):
        qbuf[h] = q_full[:, h * HD : (h + 1) * HD].astype(BF16)
    q_t[...] = jnp.transpose(q_full).astype(BF16)

    def head_cols(h):
        return slice(h * HD, (h + 1) * HD)

    def block_cols(r):
        return slice(r * toks, (r + 1) * toks)

    def scores(r):
        for h in range(heads):
            sref[h, :, block_cols(r)] = dot_nt(qbuf[h], kbuf[r, :, head_cols(h)])

    def dprobs(r):
        for h in range(heads):
            dpref[h, :, block_cols(r)] = dot_nt(ctx_h[h], vbuf[r, :, head_cols(h)])

    def pass_on(arrived, ref):
        arrived.wait_recv()
        return send(ref, ref, zpair)

    def hid_lanes(p):
        return slice(p * half, (p + 1) * half)

    f_z = pass_on(f_xn, fbuf.at[2, z_rows(0)])
    t_xn.wait_recv()
    t_fw = send(slotbuf.at[2], slotbuf.at[3], sib)
    scores(0)
    loads[5].wait()
    ctx_t[...] = jnp.transpose(ctx[...].astype(F32)).astype(BF16)
    for h in range(heads):
        ctx_h[h] = ctx[:, head_cols(h)]
    dprobs(0)
    f_z.wait_recv()
    f_fw = send(fbuf.at[2], fbuf.at[3], sib)
    k_sib.wait_recv()
    scores(1)
    f_sib.wait_recv()
    t_sib.wait_recv()
    f_fw.wait_recv()
    t_fw.wait_recv()
    rows_all = slotbuf[0] + slotbuf[1] + slotbuf[2] + slotbuf[3]
    donor_row = rows_all[0:1, :]
    accept_row = rows_all[1:2, :]
    pred_row = rows_all[2:3, :]
    tok_iota = lax.broadcasted_iota(jnp.int32, (toks, n_slots), 0)
    own_donor = None
    own_accept = None
    donor_t = jnp.zeros((PJ, n_slots), F32)
    accept_t = jnp.zeros((PJ, n_slots), F32)
    for r, shard in enumerate((sq, s_sib, s_xn, s_dg)):
        tok = (tok_iota + shard * toks).astype(F32)
        hot_d = jnp.where(tok == donor_row, 1.0, 0.0).astype(BF16)
        hot_a = jnp.where(tok == accept_row, 1.0, 0.0).astype(BF16)
        if r == 0:
            own_donor, own_accept = hot_d, hot_a
        donor_t = donor_t + dot_tn(fbuf[r], hot_d)
        accept_t = accept_t + dot_tn(fbuf[r], hot_a)
    pair_scale = PJ**-0.5
    pair = jnp.sum(donor_t * accept_t, axis=0, keepdims=True) * pair_scale
    slot_grad = pred_row * (1.0 / (1.0 + jnp.exp(-pair))) * pair_scale
    grad_feat = dot_nt(own_donor, (slot_grad * accept_t).astype(BF16)) + dot_nt(
        own_accept, (slot_grad * donor_t).astype(BF16)
    )
    grad_feat = grad_feat.astype(BF16)

    k_xn.wait_recv()
    k_fw = send(kbuf.at[2], kbuf.at[3], sib)
    scores(2)
    k_fw.wait_recv()
    scores(3)

    rows_step = 16

    @pl.loop(0, toks // rows_step)
    def _(i):
        rows = pl.ds(pl.multiple_of(i * rows_step, rows_step), rows_step)
        raws = [sref[h, rows, :] * scale for h in range(heads)]
        tops = [jnp.max(raw, axis=-1, keepdims=True) for raw in raws]
        es = [jnp.exp(raw - top) for raw, top in zip(raws, tops)]
        sums = [jnp.sum(e, axis=-1, keepdims=True) for e in es]
        ps = [e * (1.0 / total) for e, total in zip(es, sums)]
        for h in range(heads):
            sref[h, rows, :] = ps[h]
            pb[h, rows, :] = ps[h].astype(BF16)

    def kv_terms(which, left_t, right, factor):
        def one(h, r):
            part = dot_nn(left_t[head_cols(h), :], right[h, :, block_cols(r)])
            return part * factor if factor != 1.0 else part

        for h in range(heads):
            term[which, 0, head_cols(h), :] = one(h, 3).astype(BF16)
        a = send(term.at[which, 0], from_sib.at[which, 0], sib)
        for h in range(heads):
            term[which, 1, head_cols(h), :] = one(h, 1).astype(BF16)
        b = send(term.at[which, 1], from_sib.at[which, 1], sib)
        for h in range(heads):
            own_term[which, head_cols(h), :] = one(h, 2)
        return a, b

    def kv_cross(which, a):
        a.wait_recv()
        pair_sum[which] = (own_term[which] + from_sib[which, 0].astype(F32)).astype(BF16)
        return send(pair_sum.at[which], from_xn.at[which], xn)

    def kv_own(which, left_t, right, factor):
        for h in range(heads):
            part = dot_nn(left_t[head_cols(h), :], right[h, :, block_cols(0)])
            own_term[which, head_cols(h), :] = part * factor if factor != 1.0 else part

    def g_rows(y, c):
        return pl.ds(pl.multiple_of(y * row_y + c * row_c, 16), row_c)

    g_copy = [None] * 3

    def exchange(slot):
        gcat[slot, :, 0:toks] = grads_t[slot, g_rows(iv, core), :]
        copies = []
        for b, dev, y, c in ((2, yn, 1 - iv, core), (3, ysib, 1 - iv, 1 - core), (1, sib, iv, 1 - core)):
            copies.append(
                send(grads_t.at[slot, g_rows(y, c)], gcat.at[slot, :, block_cols(b)], dev)
            )
        g_copy[slot] = copies

    def kv_final(which, slot, b, c):
        b.wait_recv()
        c.wait_recv()
        total = own_term[which] + from_sib[which, 1].astype(F32) + from_xn[which].astype(F32)
        grads_t[slot] = total.astype(BF16)
        exchange(slot)

    hid_z = [pass_on(hid_yn[0], hidbuf.at[z_rows(2 * toks), hid_lanes(0)])]
    v_a, v_b = kv_terms(1, ctx_t, pb, 1.0)
    v_sib.wait_recv()
    dprobs(1)
    v_c = kv_cross(1, v_a)
    v_xn.wait_recv()
    v_fw = send(vbuf.at[2], vbuf.at[3], sib)
    hid_sib = send(hidbuf.at[0:toks], hidbuf.at[toks : 2 * toks], sib)
    hid_z.append(pass_on(hid_yn[1], hidbuf.at[z_rows(2 * toks), hid_lanes(1)]))
    dprobs(2)
    v_fw.wait_recv()
    dprobs(3)

    @pl.loop(0, toks // rows_step)
    def _(i):
        rows = pl.ds(pl.multiple_of(i * rows_step, rows_step), rows_step)
        ps = [sref[h, rows, :] for h in range(heads)]
        dps = [dpref[h, rows, :] for h in range(heads)]
        deltas = [jnp.sum(p * dp, axis=-1, keepdims=True) for p, dp in zip(ps, dps)]
        for h in range(heads):
            dsb[h, rows, :] = (ps[h] * (dps[h] - deltas[h])).astype(BF16)

    k_a, k_b = kv_terms(0, q_t, dsb, scale)

    q_parts = []
    for h in range(heads):
        acc = dot_nn(dsb[h, :, block_cols(0)], kbuf[0, :, head_cols(h)])
        for r in range(1, 4):
            acc = acc + dot_nn(dsb[h, :, block_cols(r)], kbuf[r, :, head_cols(h)])
        q_parts.append(acc * scale)
    k_c = kv_cross(0, k_a)
    q_grad = jnp.concatenate(q_parts, axis=-1)
    grads_t[0] = jnp.transpose(q_grad).astype(BF16)
    exchange(0)
    grads[0] = q_grad.astype(BF16)

    hid_fw = []
    for p in range(2):
        lanes = hid_lanes(p)
        hid_z[p].wait_recv()
        hid_fw.append(
            send(hidbuf.at[2 * toks : 3 * toks, lanes], hidbuf.at[3 * toks : 4 * toks, lanes], sib)
        )

    outs = (out_q, out_k, out_v)
    rs_copy = {}
    piece_copy = {}
    fwd_copy = {}
    sib_copy = {0: [], 1: [], 2: []}

    def x_rows(x):
        return pl.ds(pl.multiple_of(x * row_x, 16), row_x)

    def piece(w, p, y, x):
        start = pl.multiple_of(y * row_y + core * row_c + x * row_x, 16)
        return outs[w].at[pl.ds(start, row_x), slice(p * half, (p + 1) * half)]

    def to_sib(w, ref):
        sib_copy[w].append(send(ref, ref, sib))

    def dw_start(w):
        for copy in g_copy[w]:
            copy.wait_recv()
        for p in range(2):
            dwp[w, p] = dot_nn(gcat[w], hidbuf[:, p * half : (p + 1) * half]).astype(BF16)
            rs_copy[w, p] = send(dwp.at[w, p, x_rows(1 - xi)], rsum.at[w, p], xn)

    def dw_final(w):
        for p in range(2):
            rs_copy[w, p].wait_recv()
            done = dwp[w, p, x_rows(xi), :].astype(F32) + rsum[w, p].astype(F32)
            ref = piece(w, p, iv, xi)
            ref[...] = done.astype(BF16)
            cx = send(ref, ref, xn)
            cy = send(ref, ref, yn)
            piece_copy[w, p] = (cx, cy)
            to_sib(w, ref)

    def dw_forward(w):
        for p in range(2):
            cx, cy = piece_copy[w, p]
            cx_ref = piece(w, p, iv, 1 - xi)
            cy_ref = piece(w, p, 1 - iv, xi)
            first, ref, dev = ((cx, cx_ref, yn), (cy, cy_ref, xn))[p]
            first.wait_recv()
            fwd_copy[w, p] = send(ref, ref, dev)
            to_sib(w, ref)
        for p in range(2):
            cx, cy = piece_copy[w, p]
            if p == 0:
                cy.wait_recv()
                to_sib(w, piece(w, p, 1 - iv, xi))
            else:
                cx.wait_recv()
                to_sib(w, piece(w, p, iv, 1 - xi))

    def dw_last(w):
        for p in range(2):
            fwd_copy[w, p].wait_recv()
            to_sib(w, piece(w, p, 1 - iv, 1 - xi))

    def dw_out(w):
        for copy in sib_copy[w]:
            copy.wait_recv()

    kv_own(1, ctx_t, pb, 1.0)
    kv_final(1, 2, v_b, v_c)
    kv_own(0, q_t, dsb, scale)
    hid_sib.wait_recv()
    hid_fw[0].wait_recv()
    hid_fw[1].wait_recv()
    dw_start(0)
    kv_final(0, 1, k_b, k_c)
    dw_start(2)
    dw_final(0)
    dw_start(1)
    for slot in (1, 2):
        grads[slot] = jnp.transpose(grads_t[slot].astype(F32)).astype(BF16)
    dw_final(2)

    cols = width // n_head
    z_copy = []

    def input_block(d):
        owner = lax.rem(hd + d, n_head) if d > 0 else hd
        lanes = pl.ds(pl.multiple_of(owner * cols, 128), cols)
        acc = dot_nn(grads[0], wq[:, lanes]) + dot_nn(grads[1], wk[:, lanes])
        acc = acc + dot_nn(grads[2], wv[:, lanes])
        return acc + dot_nt(grad_feat, wj[lanes, :])

    def input_send(d):
        zsend[d - 1] = input_block(d).astype(BF16)
        z_copy.append((d, send(zsend.at[d - 1], zrecv.at[d - 1], zpeers[d - 1])))

    input_send(2)
    dw_final(1)
    input_send(1)
    dw_forward(0)
    input_send(3)
    dw_forward(2)
    zown[...] = input_block(0)
    dw_forward(1)
    dw_last(0)
    dw_last(2)
    dw_out(0)
    dw_last(1)
    for d, copy in z_copy:
        copy.wait_recv()
    total = zown[...]
    for d in range(n_head - 1):
        total = total + zrecv[d].astype(F32)
    out_in[...] = total.astype(BF16)
    dw_out(2)
    dw_out(1)
    for copy in started:
        copy.wait_send()
    assert counter[0] <= n_copies


def write_kernel(n, *refs):
    sems = refs[2 * n]
    copies = [pltpu.make_async_copy(refs[i], refs[n + i], sems.at[i]) for i in range(n)]
    for copy in copies:
        copy.start()
    for copy in copies:
        copy.wait()


def fused_device(
    n_head,
    hidden_in,
    ctx_grad,
    w_query,
    w_key,
    w_value,
    w_junction,
    donor_pos,
    acceptor_pos,
    junction_counts,
    pred_grad,
):
    toks, width = hidden_in.shape[1:]
    feats = w_query.shape[0]
    heads = feats // HD
    n_seq = 4
    n_slots = n_seq * donor_pos.shape[2] * donor_pos.shape[3]
    n_copies = 96
    vmem = pl.BlockSpec(memory_space=pltpu.VMEM)
    hbm = pl.BlockSpec(memory_space=pl.ANY)
    half = width // 2
    cols = width // n_head
    scratch = [
        pltpu.VMEM((4 * toks, width), BF16),
        pltpu.VMEM((toks, feats), BF16),
        pltpu.VMEM((feats, width), BF16),
        pltpu.VMEM((feats, width), BF16),
        pltpu.VMEM((feats, width), BF16),
        pltpu.VMEM((width, PJ), BF16),
        pltpu.VMEM((4, toks, feats), BF16),
        pltpu.VMEM((4, toks, feats), BF16),
        pltpu.VMEM((4, toks, PJ), BF16),
        pltpu.VMEM((4, 8, n_slots), F32),
        pltpu.VMEM((heads, toks, HD), BF16),
        pltpu.VMEM((heads, toks, HD), BF16),
        pltpu.VMEM((feats, toks), BF16),
        pltpu.VMEM((feats, toks), BF16),
        pltpu.VMEM((heads, toks, 4 * toks), F32),
        pltpu.VMEM((heads, toks, 4 * toks), F32),
        pltpu.VMEM((heads, toks, 4 * toks), BF16),
        pltpu.VMEM((heads, toks, 4 * toks), BF16),
        pltpu.VMEM((2, 2, feats, toks), BF16),
        pltpu.VMEM((2, 2, feats, toks), BF16),
        pltpu.VMEM((2, feats, toks), BF16),
        pltpu.VMEM((2, feats, toks), BF16),
        pltpu.VMEM((2, feats, toks), F32),
        pltpu.VMEM((3, toks, feats), BF16),
        pltpu.VMEM((3, feats, toks), BF16),
        pltpu.VMEM((3, feats // 4, 4 * toks), BF16),
        pltpu.VMEM((3, 2, feats // 4, half), BF16),
        pltpu.VMEM((3, 2, feats // 8, half), BF16),
        pltpu.VMEM((n_head - 1, toks, cols), BF16),
        pltpu.VMEM((n_head - 1, toks, cols), BF16),
        pltpu.VMEM((toks, cols), F32),
        pltpu.SemaphoreType.DMA((n_copies,)),
        pltpu.SemaphoreType.DMA((n_copies,)),
        pltpu.SemaphoreType.DMA((6,)),
    ]
    grad_w = jax.ShapeDtypeStruct((feats, width), BF16)
    shapes = (grad_w, grad_w, grad_w, jax.ShapeDtypeStruct((toks, cols), BF16))
    results = pl.pallas_call(
        functools.partial(fused_kernel, n_head, n_copies),
        out_shape=tuple(pltpu.VMEM(s.shape, s.dtype) for s in shapes),
        in_specs=[hbm] * 6 + [vmem] * 4,
        out_specs=(vmem,) * 4,
        scratch_shapes=scratch,
        compiler_params=pltpu.CompilerParams(
            collective_id=0, has_side_effects=True, vmem_limit_bytes=59 * 1024 * 1024
        ),
        name="attention_backward",
    )(
        hidden_in,
        ctx_grad,
        w_query,
        w_key,
        w_value,
        w_junction,
        donor_pos,
        acceptor_pos,
        junction_counts,
        pred_grad,
    )
    out_q, out_k, out_v, out_in = pl.pallas_call(
        functools.partial(write_kernel, 4),
        out_shape=shapes,
        in_specs=[vmem] * 4,
        out_specs=(hbm,) * 4,
        scratch_shapes=[pltpu.SemaphoreType.DMA((4,))],
        compiler_params=pltpu.CompilerParams(vmem_limit_bytes=16 * 1024 * 1024),
        name="write_results",
    )(*results)
    return out_in[None], out_q, out_k, out_v


def on_device(
    hidden_in,
    ctx_grad,
    w_query,
    w_key,
    w_value,
    w_junction,
    donor_pos,
    acceptor_pos,
    junction_counts,
    pred_grad,
):
    hidden = hidden_in[0]
    local_len = hidden.shape[0]
    shard_count = lax.axis_size("seq")
    total_len = local_len * shard_count
    heads_dev = w_query.shape[0] // HD
    softmax_scale = HD ** (-0.5)
    pair_scale = PJ ** (-0.5)
    queries = jnp.einsum("td,cd->tc", hidden, w_query, preferred_element_type=jnp.float32).astype(
        jnp.bfloat16
    )
    key_rows = jnp.einsum("td,cd->tc", hidden, w_key, preferred_element_type=jnp.float32).astype(
        jnp.bfloat16
    )
    value_rows = jnp.einsum(
        "td,cd->tc", hidden, w_value, preferred_element_type=jnp.float32
    ).astype(jnp.bfloat16)
    features = jnp.dot(hidden, w_junction, preferred_element_type=jnp.float32).astype(jnp.bfloat16)
    all_keys, all_values, all_features = (
        lax.all_gather(key_rows, "seq", axis=0, tiled=True),
        lax.all_gather(value_rows, "seq", axis=0, tiled=True),
        lax.all_gather(features, "seq", axis=0, tiled=True),
    )
    query_heads = queries.reshape(local_len, heads_dev, HD)
    grad_heads = ctx_grad[0].reshape(local_len, heads_dev, HD)
    key_heads = all_keys.reshape(total_len, heads_dev, HD)
    value_heads = all_values.reshape(total_len, heads_dev, HD)
    scores = (
        jnp.einsum("qhd,khd->hqk", query_heads, key_heads, preferred_element_type=jnp.float32)
        * softmax_scale
    )
    row_max = jnp.max(scores, axis=-1, keepdims=True)
    expd = jnp.exp(scores - row_max)
    probs = expd / jnp.sum(expd, axis=-1, keepdims=True)
    dprobs = jnp.einsum("qhd,khd->hqk", grad_heads, value_heads, preferred_element_type=jnp.float32)
    row_delta = jnp.sum(probs * dprobs, axis=-1, keepdims=True)
    dscores = probs * (dprobs - row_delta)
    probs_b = probs.astype(jnp.bfloat16)
    dscores_b = dscores.astype(jnp.bfloat16)
    query_grad = (
        (
            jnp.einsum("hqk,khd->qhd", dscores_b, key_heads, preferred_element_type=jnp.float32)
            * softmax_scale
        )
        .astype(jnp.bfloat16)
        .reshape(local_len, heads_dev * HD)
    )
    key_term = (
        jnp.einsum("hqk,qhd->khd", dscores_b, query_heads, preferred_element_type=jnp.float32)
        * softmax_scale
    ).reshape(total_len, heads_dev * HD)
    value_term = jnp.einsum(
        "hqk,qhd->khd", probs_b, grad_heads, preferred_element_type=jnp.float32
    ).reshape(total_len, heads_dev * HD)
    key_sum, value_sum = (
        lax.psum_scatter(
            key_term.astype(jnp.bfloat16), "seq", scatter_dimension=0, tiled=True
        ).astype(jnp.float32),
        lax.psum_scatter(
            value_term.astype(jnp.bfloat16), "seq", scatter_dimension=0, tiled=True
        ).astype(jnp.float32),
    )
    key_grad = key_sum.astype(jnp.bfloat16)
    value_grad = value_sum.astype(jnp.bfloat16)
    donor_idx = donor_pos[0, 0]
    accept_idx = acceptor_pos[0, 0]
    slot_dev = donor_idx.shape[1]
    slot_ids = lax.axis_index("head") * slot_dev + jnp.arange(slot_dev, dtype=jnp.int32)
    live_slots = slot_ids[None, :] < junction_counts[0, 0][:, None]
    donor_feat = features[donor_idx].astype(jnp.float32)
    accept_glob = jnp.arange(shard_count, dtype=jnp.int32)[:, None] * local_len + accept_idx
    accept_rows = all_features[accept_glob]
    accept_feat = accept_rows.astype(jnp.float32)
    pair_score = jnp.sum(donor_feat * accept_feat, axis=-1) * pair_scale
    slot_grad = (
        jnp.where(live_slots, pred_grad[0, 0] * jax.nn.sigmoid(pair_score), 0.0) * pair_scale
    )
    donor_term = slot_grad[..., None] * accept_feat
    accept_term = slot_grad[..., None] * donor_feat
    pair_width = features.shape[1]
    grad_feat = (
        jnp.zeros((local_len, pair_width), jnp.float32)
        .at[donor_idx.reshape(-1)]
        .add(donor_term.reshape(-1, pair_width))
    )
    spread_term = (
        jnp.zeros((total_len, pair_width), jnp.float32)
        .at[accept_glob.reshape(-1)]
        .add(accept_term.reshape(-1, pair_width))
    )
    grad_feat = grad_feat + lax.psum_scatter(
        spread_term.astype(jnp.bfloat16), "seq", scatter_dimension=0, tiled=True
    ).astype(jnp.float32)
    grad_feat_b = grad_feat.astype(jnp.bfloat16)
    input_term = jnp.einsum("tc,cd->td", query_grad, w_query, preferred_element_type=jnp.float32)
    input_term = input_term + jnp.einsum(
        "tc,cd->td", key_grad, w_key, preferred_element_type=jnp.float32
    )
    input_term = input_term + jnp.einsum(
        "tc,cd->td", value_grad, w_value, preferred_element_type=jnp.float32
    )
    input_term = input_term + jnp.einsum(
        "tp,dp->td", grad_feat_b, w_junction, preferred_element_type=jnp.float32
    )
    grad_input = lax.psum_scatter(
        input_term.astype(jnp.bfloat16), "head", scatter_dimension=1, tiled=True
    )
    key_wterm = jnp.einsum("tc,td->cd", key_grad, hidden, preferred_element_type=jnp.float32)
    value_wterm = jnp.einsum("tc,td->cd", value_grad, hidden, preferred_element_type=jnp.float32)
    query_wterm = jnp.einsum("tc,td->cd", query_grad, hidden, preferred_element_type=jnp.float32)
    query_wsum, key_wsum, value_wsum = lax.psum(
        (query_wterm, key_wterm, value_wterm), ("interval", "seq")
    )
    return (
        grad_input[None],
        query_wsum.astype(jnp.bfloat16),
        key_wsum.astype(jnp.bfloat16),
        value_wsum.astype(jnp.bfloat16),
    )


def solution(mesh):
    placed = (
        P("interval", "seq", None),
        P("interval", "seq", "head"),
        P("head", None),
        P("head", None),
        P("head", None),
        P(),
        P("interval", "seq", None, "head"),
        P("interval", "seq", None, "head"),
        P("interval", "seq", None),
        P("interval", "seq", None, "head"),
    )
    shape = dict(mesh.shape)
    fits = shape["interval"] == 2 and shape["seq"] == 4 and shape["head"] == 4
    run = functools.partial(fused_device, shape["head"]) if fits else on_device
    return jax.shard_map(
        run,
        mesh=mesh,
        in_specs=placed,
        out_specs=(P("interval", "seq", "head"), P("head", None), P("head", None), P("head", None)),
        check_vma=False,
    )
```

```python
import functools

import jax
import jax.numpy as jnp
from jax import lax
from jax.experimental import pallas as pl
from jax.experimental.pallas import tpu as pltpu
from jax.sharding import PartitionSpec as P

HD = 192
PJ = 128
MESH = pl.DeviceIdType.MESH
F32 = jnp.float32
BF16 = jnp.bfloat16


def dot_nn(a, b):
    return lax.dot_general(a, b, (((1,), (0,)), ((), ())), preferred_element_type=F32)


def dot_nt(a, b):
    return lax.dot_general(a, b, (((1,), (1,)), ((), ())), preferred_element_type=F32)


def dot_tn(a, b):
    return lax.dot_general(a, b, (((0,), (0,)), ((), ())), preferred_element_type=F32)


def fused_kernel(
    n_head,
    n_copies,
    hid_hbm,
    ctx_hbm,
    wq_hbm,
    wk_hbm,
    wv_hbm,
    wj_hbm,
    donor,
    accept,
    counts,
    pred,
    out_q,
    out_k,
    out_v,
    out_in,
    hidbuf,
    ctx,
    wq,
    wk,
    wv,
    wj,
    kbuf,
    vbuf,
    fbuf,
    slotbuf,
    qbuf,
    ctx_h,
    q_t,
    ctx_t,
    sref,
    dpref,
    pb,
    dsb,
    term,
    from_sib,
    pair_sum,
    from_xn,
    own_term,
    grads,
    grads_t,
    gcat,
    dwp,
    rsum,
    zsend,
    zrecv,
    zown,
    send_sems,
    recv_sems,
    load_sems,
):
    toks = ctx.shape[0]
    width = hidbuf.shape[1]
    feats = wq.shape[0]
    heads = feats // HD
    half = width // 2
    row_y = feats // 2
    row_c = feats // 4
    row_x = feats // 8
    scale = HD**-0.5
    iv = lax.axis_index("interval")
    sq = lax.axis_index("seq")
    hd = lax.axis_index("head")
    xi = lax.div(sq, 2)
    core = lax.rem(sq, 2)
    s_sib = sq + 1 - 2 * core
    s_xn = lax.rem(sq + 2, 4)
    s_dg = lax.rem(s_sib + 2, 4)
    sib = (iv, s_sib, hd)
    xn = (iv, s_xn, hd)
    yn = (1 - iv, sq, hd)
    ysib = (1 - iv, s_sib, hd)
    zpeers = [(iv, sq, lax.rem(hd + d, n_head)) for d in range(1, n_head)]
    zpair = (iv, sq, hd + 1 - 2 * lax.rem(hd, 2))
    split = toks // 2
    mine_z = lax.rem(hd, 2) * split
    hid = hidbuf.at[0:toks]

    def z_rows(base):
        return pl.ds(pl.multiple_of(base + mine_z, 16), split)


    loads = []
    for i, (src, dst) in enumerate(
        (
            (hid_hbm.at[0], hid),
            (wj_hbm, wj),
            (wk_hbm, wk),
            (wv_hbm, wv),
            (wq_hbm, wq),
            (ctx_hbm.at[0], ctx),
        )
    ):
        load = pltpu.make_async_copy(src, dst, load_sems.at[i])
        load.start()
        loads.append(load)

    counter = [0]
    started = []

    def send(src, dst, dev):
        i = counter[0]
        counter[0] += 1
        copy = pltpu.make_async_remote_copy(
            src_ref=src,
            dst_ref=dst,
            send_sem=send_sems.at[i],
            recv_sem=recv_sems.at[i],
            device_id=dev,
            device_id_type=MESH,
        )
        copy.start()
        started.append(copy)
        return copy

    barrier = pltpu.get_barrier_semaphore()
    peers = [sib, xn, yn, ysib] + zpeers
    for dev in peers:
        pl.semaphore_signal(barrier, inc=1, device_id=dev, device_id_type=MESH)

    loads[0].wait()
    loads[1].wait()
    fbuf[0] = dot_nn(hid[...], wj[...]).astype(BF16)
    loads[2].wait()
    kbuf[0] = dot_nt(hid[...], wk[...]).astype(BF16)
    pl.semaphore_wait(barrier, len(peers))
    f_xn = send(fbuf.at[0, z_rows(0)], fbuf.at[2, z_rows(0)], xn)
    f_sib = send(fbuf.at[0], fbuf.at[1], sib)
    k_xn = send(kbuf.at[0], kbuf.at[2], xn)
    k_sib = send(kbuf.at[0], kbuf.at[1], sib)
    hid_yn = []
    for p in range(2):
        lanes = slice(p * half, (p + 1) * half)
        hid_yn.append(
            send(hidbuf.at[z_rows(0), lanes], hidbuf.at[z_rows(2 * toks), lanes], yn)
        )
    n_acc, slot_dev = donor.shape[2], donor.shape[3]
    n_slots = slotbuf.shape[2]
    acc_iota = lax.broadcasted_iota(jnp.int32, (n_acc, slot_dev), 0)
    slot_ids = lax.broadcasted_iota(jnp.int32, (n_acc, slot_dev), 1) + hd * slot_dev
    live_count = jnp.zeros((n_acc, slot_dev), jnp.int32)
    for j in range(n_acc):
        live_count = jnp.where(acc_iota == j, counts[0, :, j : j + 1], live_count)
    donor_tok = (donor[0, 0] + sq * toks).astype(F32)
    accept_tok = (accept[0, 0] + acc_iota * toks).astype(F32)
    pred_live = jnp.where(slot_ids < live_count, pred[0, 0], 0.0)
    lane_iota = lax.broadcasted_iota(jnp.int32, (n_acc, n_slots), 1)
    row_iota = lax.broadcasted_iota(jnp.int32, (n_acc, n_slots), 0)
    place = lane_iota - (sq * n_acc + row_iota) * slot_dev
    slotbuf[0] = jnp.zeros(slotbuf.shape[1:], F32)
    for i, values in enumerate((donor_tok, accept_tok, pred_live)):
        spread = jnp.zeros((n_acc, n_slots), F32)
        for j in range(slot_dev):
            spread = jnp.where(place == j, values[:, j : j + 1], spread)
        slotbuf[0, i : i + 1, :] = jnp.sum(spread, axis=0, keepdims=True)
    t_xn = send(slotbuf.at[0], slotbuf.at[2], xn)
    t_sib = send(slotbuf.at[0], slotbuf.at[1], sib)
    loads[3].wait()
    vbuf[0] = dot_nt(hid[...], wv[...]).astype(BF16)
    v_xn = send(vbuf.at[0], vbuf.at[2], xn)
    v_sib = send(vbuf.at[0], vbuf.at[1], sib)
    loads[4].wait()
    q_full = dot_nt(hid[...], wq[...])
    for h in range(heads):
        qbuf[h] = q_full[:, h * HD : (h + 1) * HD].astype(BF16)
    q_t[...] = jnp.transpose(q_full).astype(BF16)

    def head_cols(h):
        return slice(h * HD, (h + 1) * HD)

    def block_cols(r):
        return slice(r * toks, (r + 1) * toks)

    def scores(r):
        for h in range(heads):
            sref[h, :, block_cols(r)] = dot_nt(qbuf[h], kbuf[r, :, head_cols(h)])

    def dprobs(r):
        for h in range(heads):
            dpref[h, :, block_cols(r)] = dot_nt(ctx_h[h], vbuf[r, :, head_cols(h)])

    def pass_on(arrived, ref):
        arrived.wait_recv()
        return send(ref, ref, zpair)

    def hid_lanes(p):
        return slice(p * half, (p + 1) * half)

    f_z = pass_on(f_xn, fbuf.at[2, z_rows(0)])
    t_xn.wait_recv()
    t_fw = send(slotbuf.at[2], slotbuf.at[3], sib)
    scores(0)
    loads[5].wait()
    ctx_t[...] = jnp.transpose(ctx[...].astype(F32)).astype(BF16)
    for h in range(heads):
        ctx_h[h] = ctx[:, head_cols(h)]
    dprobs(0)
    f_z.wait_recv()
    f_fw = send(fbuf.at[2], fbuf.at[3], sib)
    k_sib.wait_recv()
    scores(1)
    f_sib.wait_recv()
    t_sib.wait_recv()
    f_fw.wait_recv()
    t_fw.wait_recv()
    rows_all = slotbuf[0] + slotbuf[1] + slotbuf[2] + slotbuf[3]
    donor_row = rows_all[0:1, :]
    accept_row = rows_all[1:2, :]
    pred_row = rows_all[2:3, :]
    tok_iota = lax.broadcasted_iota(jnp.int32, (toks, n_slots), 0)
    own_donor = None
    own_accept = None
    donor_t = jnp.zeros((PJ, n_slots), F32)
    accept_t = jnp.zeros((PJ, n_slots), F32)
    for r, shard in enumerate((sq, s_sib, s_xn, s_dg)):
        tok = (tok_iota + shard * toks).astype(F32)
        hot_d = jnp.where(tok == donor_row, 1.0, 0.0).astype(BF16)
        hot_a = jnp.where(tok == accept_row, 1.0, 0.0).astype(BF16)
        if r == 0:
            own_donor, own_accept = hot_d, hot_a
        donor_t = donor_t + dot_tn(fbuf[r], hot_d)
        accept_t = accept_t + dot_tn(fbuf[r], hot_a)
    pair_scale = PJ**-0.5
    pair = jnp.sum(donor_t * accept_t, axis=0, keepdims=True) * pair_scale
    slot_grad = pred_row * (1.0 / (1.0 + jnp.exp(-pair))) * pair_scale
    grad_feat = dot_nt(own_donor, (slot_grad * accept_t).astype(BF16)) + dot_nt(
        own_accept, (slot_grad * donor_t).astype(BF16)
    )
    grad_feat = grad_feat.astype(BF16)

    k_xn.wait_recv()
    k_fw = send(kbuf.at[2], kbuf.at[3], sib)
    scores(2)
    k_fw.wait_recv()
    scores(3)

    rows_step = 16

    @pl.loop(0, toks // rows_step)
    def _(i):
        rows = pl.ds(pl.multiple_of(i * rows_step, rows_step), rows_step)
        raws = [sref[h, rows, :] * scale for h in range(heads)]
        tops = [jnp.max(raw, axis=-1, keepdims=True) for raw in raws]
        es = [jnp.exp(raw - top) for raw, top in zip(raws, tops)]
        sums = [jnp.sum(e, axis=-1, keepdims=True) for e in es]
        ps = [e * (1.0 / total) for e, total in zip(es, sums)]
        for h in range(heads):
            sref[h, rows, :] = ps[h]
            pb[h, rows, :] = ps[h].astype(BF16)

    def kv_terms(which, left_t, right, factor):
        def one(h, r):
            part = dot_nn(left_t[head_cols(h), :], right[h, :, block_cols(r)])
            return part * factor if factor != 1.0 else part

        for h in range(heads):
            term[which, 0, head_cols(h), :] = one(h, 3).astype(BF16)
        a = send(term.at[which, 0], from_sib.at[which, 0], sib)
        for h in range(heads):
            term[which, 1, head_cols(h), :] = one(h, 1).astype(BF16)
        b = send(term.at[which, 1], from_sib.at[which, 1], sib)
        for h in range(heads):
            own_term[which, head_cols(h), :] = one(h, 2)
        return a, b

    def kv_cross(which, a):
        a.wait_recv()
        pair_sum[which] = (own_term[which] + from_sib[which, 0].astype(F32)).astype(BF16)
        return send(pair_sum.at[which], from_xn.at[which], xn)

    def kv_own(which, left_t, right, factor):
        for h in range(heads):
            part = dot_nn(left_t[head_cols(h), :], right[h, :, block_cols(0)])
            own_term[which, head_cols(h), :] = part * factor if factor != 1.0 else part

    def g_rows(y, c):
        return pl.ds(pl.multiple_of(y * row_y + c * row_c, 16), row_c)

    g_copy = [None] * 3

    def exchange(slot):
        gcat[slot, :, 0:toks] = grads_t[slot, g_rows(iv, core), :]
        copies = []
        for b, dev, y, c in ((2, yn, 1 - iv, core), (3, ysib, 1 - iv, 1 - core), (1, sib, iv, 1 - core)):
            copies.append(
                send(grads_t.at[slot, g_rows(y, c)], gcat.at[slot, :, block_cols(b)], dev)
            )
        g_copy[slot] = copies

    def kv_final(which, slot, b, c):
        b.wait_recv()
        c.wait_recv()
        total = own_term[which] + from_sib[which, 1].astype(F32) + from_xn[which].astype(F32)
        grads_t[slot] = total.astype(BF16)
        exchange(slot)

    hid_z = [pass_on(hid_yn[0], hidbuf.at[z_rows(2 * toks), hid_lanes(0)])]
    v_a, v_b = kv_terms(1, ctx_t, pb, 1.0)
    v_sib.wait_recv()
    dprobs(1)
    v_c = kv_cross(1, v_a)
    v_xn.wait_recv()
    v_fw = send(vbuf.at[2], vbuf.at[3], sib)
    hid_sib = send(hidbuf.at[0:toks], hidbuf.at[toks : 2 * toks], sib)
    hid_z.append(pass_on(hid_yn[1], hidbuf.at[z_rows(2 * toks), hid_lanes(1)]))
    dprobs(2)
    v_fw.wait_recv()
    dprobs(3)

    @pl.loop(0, toks // rows_step)
    def _(i):
        rows = pl.ds(pl.multiple_of(i * rows_step, rows_step), rows_step)
        ps = [sref[h, rows, :] for h in range(heads)]
        dps = [dpref[h, rows, :] for h in range(heads)]
        deltas = [jnp.sum(p * dp, axis=-1, keepdims=True) for p, dp in zip(ps, dps)]
        for h in range(heads):
            dsb[h, rows, :] = (ps[h] * (dps[h] - deltas[h])).astype(BF16)

    k_a, k_b = kv_terms(0, q_t, dsb, scale)

    q_parts = []
    for h in range(heads):
        acc = dot_nn(dsb[h, :, block_cols(0)], kbuf[0, :, head_cols(h)])
        for r in range(1, 4):
            acc = acc + dot_nn(dsb[h, :, block_cols(r)], kbuf[r, :, head_cols(h)])
        q_parts.append(acc * scale)
    k_c = kv_cross(0, k_a)
    q_grad = jnp.concatenate(q_parts, axis=-1)
    grads_t[0] = jnp.transpose(q_grad).astype(BF16)
    exchange(0)
    grads[0] = q_grad.astype(BF16)

    hid_fw = []
    for p in range(2):
        lanes = hid_lanes(p)
        hid_z[p].wait_recv()
        hid_fw.append(
            send(hidbuf.at[2 * toks : 3 * toks, lanes], hidbuf.at[3 * toks : 4 * toks, lanes], sib)
        )

    outs = (out_q, out_k, out_v)
    rs_copy = {}
    piece_copy = {}
    fwd_copy = {}
    sib_copy = {0: [], 1: [], 2: []}

    def x_rows(x):
        return pl.ds(pl.multiple_of(x * row_x, 16), row_x)

    def piece(w, p, y, x):
        start = pl.multiple_of(y * row_y + core * row_c + x * row_x, 16)
        return outs[w].at[pl.ds(start, row_x), slice(p * half, (p + 1) * half)]

    def to_sib(w, ref):
        sib_copy[w].append(send(ref, ref, sib))

    def dw_start(w):
        for copy in g_copy[w]:
            copy.wait_recv()
        for p in range(2):
            dwp[w, p] = dot_nn(gcat[w], hidbuf[:, p * half : (p + 1) * half]).astype(BF16)
            rs_copy[w, p] = send(dwp.at[w, p, x_rows(1 - xi)], rsum.at[w, p], xn)

    def dw_final(w):
        for p in range(2):
            rs_copy[w, p].wait_recv()
            done = dwp[w, p, x_rows(xi), :].astype(F32) + rsum[w, p].astype(F32)
            ref = piece(w, p, iv, xi)
            ref[...] = done.astype(BF16)
            cx = send(ref, ref, xn)
            cy = send(ref, ref, yn)
            piece_copy[w, p] = (cx, cy)
            to_sib(w, ref)

    def dw_forward(w):
        for p in range(2):
            cx, cy = piece_copy[w, p]
            cx_ref = piece(w, p, iv, 1 - xi)
            cy_ref = piece(w, p, 1 - iv, xi)
            first, ref, dev = ((cx, cx_ref, yn), (cy, cy_ref, xn))[p]
            first.wait_recv()
            fwd_copy[w, p] = send(ref, ref, dev)
            to_sib(w, ref)
        for p in range(2):
            cx, cy = piece_copy[w, p]
            if p == 0:
                cy.wait_recv()
                to_sib(w, piece(w, p, 1 - iv, xi))
            else:
                cx.wait_recv()
                to_sib(w, piece(w, p, iv, 1 - xi))

    def dw_last(w):
        for p in range(2):
            fwd_copy[w, p].wait_recv()
            to_sib(w, piece(w, p, 1 - iv, 1 - xi))

    def dw_out(w):
        for copy in sib_copy[w]:
            copy.wait_recv()

    kv_own(1, ctx_t, pb, 1.0)
    kv_final(1, 2, v_b, v_c)
    kv_own(0, q_t, dsb, scale)
    hid_sib.wait_recv()
    hid_fw[0].wait_recv()
    hid_fw[1].wait_recv()
    dw_start(0)
    kv_final(0, 1, k_b, k_c)
    dw_start(2)
    dw_final(0)
    dw_start(1)
    for slot in (1, 2):
        grads[slot] = jnp.transpose(grads_t[slot].astype(F32)).astype(BF16)
    dw_final(2)

    cols = width // n_head
    z_copy = []

    def input_block(d):
        owner = lax.rem(hd + d, n_head) if d > 0 else hd
        lanes = pl.ds(pl.multiple_of(owner * cols, 128), cols)
        acc = dot_nn(grads[0], wq[:, lanes]) + dot_nn(grads[1], wk[:, lanes])
        acc = acc + dot_nn(grads[2], wv[:, lanes])
        return acc + dot_nt(grad_feat, wj[lanes, :])

    def input_send(d):
        zsend[d - 1] = input_block(d).astype(BF16)
        z_copy.append((d, send(zsend.at[d - 1], zrecv.at[d - 1], zpeers[d - 1])))

    input_send(2)
    dw_forward(0)
    dw_final(1)
    input_send(1)
    dw_forward(2)
    input_send(3)
    dw_last(0)
    dw_forward(1)
    zown[...] = input_block(0)
    dw_last(2)
    dw_out(0)
    dw_last(1)
    for d, copy in z_copy:
        copy.wait_recv()
    total = zown[...]
    for d in range(n_head - 1):
        total = total + zrecv[d].astype(F32)
    out_in[...] = total.astype(BF16)
    dw_out(2)
    dw_out(1)
    for copy in started:
        copy.wait_send()
    assert counter[0] <= n_copies


def write_kernel(n, *refs):
    sems = refs[2 * n]
    copies = [pltpu.make_async_copy(refs[i], refs[n + i], sems.at[i]) for i in range(n)]
    for copy in copies:
        copy.start()
    for copy in copies:
        copy.wait()


def fused_device(
    n_head,
    hidden_in,
    ctx_grad,
    w_query,
    w_key,
    w_value,
    w_junction,
    donor_pos,
    acceptor_pos,
    junction_counts,
    pred_grad,
):
    toks, width = hidden_in.shape[1:]
    feats = w_query.shape[0]
    heads = feats // HD
    n_seq = 4
    n_slots = n_seq * donor_pos.shape[2] * donor_pos.shape[3]
    n_copies = 96
    vmem = pl.BlockSpec(memory_space=pltpu.VMEM)
    hbm = pl.BlockSpec(memory_space=pl.ANY)
    half = width // 2
    cols = width // n_head
    scratch = [
        pltpu.VMEM((4 * toks, width), BF16),
        pltpu.VMEM((toks, feats), BF16),
        pltpu.VMEM((feats, width), BF16),
        pltpu.VMEM((feats, width), BF16),
        pltpu.VMEM((feats, width), BF16),
        pltpu.VMEM((width, PJ), BF16),
        pltpu.VMEM((4, toks, feats), BF16),
        pltpu.VMEM((4, toks, feats), BF16),
        pltpu.VMEM((4, toks, PJ), BF16),
        pltpu.VMEM((4, 8, n_slots), F32),
        pltpu.VMEM((heads, toks, HD), BF16),
        pltpu.VMEM((heads, toks, HD), BF16),
        pltpu.VMEM((feats, toks), BF16),
        pltpu.VMEM((feats, toks), BF16),
        pltpu.VMEM((heads, toks, 4 * toks), F32),
        pltpu.VMEM((heads, toks, 4 * toks), F32),
        pltpu.VMEM((heads, toks, 4 * toks), BF16),
        pltpu.VMEM((heads, toks, 4 * toks), BF16),
        pltpu.VMEM((2, 2, feats, toks), BF16),
        pltpu.VMEM((2, 2, feats, toks), BF16),
        pltpu.VMEM((2, feats, toks), BF16),
        pltpu.VMEM((2, feats, toks), BF16),
        pltpu.VMEM((2, feats, toks), F32),
        pltpu.VMEM((3, toks, feats), BF16),
        pltpu.VMEM((3, feats, toks), BF16),
        pltpu.VMEM((3, feats // 4, 4 * toks), BF16),
        pltpu.VMEM((3, 2, feats // 4, half), BF16),
        pltpu.VMEM((3, 2, feats // 8, half), BF16),
        pltpu.VMEM((n_head - 1, toks, cols), BF16),
        pltpu.VMEM((n_head - 1, toks, cols), BF16),
        pltpu.VMEM((toks, cols), F32),
        pltpu.SemaphoreType.DMA((n_copies,)),
        pltpu.SemaphoreType.DMA((n_copies,)),
        pltpu.SemaphoreType.DMA((6,)),
    ]
    grad_w = jax.ShapeDtypeStruct((feats, width), BF16)
    shapes = (grad_w, grad_w, grad_w, jax.ShapeDtypeStruct((toks, cols), BF16))
    results = pl.pallas_call(
        functools.partial(fused_kernel, n_head, n_copies),
        out_shape=tuple(pltpu.VMEM(s.shape, s.dtype) for s in shapes),
        in_specs=[hbm] * 6 + [vmem] * 4,
        out_specs=(vmem,) * 4,
        scratch_shapes=scratch,
        compiler_params=pltpu.CompilerParams(
            collective_id=0, has_side_effects=True, vmem_limit_bytes=59 * 1024 * 1024
        ),
        name="attention_backward",
    )(
        hidden_in,
        ctx_grad,
        w_query,
        w_key,
        w_value,
        w_junction,
        donor_pos,
        acceptor_pos,
        junction_counts,
        pred_grad,
    )
    out_q, out_k, out_v, out_in = pl.pallas_call(
        functools.partial(write_kernel, 4),
        out_shape=shapes,
        in_specs=[vmem] * 4,
        out_specs=(hbm,) * 4,
        scratch_shapes=[pltpu.SemaphoreType.DMA((4,))],
        compiler_params=pltpu.CompilerParams(vmem_limit_bytes=16 * 1024 * 1024),
        name="write_results",
    )(*results)
    return out_in[None], out_q, out_k, out_v


def on_device(
    hidden_in,
    ctx_grad,
    w_query,
    w_key,
    w_value,
    w_junction,
    donor_pos,
    acceptor_pos,
    junction_counts,
    pred_grad,
):
    hidden = hidden_in[0]
    local_len = hidden.shape[0]
    shard_count = lax.axis_size("seq")
    total_len = local_len * shard_count
    heads_dev = w_query.shape[0] // HD
    softmax_scale = HD ** (-0.5)
    pair_scale = PJ ** (-0.5)
    queries = jnp.einsum("td,cd->tc", hidden, w_query, preferred_element_type=jnp.float32).astype(
        jnp.bfloat16
    )
    key_rows = jnp.einsum("td,cd->tc", hidden, w_key, preferred_element_type=jnp.float32).astype(
        jnp.bfloat16
    )
    value_rows = jnp.einsum(
        "td,cd->tc", hidden, w_value, preferred_element_type=jnp.float32
    ).astype(jnp.bfloat16)
    features = jnp.dot(hidden, w_junction, preferred_element_type=jnp.float32).astype(jnp.bfloat16)
    all_keys, all_values, all_features = (
        lax.all_gather(key_rows, "seq", axis=0, tiled=True),
        lax.all_gather(value_rows, "seq", axis=0, tiled=True),
        lax.all_gather(features, "seq", axis=0, tiled=True),
    )
    query_heads = queries.reshape(local_len, heads_dev, HD)
    grad_heads = ctx_grad[0].reshape(local_len, heads_dev, HD)
    key_heads = all_keys.reshape(total_len, heads_dev, HD)
    value_heads = all_values.reshape(total_len, heads_dev, HD)
    scores = (
        jnp.einsum("qhd,khd->hqk", query_heads, key_heads, preferred_element_type=jnp.float32)
        * softmax_scale
    )
    row_max = jnp.max(scores, axis=-1, keepdims=True)
    expd = jnp.exp(scores - row_max)
    probs = expd / jnp.sum(expd, axis=-1, keepdims=True)
    dprobs = jnp.einsum("qhd,khd->hqk", grad_heads, value_heads, preferred_element_type=jnp.float32)
    row_delta = jnp.sum(probs * dprobs, axis=-1, keepdims=True)
    dscores = probs * (dprobs - row_delta)
    probs_b = probs.astype(jnp.bfloat16)
    dscores_b = dscores.astype(jnp.bfloat16)
    query_grad = (
        (
            jnp.einsum("hqk,khd->qhd", dscores_b, key_heads, preferred_element_type=jnp.float32)
            * softmax_scale
        )
        .astype(jnp.bfloat16)
        .reshape(local_len, heads_dev * HD)
    )
    key_term = (
        jnp.einsum("hqk,qhd->khd", dscores_b, query_heads, preferred_element_type=jnp.float32)
        * softmax_scale
    ).reshape(total_len, heads_dev * HD)
    value_term = jnp.einsum(
        "hqk,qhd->khd", probs_b, grad_heads, preferred_element_type=jnp.float32
    ).reshape(total_len, heads_dev * HD)
    key_sum, value_sum = (
        lax.psum_scatter(
            key_term.astype(jnp.bfloat16), "seq", scatter_dimension=0, tiled=True
        ).astype(jnp.float32),
        lax.psum_scatter(
            value_term.astype(jnp.bfloat16), "seq", scatter_dimension=0, tiled=True
        ).astype(jnp.float32),
    )
    key_grad = key_sum.astype(jnp.bfloat16)
    value_grad = value_sum.astype(jnp.bfloat16)
    donor_idx = donor_pos[0, 0]
    accept_idx = acceptor_pos[0, 0]
    slot_dev = donor_idx.shape[1]
    slot_ids = lax.axis_index("head") * slot_dev + jnp.arange(slot_dev, dtype=jnp.int32)
    live_slots = slot_ids[None, :] < junction_counts[0, 0][:, None]
    donor_feat = features[donor_idx].astype(jnp.float32)
    accept_glob = jnp.arange(shard_count, dtype=jnp.int32)[:, None] * local_len + accept_idx
    accept_rows = all_features[accept_glob]
    accept_feat = accept_rows.astype(jnp.float32)
    pair_score = jnp.sum(donor_feat * accept_feat, axis=-1) * pair_scale
    slot_grad = (
        jnp.where(live_slots, pred_grad[0, 0] * jax.nn.sigmoid(pair_score), 0.0) * pair_scale
    )
    donor_term = slot_grad[..., None] * accept_feat
    accept_term = slot_grad[..., None] * donor_feat
    pair_width = features.shape[1]
    grad_feat = (
        jnp.zeros((local_len, pair_width), jnp.float32)
        .at[donor_idx.reshape(-1)]
        .add(donor_term.reshape(-1, pair_width))
    )
    spread_term = (
        jnp.zeros((total_len, pair_width), jnp.float32)
        .at[accept_glob.reshape(-1)]
        .add(accept_term.reshape(-1, pair_width))
    )
    grad_feat = grad_feat + lax.psum_scatter(
        spread_term.astype(jnp.bfloat16), "seq", scatter_dimension=0, tiled=True
    ).astype(jnp.float32)
    grad_feat_b = grad_feat.astype(jnp.bfloat16)
    input_term = jnp.einsum("tc,cd->td", query_grad, w_query, preferred_element_type=jnp.float32)
    input_term = input_term + jnp.einsum(
        "tc,cd->td", key_grad, w_key, preferred_element_type=jnp.float32
    )
    input_term = input_term + jnp.einsum(
        "tc,cd->td", value_grad, w_value, preferred_element_type=jnp.float32
    )
    input_term = input_term + jnp.einsum(
        "tp,dp->td", grad_feat_b, w_junction, preferred_element_type=jnp.float32
    )
    grad_input = lax.psum_scatter(
        input_term.astype(jnp.bfloat16), "head", scatter_dimension=1, tiled=True
    )
    key_wterm = jnp.einsum("tc,td->cd", key_grad, hidden, preferred_element_type=jnp.float32)
    value_wterm = jnp.einsum("tc,td->cd", value_grad, hidden, preferred_element_type=jnp.float32)
    query_wterm = jnp.einsum("tc,td->cd", query_grad, hidden, preferred_element_type=jnp.float32)
    query_wsum, key_wsum, value_wsum = lax.psum(
        (query_wterm, key_wterm, value_wterm), ("interval", "seq")
    )
    return (
        grad_input[None],
        query_wsum.astype(jnp.bfloat16),
        key_wsum.astype(jnp.bfloat16),
        value_wsum.astype(jnp.bfloat16),
    )


def solution(mesh):
    placed = (
        P("interval", "seq", None),
        P("interval", "seq", "head"),
        P("head", None),
        P("head", None),
        P("head", None),
        P(),
        P("interval", "seq", None, "head"),
        P("interval", "seq", None, "head"),
        P("interval", "seq", None),
        P("interval", "seq", None, "head"),
    )
    shape = dict(mesh.shape)
    fits = shape["interval"] == 2 and shape["seq"] == 4 and shape["head"] == 4
    run = functools.partial(fused_device, shape["head"]) if fits else on_device
    return jax.shard_map(
        run,
        mesh=mesh,
        in_specs=placed,
        out_specs=(P("interval", "seq", "head"), P("head", None), P("head", None), P("head", None)),
        check_vma=False,
    )
```
